32 devices in a mesh: seq: 4 (over x, core), fsdp: 8 (over z, y).
Axes of the slice: x: 2, y: 2, z: 4, core: 2. Of those that a mesh axis runs over, the one named last changes fastest.
Arguments:
- tokens_in: bfloat16 [8, 56, 56, 128], P('fsdp', 'seq'), may hold values from -6 to 6
- first_gain: bfloat16 [128], P('fsdp'), may hold values from 0.5 to 1.5
- first_shift: bfloat16 [128], P('fsdp'), may hold values from -2 to 2
- qkv_weight: bfloat16 [128, 384], P('fsdp'), may hold values from -0.5 to 0.5
- query_bias: bfloat16 [128], P('fsdp'), may hold values from -3 to 3
- value_bias: bfloat16 [128], P('fsdp'), may hold values from -3 to 3
- proj_weight: bfloat16 [128, 128], P('fsdp'), may hold values from -2 to 2
- proj_bias: bfloat16 [128], P('fsdp'), may hold values from -2 to 2
- second_gain: bfloat16 [128], P('fsdp'), may hold values from 0.5 to 1.5
- second_shift: bfloat16 [128], P('fsdp'), may hold values from -2 to 2
- up_weight: bfloat16 [128, 512], P('fsdp'), may hold values from -0.5 to 0.5
- up_bias: bfloat16 [512], P('fsdp'), may hold values from -3 to 3
- down_weight: bfloat16 [512, 128], P('fsdp'), may hold values from -0.375 to 0.375
- down_bias: bfloat16 [128], P('fsdp'), may hold values from -2 to 2
- bias_table: float32 [169, 4], replicated, may hold values from -5 to 5
- table_index: int32 [49, 49], replicated, may hold values from 0 to 168
- region_ids: int32 [8, 56, 56], P('fsdp', 'seq'), may hold values from 0 to 2
- cotangent: bfloat16 [8, 56, 56, 128], P('fsdp', 'seq'), may hold values from -6 to 6
Outputs:
- block_out: bfloat16 [8, 56, 56, 128], P('fsdp', 'seq')
- tokens_grad: float32 [8, 56, 56, 128], P('fsdp', 'seq')
- first_gain_grad: float32 [128], P('fsdp')
- first_shift_grad: float32 [128], P('fsdp')
- qkv_weight_grad: float32 [128, 384], P('fsdp')
- query_bias_grad: float32 [128], P('fsdp')
- value_bias_grad: float32 [128], P('fsdp')
- proj_weight_grad: float32 [128, 128], P('fsdp')
- proj_bias_grad: float32 [128], P('fsdp')
- second_gain_grad: float32 [128], P('fsdp')
- second_shift_grad: float32 [128], P('fsdp')
- up_weight_grad: float32 [128, 512], P('fsdp')
- up_bias_grad: float32 [512], P('fsdp')
- down_weight_grad: float32 [512, 128], P('fsdp')
- down_bias_grad: float32 [128], P('fsdp')
- bias_table_grad: float32 [169, 4], replicated
The draws below stay inside these ranges and needn't reach their ends.
Inputs may be any that keep to these rules, and one draw needn't show every extreme that they name: `region_ids`: two tokens of a window attend to each other only where their regions are equal; a token always attends to itself. `table_index`: entry (i, j) names the row of bias_table for query position i and key position j.
All inputs are finite; a program needn't handle non-finite values.
Results may differ from the reference program's by a relative error of at most 0.012.
Values may be sent and summed in bfloat16 or wider, within the bound.
No kernel may reach another device: no remote copies, remote signals or barrier semaphores. Data moves between devices by JAX's collectives and lax.ppermute only.
A program may use at most 64 MiB of HBM per device.

```python
import jax
import jax.numpy as jnp
from jax import lax

C = 128
HEADS = 4
MLP = 512
WIN = 7
SHIFT = 3
TABLE = 169
HEIGHT = 56
WIDTH = 56
IMAGES = 8


def plant(entries, rng, least, high):
    shape = entries.shape
    spot = [jax.random.randint(jax.random.fold_in(rng, axis), (), 0, shape[axis]) for axis in range(len(shape))]
    entries = entries.at[tuple(spot)].set(least)
    longest = shape.index(max(shape))
    spot[longest] = (spot[longest] + 1) % shape[longest]
    return entries.at[tuple(spot)].set(high)


def level_of(stream_key, extent, cuts, low, largest):
    def one(axis_at, shards_of):
        draws = jax.random.uniform(jax.random.fold_in(jax.random.fold_in(stream_key, 6), axis_at), (shards_of,), jnp.float32, low / len(cuts), largest / len(cuts))
        return jnp.repeat(jnp.exp(draws), extent[axis_at] // shards_of).reshape((-1,) + (1,) * (len(extent) - axis_at - 1))

    factor_of = one(*cuts[0])
    for cut in cuts[1:]:
        factor_of = factor_of * one(*cut)
    return factor_of


def noise(key, extent, deviation, reach, pieces=(), dtype=jnp.bfloat16):
    result = jax.random.normal(key, extent, jnp.float32) * deviation
    if len(pieces) > 0:
        result = level_of(key, extent, pieces, -0.22, 0.18) * result
    return jnp.clip(result, min=-reach, max=reach).astype(dtype)


def setup_inputs(seed: int = 0) -> dict:
    arg_keys = jax.random.split(jax.random.key(seed), 19)
    return {
        "tokens_in": noise(arg_keys[0], (IMAGES, HEIGHT, WIDTH, C), 1.0, 6.0, ((0, 8), (1, 4))),
        "first_gain": jnp.clip(1.0 + 0.1 * jax.random.normal(arg_keys[1], (C,), jnp.float32), 0.5, 1.5).astype(jnp.bfloat16),
        "first_shift": noise(arg_keys[2], (C,), 0.3, 2.0, ((0, 8),)),
        "qkv_weight": noise(arg_keys[3], (C, 3 * C), C ** -0.5, 0.5, ((0, 8),)),
        "query_bias": noise(arg_keys[4], (C,), 0.5, 3.0, ((0, 8),)),
        "value_bias": noise(arg_keys[5], (C,), 0.5, 3.0, ((0, 8),)),
        "proj_weight": noise(arg_keys[6], (C, C), (C // 16) ** -0.5, 2.0, ((0, 8),)),
        "proj_bias": noise(arg_keys[7], (C,), 0.3, 2.0, ((0, 8),)),
        "second_gain": jnp.clip(1.0 + 0.1 * jax.random.normal(arg_keys[8], (C,), jnp.float32), 0.5, 1.5).astype(jnp.bfloat16),
        "second_shift": noise(arg_keys[9], (C,), 0.3, 2.0, ((0, 8),)),
        "up_weight": noise(arg_keys[10], (C, MLP), C ** -0.5, 0.5, ((0, 8),)),
        "up_bias": noise(arg_keys[11], (MLP,), 0.5, 3.0, ((0, 8),)),
        "down_weight": noise(arg_keys[12], (MLP, C), (MLP // 2) ** -0.5, 0.375, ((0, 8),)),
        "down_bias": noise(arg_keys[13], (C,), 0.3, 2.0, ((0, 8),)),
        "bias_table": noise(arg_keys[14], (TABLE, HEADS), 1.0, 5.0, (), jnp.float32),
        "table_index": plant(jax.random.randint(arg_keys[15], (WIN * WIN, WIN * WIN), 0, TABLE), jax.random.fold_in(arg_keys[15], 1), 0, TABLE - 1).astype(jnp.int32),
        "region_ids": plant(jax.random.randint(arg_keys[16], (IMAGES, HEIGHT, WIDTH), 0, 3), jax.random.fold_in(arg_keys[16], 1), 0, 2).astype(jnp.int32),
        "cotangent": noise(arg_keys[17], (IMAGES, HEIGHT, WIDTH, C), 1.0, 6.0, ((0, 8), (1, 4))),
    }


norm_eps = 1e-05
masked_fill = -1e+30

@jax.custom_vjp
def low(v):
    return lax.optimization_barrier(v.astype(jnp.bfloat16)).astype(jnp.float32)

@jax.custom_vjp
def low_back(v):
    return v

def low_keep(v):
    return (low(v), None)

def low_pass(kept, grad):
    return (grad,)

def back_keep(v):
    return (v, None)

def back_low(kept, grad):
    return (low(grad),)
low.defvjp(low_keep, low_pass)
low_back.defvjp(back_keep, back_low)

def layer_norm(values, gain, shift):
    mean_val = lax.optimization_barrier(jnp.mean(values, axis=-1, keepdims=True))
    centred = values - mean_val
    var_val = lax.optimization_barrier(jnp.mean(centred * centred, axis=-1, keepdims=True))
    return centred * lax.rsqrt(var_val + norm_eps) * gain + shift

def to_windows(image_map):
    row_count, col_count, depth_count = image_map.shape
    image_map = image_map.reshape(row_count // WIN, WIN, col_count // WIN, WIN, depth_count)
    image_map = image_map.transpose(0, 2, 1, 3, 4)
    return image_map.reshape(-1, WIN * WIN, depth_count)

def from_windows(window_vals, row_count, col_count):
    window_vals = window_vals.reshape(row_count // WIN, col_count // WIN, WIN, WIN, -1)
    return window_vals.transpose(0, 2, 1, 3, 4).reshape(row_count, col_count, -1)

def one_image(params, rel_bias, image, labels):
    gain_one, shift_one, w_qkv, bias_query, bias_value, w_proj, bias_proj, gain_two, shift_two, w_up, bias_up, w_down, bias_down = params
    row_count, col_count, chan_count = image.shape
    head_dim = chan_count // HEADS
    highest = lax.Precision.HIGHEST
    normed = low(layer_norm(image, gain_one, shift_one))
    rolled = jnp.roll(normed, (-SHIFT, -SHIFT), (0, 1))
    win_tok = to_windows(rolled)
    win_count = win_tok.shape[0]
    mixed = jnp.dot(win_tok, w_qkv, precision=highest)
    query_v = low_back(low(mixed[..., :chan_count] + bias_query)).reshape(win_count, WIN * WIN, HEADS, head_dim)
    key_v = low_back(low(mixed[..., chan_count:2 * chan_count])).reshape(win_count, WIN * WIN, HEADS, head_dim)
    value_v = low_back(low(mixed[..., 2 * chan_count:] + bias_value)).reshape(win_count, WIN * WIN, HEADS, head_dim)
    scores = jnp.einsum('nihd,njhd->nhij', query_v, key_v, precision=highest) * head_dim ** (-0.5) + rel_bias[None]
    scores = low_back(scores)
    region = to_windows(labels[:, :, None])[..., 0]
    allowed = region[:, None, :, None] == region[:, None, None, :]
    masked = jnp.where(allowed, scores, masked_fill)
    expo = jnp.exp(masked - lax.optimization_barrier(jnp.max(masked, axis=-1, keepdims=True)))
    probs = low(expo / lax.optimization_barrier(jnp.sum(expo, axis=-1, keepdims=True)))
    attended = jnp.einsum('nhij,njhd->nihd', probs, value_v, precision=highest)
    attended = low_back(low(attended)).reshape(win_count, WIN * WIN, chan_count)
    moved = jnp.roll(from_windows(attended, row_count, col_count), (SHIFT, SHIFT), (0, 1))
    branch = low_back(jnp.dot(moved, w_proj, precision=highest) + bias_proj)
    middle = image + branch
    normed_two = low(layer_norm(middle, gain_two, shift_two))
    hidden = low_back(jnp.dot(normed_two, w_up, precision=highest) + bias_up)
    activ = low(jax.nn.gelu(hidden, approximate=False))
    return middle + jnp.dot(activ, w_down, precision=highest) + bias_down

def reference(tokens_in, first_gain, first_shift, qkv_weight, query_bias, value_bias, proj_weight, proj_bias, second_gain, second_shift, up_weight, up_bias, down_weight, down_bias, bias_table, table_index, region_ids, cotangent):
    params = tuple((p.astype(jnp.float32) for p in (first_gain, first_shift, qkv_weight, query_bias, value_bias, proj_weight, proj_bias, second_gain, second_shift, up_weight, up_bias, down_weight, down_bias)))
    checked = jax.checkpoint(one_image)

    def forward(tok_vals, param_vals, table_vals):
        rel_bias = jnp.take(table_vals, table_index.astype(jnp.int32), axis=0).transpose(2, 0, 1)
        return lax.map(lambda pair_in: checked(param_vals, rel_bias, pair_in[0], pair_in[1]), (tok_vals, region_ids))
    out_vals, back_fn = jax.vjp(forward, tokens_in.astype(jnp.float32), params, bias_table.astype(jnp.float32))
    grad_tok, grad_params, grad_table = back_fn(cotangent.astype(jnp.float32))
    return (out_vals.astype(jnp.bfloat16), grad_tok, grad_params[0], grad_params[1], grad_params[2], grad_params[3], grad_params[4], grad_params[5], grad_params[6], grad_params[7], grad_params[8], grad_params[9], grad_params[10], grad_params[11], grad_params[12], grad_table)
```

```python
import functools

import jax
import jax.numpy as jnp
from jax import lax
from jax.experimental import pallas as pl
from jax.experimental.pallas import tpu as pltpu
from jax.sharding import PartitionSpec as P

HEADS = 4
WIN = 7
SHIFT = 3
TABLE = 169
PADDED = 8
WTOK = WIN * PADDED
QPAD = 64
SMALL = 16

norm_eps = 1e-05
masked_fill = -1e30
f32 = jnp.float32
bf16 = jnp.bfloat16
NT = (((1,), (1,)), ((), ()))
TN = (((0,), (0,)), ((), ()))
VMEM = pltpu.VMEM


def mm(left, right, dims=(((1,), (0,)), ((), ()))):
    return lax.dot_general(left, right, dims, preferred_element_type=f32)


def iota(shape, axis):
    return lax.broadcasted_iota(jnp.int32, shape, axis)


def place_matrix(cols, roll):
    spots = cols // WIN * PADDED
    spot, col = iota((spots, cols), 0), iota((spots, cols), 1)
    place = spot % PADDED
    target = spot // PADDED * WIN + place + roll
    target = jnp.where(target >= cols, target - cols, target)
    return jnp.where((place < WIN) & (col == target), 1.0, 0.0).astype(bf16)


def head_mask(shape, lane_axis=1):
    chans = shape[-1] // HEADS
    return jnp.where(iota(shape, len(shape) - 1) // chans == iota(shape, 0), 1.0, 0.0)


def expand_heads(tokens, hmask):
    zeros = jnp.zeros((QPAD - WTOK, tokens.shape[1]), f32)
    full = jnp.concatenate([tokens, zeros], axis=0)
    return (full[None] * hmask).reshape(HEADS * QPAD, tokens.shape[1]).astype(bf16)


def merge_heads(stacked, hmask):
    parts = stacked.reshape(HEADS, QPAD, stacked.shape[1]) * hmask
    return ((parts[0] + parts[1]) + (parts[2] + parts[3]))[:WTOK]


def one_hot_rows(row, tall):
    spots = iota((tall, row.shape[1]), 0).astype(f32)
    return jnp.where(spots == row, 1.0, 0.0).astype(bf16)


def lane_mean(values):
    return jnp.mean(values, axis=-1, keepdims=True)


def pack_body(*refs):
    given, (out_a, out_b, out_h), scratch, sems = refs[:15], refs[15:18], refs[18:-1], refs[-1]
    sources = list(given[:13]) + [ref.at[0:SHIFT] for ref in given[13:]]
    targets = list(scratch) + [out_h.at[0], out_h.at[1]]
    copies = [
        pltpu.make_async_copy(source, target, sems.at[i])
        for i, (source, target) in enumerate(zip(sources, targets))
    ]
    for copy in copies:
        copy.start()
    for copy in copies:
        copy.wait()
    vectors, (qkv, proj, up, down) = scratch[:9], scratch[9:]
    count = out_a.shape[0]
    depth, chan = proj.shape
    blocks, ups = qkv.shape[1] // chan, up.shape[1] // chan
    small = jnp.concatenate(
        [jnp.pad(vector[...].astype(f32), ((0, 0), (0, chan - vector.shape[1]))) for vector in vectors]
        + [jnp.zeros((SMALL - 9, chan), f32)],
        axis=0,
    ).astype(bf16)
    for step in range(count):
        for col in range(blocks):
            out_a[step, col * depth : (col + 1) * depth] = qkv[:, col * chan : (col + 1) * chan]
        out_a[step, blocks * depth :] = small
        out_b[step, 0:depth] = proj[...]
        for col in range(ups):
            out_b[step, (1 + col) * depth : (2 + col) * depth] = up[:, col * chan : (col + 1) * chan]
        out_b[step, (1 + ups) * depth :] = down[...]


def bias_body(region, table, index, out_bm, out_idx, tab, rel, ident):
    rows, _, cols = region.shape
    tokens = index.shape[0]
    wide = HEADS * QPAD
    tall = (TABLE + 15) // 16 * 16
    token_a, spot_a = iota((tokens, WTOK), 0), iota((tokens, WTOK), 1)
    keys_at = jnp.where(token_a // WIN * PADDED + token_a % WIN == spot_a, 1.0, 0.0).astype(bf16)
    token_b, lane_b = iota((tokens, wide), 0), iota((tokens, wide), 1)
    queries_at = jnp.where(token_b // WIN * PADDED + token_b % WIN == lane_b % QPAD, 1.0, 0.0).astype(bf16)
    half = mm(index[...].astype(f32).astype(bf16), keys_at).astype(bf16)
    out_idx[...] = mm(half, queries_at, TN)
    tab[...] = jnp.zeros_like(tab)
    whole = table[...]
    first = whole.astype(bf16).astype(f32)
    second = (whole - first).astype(bf16).astype(f32)
    third = whole - first - second
    tab[0:HEADS, 0:TABLE] = first
    tab[HEADS : 2 * HEADS, 0:TABLE] = second
    tab[2 * HEADS : 3 * HEADS, 0:TABLE] = third
    terms = tab[...][:, :tall].astype(bf16)
    own = jnp.where(iota((SMALL, wide), 0) % HEADS == iota((SMALL, wide), 1) // QPAD, 1.0, 0.0)

    def one_key(key, carry):
        hot = one_hot_rows(out_idx[pl.ds(key, 1), :], tall)
        rel[pl.ds(key, 1), :] = jnp.sum(mm(terms, hot) * own, axis=0, keepdims=True)
        return carry

    lax.fori_loop(0, WTOK, one_key, 0, unroll=8)
    place = place_matrix(cols, 0)
    across = cols // WIN
    for row in range(rows):
        classes = jnp.where(iota((128, cols), 0) == region[row], 1.0, 0.0).astype(bf16)
        at = row // WIN * across
        down = row % WIN * PADDED
        ident[at : at + across, down : down + PADDED, :] = mm(place, classes, NT).reshape(
            across, PADDED, 128
        )
    bias = rel[...]
    for win in range(rows // WIN * across):
        here = ident[win]
        other = jnp.concatenate([here, jnp.zeros((QPAD - WTOK, 128), f32)], axis=0)
        other = jnp.broadcast_to(other[None], (HEADS, QPAD, 128)).reshape(wide, 128).astype(bf16)
        out_bm[win] = jnp.where(mm(here.astype(bf16), other, NT) > 0.5, bias, masked_fill)


def assemble_vectors(pieces, offset, out_small):
    count, _, chan = pieces.shape
    per, per_up = chan // count, 4 * chan // count
    row = iota((8, chan), 0)
    vecs, ups = jnp.zeros((8, chan), f32), jnp.zeros((8, chan), f32)
    for source in range(count):
        block = pieces[source, offset : offset + SMALL].astype(f32)
        at = source * per
        vecs += pltpu.roll(block[0:8], at, 1) if at else block[0:8]
        at = source * per_up
        line = jnp.broadcast_to(block[8:9], (8, chan))
        line = pltpu.roll(line, at % chan, 1) if at % chan else line
        ups += jnp.where(row == at // chan, line, 0.0)
    out_small[0:8] = vecs
    out_small[8:16] = ups


def attend_body(count, tok, halo, bm, *refs):
    taken = 1 if count else 2
    given = refs[:taken]
    out_xw, out_nb, out_q, out_k, out_v, out_p, out_att, out_small, out_w = refs[taken:]
    rows, cols, chan = tok.shape
    across = cols // WIN
    wins = rows // WIN * across
    if count:
        depth = chan // count
        for source in range(count):
            at = source * depth
            for col in range(3):
                out_w[at : at + depth, col * chan : (col + 1) * chan] = given[0][
                    source, col * depth : (col + 1) * depth
                ]
        assemble_vectors(given[0], 3 * depth, out_small)
    else:
        out_w[...] = given[0][...]
        out_small[...] = given[1][...]
    place = place_matrix(cols, SHIFT)
    for row in range(rows):
        source = tok[row + SHIFT] if row + SHIFT < rows else halo[0, row + SHIFT - rows]
        at, down = row // WIN * across, row % WIN * PADDED
        out_xw[at : at + across, down : down + PADDED, :] = mm(place, source).reshape(across, PADDED, chan)
    small = out_small[...]
    gain, shift, bias_q, bias_v = small[0:1], small[1:2], small[2:3], small[3:4]
    weight = out_w[...]
    step_wins = 4
    for at in range(0, wins, step_wins):
        values = out_xw[at : at + step_wins].reshape(step_wins * WTOK, chan)
        centred = values - lane_mean(values)
        rstd = lax.rsqrt(lane_mean(centred * centred) + norm_eps)
        normed = (centred * rstd * gain + shift).astype(bf16)
        out_nb[at * WTOK : (at + step_wins) * WTOK] = normed
        mixed = mm(normed, weight)
        query = mixed[:, :chan] + bias_q
        key = mixed[:, chan : 2 * chan]
        value = mixed[:, 2 * chan :] + bias_v
        for win in range(step_wins):
            span = slice(win * WTOK, (win + 1) * WTOK)
            out_q[at + win] = query[span].astype(bf16)
            out_k[at + win] = key[span].astype(bf16)
            out_v[at + win] = value[span].astype(bf16)
    hmask = head_mask((HEADS, QPAD, chan))
    scale = (chan // HEADS) ** -0.5
    for win in range(wins):
        queries = expand_heads(out_q[win].astype(f32), hmask)
        scores = mm(out_k[win], queries, NT) * scale + bm[win]
        expo = jnp.exp(scores - jnp.max(scores, axis=0, keepdims=True))
        probs = expo * (1.0 / jnp.sum(expo, axis=0, keepdims=True))
        out_p[win] = probs
        out_att[win] = merge_heads(mm(probs.astype(bf16), out_v[win], TN), hmask)


def gelu_parts(hidden):
    size = jnp.abs(hidden) * (0.5**0.5)
    term = 1.0 / (1.0 + 0.3275911 * size)
    bell = jnp.exp(-0.5 * hidden * hidden)
    poly = 1.061405429 * term - 1.453152027
    poly = poly * term + 1.421413741
    poly = poly * term - 0.284496736
    poly = poly * term + 0.254829592
    tail = 0.5 * poly * term * bell
    cdf = jnp.where(hidden >= 0, 1.0 - tail, tail)
    return cdf, cdf + hidden * bell * 0.3989422804014327


def out_rows(windows, place_t, row, across):
    at, down = row // WIN * across, row % WIN * PADDED
    block = windows[at : at + across, down : down + PADDED, :]
    return block.reshape(across * PADDED, block.shape[-1])


def mlp_body(count, cot, halo, att, xw, small_ref, *refs):
    taken = 1 if count else 3
    given, refs = refs[:taken], refs[taken:]
    out_bo, out_bo_halo, out_dmid, out_datt, refs = refs[0], refs[1], refs[2], refs[3], refs[4:]
    sent = 1 if count else 4
    outs, scratch = refs[:sent], refs[sent:]
    cw, bw, w_proj, w_up, w_down, att_b, n2_b, dbr_b, dy_b, act_b, dh_b, g_down, g_up, g_proj, g_small = scratch
    rows, cols, chan = cot.shape
    wide = w_up.shape[1]
    across = cols // WIN
    wins = rows // WIN * across
    if count:
        depth = chan // count
        ups = wide // chan
        deep = ups * depth
        for source in range(count):
            at = source * depth
            w_proj[at : at + depth] = given[0][source, 0:depth]
            for col in range(ups):
                w_up[at : at + depth, col * chan : (col + 1) * chan] = given[0][
                    source, (1 + col) * depth : (2 + col) * depth
                ]
            w_down[source * deep : (source + 1) * deep] = given[0][source, (1 + ups) * depth :]
    else:
        w_proj[...] = given[0][...]
        w_up[...] = given[1][...]
        w_down[...] = given[2][...]
    place = place_matrix(cols, SHIFT)
    for row in range(rows):
        source = cot[row + SHIFT] if row + SHIFT < rows else halo[1, row + SHIFT - rows]
        at, down = row // WIN * across, row % WIN * PADDED
        cw[at : at + across, down : down + PADDED, :] = mm(place, source).reshape(across, PADDED, chan)
    small = small_ref[...]
    bias_p, gain, shift, bias_d = small[4:5], small[5:6], small[6:7], small[7:8]
    bias_u = jnp.concatenate([small[8 + i : 9 + i] for i in range(wide // chan)], axis=1)
    weight_p, weight_u, weight_d = w_proj[...], w_up[...], w_down[...]
    step_wins = 4
    sums = [jnp.zeros((1, chan), f32) for _ in range(4)]
    sum_up = jnp.zeros((1, wide), f32)
    for at in range(0, wins, step_wins):
        flat = slice(at * WTOK, (at + step_wins) * WTOK)
        full = (step_wins * WTOK, chan)
        split = (step_wins, WTOK, chan)
        attended = att[at : at + step_wins].reshape(full).astype(bf16)
        att_b[flat] = attended
        middle = xw[at : at + step_wins].reshape(full) + (mm(attended, weight_p) + bias_p)
        centred = middle - lane_mean(middle)
        rstd = lax.rsqrt(lane_mean(centred * centred) + norm_eps)
        unit = centred * rstd
        normed = (unit * gain + shift).astype(bf16)
        n2_b[flat] = normed
        hidden = mm(normed, weight_u) + bias_u
        cdf, slope = gelu_parts(hidden)
        activ = (hidden * cdf).astype(bf16)
        act_b[flat] = activ
        bw[at : at + step_wins] = (middle + mm(activ, weight_d) + bias_d).reshape(split)
        grad = cw[at : at + step_wins].reshape(full)
        grad_b = grad.astype(bf16)
        dy_b[flat] = grad_b
        d_hidden = (mm(grad_b, weight_d, NT) * slope).astype(bf16)
        dh_b[flat] = d_hidden
        d_normed = mm(d_hidden, weight_u, NT)
        d_unit = d_normed * gain
        back = d_unit - lane_mean(d_unit) - unit * lane_mean(d_unit * unit)
        d_middle = grad + rstd * back
        out_dmid[at : at + step_wins] = d_middle.reshape(split)
        d_branch = d_middle.astype(bf16)
        dbr_b[flat] = d_branch
        out_datt[at : at + step_wins] = mm(d_branch, weight_p, NT).reshape(split)
        terms = (d_branch.astype(f32), d_normed * unit, d_normed, grad)
        sums = [have + jnp.sum(term, axis=0, keepdims=True) for have, term in zip(sums, terms)]
        sum_up = sum_up + jnp.sum(d_hidden.astype(f32), axis=0, keepdims=True)
    g_small[...] = jnp.zeros_like(g_small)
    for row in range(4):
        g_small[row : row + 1] = sums[row]
    for col in range(wide // chan):
        g_small[4 + col : 5 + col] = sum_up[:, col * chan : (col + 1) * chan]
    g_down[...] = mm(dy_b[...], act_b[...], TN).T
    g_up[...] = mm(n2_b[...], dh_b[...], TN)
    g_proj[...] = mm(att_b[...], dbr_b[...], TN)
    if count:
        tail = g_small[...].astype(bf16)
        for dest in range(count):
            out, at = outs[0].at[dest], dest * depth
            out[0:depth] = g_proj[at : at + depth].astype(bf16)
            for col in range(ups):
                part = g_up[at : at + depth, col * chan : (col + 1) * chan]
                out[(1 + col) * depth : (2 + col) * depth] = part.astype(bf16)
            part = g_down[dest * deep : (dest + 1) * deep]
            out[(1 + ups) * depth : (1 + ups) * depth + deep] = part.astype(bf16)
            out[(1 + ups) * depth + deep :] = tail
    else:
        outs[0][...] = g_proj[...]
        outs[1][...] = g_up[...]
        outs[2][...] = g_down[...]
        outs[3][...] = g_small[...]
    for row in range(rows):
        block = mm(place, out_rows(bw, place, row, across).astype(bf16), TN).astype(bf16)
        if row + SHIFT < rows:
            out_bo[row + SHIFT] = block
        else:
            out_bo_halo[row + SHIFT - rows] = block
    for row in range(SHIFT):
        out_bo[row] = jnp.zeros((cols, chan), bf16)


def back_body(count, bo_halo, q_ref, k_ref, v_ref, p_ref, datt, dmid, nb, xw, small_ref, w_ref, idx, *refs):
    out_tg, out_halo, refs = refs[0], refs[1], refs[2:]
    sent = 1 if count else 2
    outs, scratch = refs[:sent], refs[sent:]
    dq, dk, dv, tw, g_qkv, g_small, drel, mixed, spread = scratch
    wins, _, chan = q_ref.shape
    rows, cols, _ = out_tg.shape
    across = cols // WIN
    hmask = head_mask((HEADS, QPAD, chan))
    scale = (chan // HEADS) ** -0.5
    wide = HEADS * QPAD
    drel[...] = jnp.zeros_like(drel)
    for win in range(wins):
        queries = expand_heads(q_ref[win].astype(f32), hmask)
        grads = expand_heads(datt[win].astype(bf16).astype(f32), hmask)
        probs = p_ref[win]
        weighted = probs * mm(v_ref[win], grads, NT)
        d_scores = (weighted - probs * jnp.sum(weighted, axis=0, keepdims=True)).astype(bf16)
        drel[...] += d_scores.astype(f32)
        dv[win] = mm(probs.astype(bf16), grads)
        dk[win] = mm(d_scores, queries) * scale
        dq[win] = merge_heads(mm(d_scores, k_ref[win], TN), hmask) * scale
    flat = (wins * WTOK, chan)
    d_query = dq[...].reshape(flat).astype(bf16)
    d_key = dk[...].reshape(flat).astype(bf16)
    d_value = dv[...].reshape(flat).astype(bf16)
    for col, part in enumerate((d_query, d_key, d_value)):
        mixed[:, col * chan : (col + 1) * chan] = part
    g_qkv[...] = mm(nb[...], mixed[...], TN)
    small = small_ref[...]
    gain = small[0:1]
    weight = w_ref[...]
    step_wins = 4
    sum_gain, sum_shift = jnp.zeros((1, chan), f32), jnp.zeros((1, chan), f32)
    for at in range(0, wins, step_wins):
        here = slice(at * WTOK, (at + step_wins) * WTOK)
        full = (step_wins * WTOK, chan)
        d_normed = mm(mixed[here], weight, NT)
        values = xw[at : at + step_wins].reshape(full)
        centred = values - lane_mean(values)
        rstd = lax.rsqrt(lane_mean(centred * centred) + norm_eps)
        unit = centred * rstd
        d_unit = d_normed * gain
        back = d_unit - lane_mean(d_unit) - unit * lane_mean(d_unit * unit)
        total = dmid[at : at + step_wins].reshape(full) + rstd * back
        tw[at : at + step_wins] = total.reshape(step_wins, WTOK, chan)
        sum_gain += jnp.sum(d_normed * unit, axis=0, keepdims=True)
        sum_shift += jnp.sum(d_normed, axis=0, keepdims=True)
    g_small[...] = jnp.zeros_like(g_small)
    g_small[0:1] = sum_gain
    g_small[1:2] = sum_shift
    g_small[2:3] = jnp.sum(d_query.astype(f32), axis=0, keepdims=True)
    g_small[3:4] = jnp.sum(d_value.astype(f32), axis=0, keepdims=True)
    own = iota((SMALL, wide), 0) % HEADS == iota((SMALL, wide), 1) // QPAD
    which = iota((SMALL, wide), 0) // HEADS
    tall = 2 * chan

    def one_key(key, carry):
        hot = one_hot_rows(idx[pl.ds(key, 1), :], tall)
        line = drel[pl.ds(key, 1), :]
        high = line.astype(bf16).astype(f32)
        both = jnp.where(which == 0, high, jnp.where(which == 1, line - high, 0.0))
        spread[key] = mm(jnp.where(own, both, 0.0).astype(bf16), hot, NT)
        return carry

    lax.fori_loop(0, WTOK, one_key, 0, unroll=8)
    table = jnp.sum(spread[...], axis=0)
    table = table[0:HEADS] + table[HEADS : 2 * HEADS]
    g_small[4 : 4 + HEADS] = table[:, :chan]
    g_small[4 + HEADS : 4 + 2 * HEADS, 0 : tall - chan] = table[:, chan:]
    if count:
        depth = chan // count
        tail = g_small[...].astype(bf16)
        for dest in range(count):
            for col in range(3):
                part = g_qkv[dest * depth : (dest + 1) * depth, col * chan : (col + 1) * chan]
                outs[0][dest, col * depth : (col + 1) * depth] = part.astype(bf16)
            outs[0][dest, 3 * depth :] = tail
    else:
        outs[0][...] = g_qkv[...]
        outs[1][...] = g_small[...]
    place = place_matrix(cols, SHIFT)
    twice = jnp.concatenate([place, place], axis=0)
    for row in range(rows):
        block = out_rows(tw, place, row, across)
        high = block.astype(bf16)
        low = (block - high.astype(f32)).astype(bf16)
        block = mm(twice, jnp.concatenate([high, low], axis=0), TN)
        if row + SHIFT < rows:
            out_tg[row + SHIFT] = block
        else:
            out_halo[1, row + SHIFT - rows] = block.astype(bf16)
    for row in range(SHIFT):
        out_tg[row] = jnp.zeros((cols, chan), f32)
        out_halo[0, row] = bo_halo[row]


def total(refs):
    parts = [refs[source][...].astype(f32) for source in range(len(refs))]
    while len(parts) > 1:
        parts = [parts[i] + parts[i + 1] for i in range(0, len(parts), 2)]
    return parts[0]


def sum_body(one, two, out):
    out[...] = jnp.concatenate([total([one.at[i] for i in range(one.shape[0])]), total([two.at[i] for i in range(two.shape[0])])], axis=0).astype(bf16)


def final_body(bands, me_ref, bo, tg, halo, *refs):
    both, outs = refs[:bands], refs[bands:]
    (
        out_bo, out_tg, o_gain_one, o_shift_one, o_qkv, o_query, o_value, o_proj, o_bias_proj,
        o_gain_two, o_shift_two, o_up, o_bias_up, o_down, o_bias_down, o_table,
    ) = outs
    rows = bo.shape[0]
    me = me_ref[0]
    out_bo[SHIFT:] = bo[SHIFT:]
    out_tg[SHIFT:] = tg[SHIFT:]
    for row in range(SHIFT):
        out_bo[row] = halo[0, row]
        out_tg[row] = halo[1, row].astype(f32)
    depth, chan = o_proj.shape
    ups = o_up.shape[1] // chan
    summed = total(both)
    split = (1 + 2 * ups) * depth + SMALL
    first, second = summed[:split], summed[split:]
    o_proj[...] = first[0:depth]
    for col in range(ups):
        o_up[:, col * chan : (col + 1) * chan] = first[(1 + col) * depth : (2 + col) * depth]
    o_down[...] = first[(1 + ups) * depth : (1 + 2 * ups) * depth]
    for col in range(3):
        o_qkv[:, col * chan : (col + 1) * chan] = second[col * depth : (col + 1) * depth]
    early = first[(1 + 2 * ups) * depth :]
    late = second[3 * depth :]
    mine = jnp.concatenate([early[0:8], late[0:8]], axis=0)
    turned = pltpu.roll(mine, (chan - me * depth) % chan, 1)
    o_bias_proj[...] = turned[0:1, :depth]
    o_gain_two[...] = turned[1:2, :depth]
    o_shift_two[...] = turned[2:3, :depth]
    o_bias_down[...] = turned[3:4, :depth]
    o_gain_one[...] = turned[8:9, :depth]
    o_shift_one[...] = turned[9:10, :depth]
    o_query[...] = turned[10:11, :depth]
    o_value[...] = turned[11:12, :depth]
    at = me * depth * ups
    chosen = jnp.where(iota((8, chan), 0) == 4 + at // chan, early[0:8], 0.0)
    chosen = jnp.broadcast_to(jnp.sum(chosen, axis=0, keepdims=True), (8, chan))
    chosen = pltpu.roll(chosen, (chan - at % chan) % chan, 1)
    o_bias_up[...] = chosen[0:1, : depth * ups]
    o_table[:, :chan] = late[4 : 4 + HEADS]
    o_table[:, chan:] = late[4 + HEADS : 4 + 2 * HEADS, : TABLE - chan]


def call(body, outs, *args, scratch=(), smem=0, name=None, limit=40, micros=1):
    specs = [pl.BlockSpec(memory_space=pltpu.SMEM)] * smem
    specs += [pl.BlockSpec(memory_space=VMEM)] * (len(args) - smem)
    return pl.pallas_call(
        body,
        out_shape=[jax.ShapeDtypeStruct(shape, dtype) for shape, dtype in outs],
        in_specs=specs,
        out_specs=[pl.BlockSpec(memory_space=VMEM)] * len(outs),
        scratch_shapes=[VMEM(shape, dtype) for shape, dtype in scratch],
        compiler_params=pltpu.CompilerParams(vmem_limit_bytes=limit << 20),
        cost_estimate=pl.CostEstimate(flops=micros * 10**9, bytes_accessed=micros * 3 * 10**6, transcendentals=0),
        name=name,
    )(*args)


def shifted(value, axis, steps):
    count = lax.axis_size(axis)
    return lax.ppermute(value, axis, [(source, (source + steps) % count) for source in range(count)])


def swap(value, axis, step):
    count = lax.axis_size(axis)
    return lax.ppermute(value, axis, [(source, source ^ step) for source in range(count)])


def exchange(pieces, axis):
    return lax.all_to_all(pieces, axis, 0, 0, tiled=True)


def on_device(
    tokens_in, first_gain, first_shift, qkv_weight, query_bias, value_bias, proj_weight, proj_bias,
    second_gain, second_shift, up_weight, up_bias, down_weight, down_bias, bias_table, table_index,
    region_ids, cotangent,
):
    images, rows, cols, chan = tokens_in.shape
    assert images == 1
    fsdp, bands = lax.axis_size("fsdp"), lax.axis_size("seq")
    wide = up_weight.shape[1]
    depth = proj_weight.shape[0]
    wins = rows // WIN * (cols // WIN)
    direct = depth % 16 == 0
    count = fsdp if direct else 0
    tok, cot = tokens_in[0], cotangent[0]
    region = region_ids.reshape(rows, 1, cols)
    vectors = (
        first_gain, first_shift, query_bias, value_bias, proj_bias, second_gain, second_shift, down_bias, up_bias,
    )
    tokw = (wins, WTOK, chan)
    flatw = (wins * WTOK, chan)
    flatu = (wins * WTOK, wide)
    ups = wide // chan
    rows_one, rows_two = (1 + 2 * ups) * depth + SMALL, 3 * depth + SMALL
    if direct:
        held = [vector.reshape(1, -1) for vector in vectors] + [qkv_weight, proj_weight, up_weight, down_weight]
        piece_a, piece_b, halo = pl.pallas_call(
            pack_body,
            out_shape=[
                jax.ShapeDtypeStruct((fsdp, rows_two, chan), bf16),
                jax.ShapeDtypeStruct((fsdp, rows_one - SMALL, chan), bf16),
                jax.ShapeDtypeStruct((2, SHIFT, cols, chan), bf16),
            ],
            in_specs=[pl.BlockSpec(memory_space=pltpu.HBM)] * 15,
            out_specs=[pl.BlockSpec(memory_space=VMEM)] * 3,
            scratch_shapes=[VMEM(array.shape, bf16) for array in held] + [pltpu.SemaphoreType.DMA((15,))],
            compiler_params=pltpu.CompilerParams(vmem_limit_bytes=58 << 20),
            name="pack",
        )(*held, tok, cot)
        given_a = [exchange(piece_a, "fsdp")]
        piece_b, *given_a = lax.optimization_barrier((piece_b, *given_a))
        given_b = [exchange(piece_b, "fsdp")]
    else:
        halo = jnp.stack([tok[:SHIFT], cot[:SHIFT]])
        gather = functools.partial(lax.all_gather, axis_name="fsdp", axis=0, tiled=True)
        full = [gather(vector).astype(f32).reshape(-1, chan) for vector in vectors]
        full.append(jnp.zeros((SMALL - 8 - ups, chan), f32))
        given_a = [gather(qkv_weight), jnp.concatenate(full, axis=0)]
        given_b = [gather(proj_weight), gather(up_weight), gather(down_weight)]
    halo = shifted(halo, "seq", -1)
    bm, idx = call(
        bias_body,
        [((wins, WTOK, HEADS * QPAD), f32), ((WTOK, HEADS * QPAD), f32)],
        region, bias_table.T, table_index,
        scratch=[((SMALL, 256), f32), ((WTOK, HEADS * QPAD), f32), ((wins, WTOK, 128), f32)],
        name="score_bias", micros=3,
    )
    xw, nb, q_b, k_b, v_b, probs, att, small, w_qkv = call(
        functools.partial(attend_body, count),
        [
            (tokw, f32), (flatw, bf16), (tokw, bf16), (tokw, bf16), (tokw, bf16),
            ((wins, WTOK, HEADS * QPAD), f32), (tokw, f32), ((SMALL, chan), f32), ((chan, 3 * chan), bf16),
        ],
        tok, halo, bm, *given_a, name="attention", micros=4,
    )
    if direct:
        sent_one = [((fsdp, rows_one, chan), bf16)]
        sent_two = [((fsdp, rows_two, chan), bf16)]
    else:
        sent_one = [((chan, chan), f32), ((chan, wide), f32), ((wide, chan), f32), ((SMALL, chan), f32)]
        sent_two = [((chan, 3 * chan), f32), ((SMALL, chan), f32)]
    bo, bo_halo, dmid, datt, *first = call(
        functools.partial(mlp_body, count),
        [((rows, cols, chan), bf16), ((SHIFT, cols, chan), bf16), (tokw, f32), (tokw, f32)] + sent_one,
        cot, halo, att, xw, small, *given_b, name="feed_forward", micros=6,
        scratch=[
            (tokw, f32), (tokw, f32), ((chan, chan), bf16), ((chan, wide), bf16), ((wide, chan), bf16),
            (flatw, bf16), (flatw, bf16), (flatw, bf16), (flatw, bf16), (flatu, bf16), (flatu, bf16),
            ((wide, chan), f32), ((chan, wide), f32), ((chan, chan), f32), ((SMALL, chan), f32),
        ],
    )
    if direct:
        first = exchange(first[0], "fsdp")
    tg, last, *second = call(
        functools.partial(back_body, count),
        [((rows, cols, chan), f32), ((2, SHIFT, cols, chan), bf16)] + sent_two,
        bo_halo, q_b, k_b, v_b, probs, datt, dmid, nb, xw, small, w_qkv, idx, name="attention_back", micros=7,
        scratch=[
            (tokw, f32), (tokw, f32), (tokw, f32), (tokw, f32), ((chan, 3 * chan), f32), ((SMALL, chan), f32),
            ((WTOK, HEADS * QPAD), f32), ((wins * WTOK, 3 * chan), bf16),
            ((WTOK, SMALL, 2 * chan), f32),
        ],
    )
    last = shifted(last, "seq", 1)
    if not direct:
        g_proj, g_up, g_down, early, g_qkv, late = lax.psum((*first, *second), "seq")
        table = lax.psum(late[4 : 4 + 2 * HEADS], "fsdp").reshape(2, HEADS, chan)
        table = jnp.concatenate([table[0], table[1]], axis=1)[:, :TABLE]
        scatter = functools.partial(lax.psum_scatter, axis_name="fsdp", scatter_dimension=0, tiled=True)
        block_out = jnp.concatenate([last[0], bo[SHIFT:]], axis=0)
        tokens_grad = jnp.concatenate([last[1].astype(f32), tg[SHIFT:]], axis=0)
        return (
            block_out[None], tokens_grad[None], scatter(late[0]), scatter(late[1]), scatter(g_qkv),
            scatter(late[2]), scatter(late[3]), scatter(g_proj), scatter(early[0]), scatter(early[1]),
            scatter(early[2]), scatter(g_up), scatter(early[4 : 4 + ups].reshape(-1)),
            scatter(g_down), scatter(early[3]), table.T,
        )
    second, first = lax.optimization_barrier((second[0], first))
    second = exchange(second, "fsdp")
    (both,) = call(sum_body, [((rows_one + rows_two, chan), bf16)], first, second, name="sum_images")
    arrived = [both] + [swap(both, "seq", step) for step in range(1, bands)]
    line = ((1, depth), f32)
    me = lax.axis_index("fsdp").astype(jnp.int32).reshape(1)
    outs = call(
        functools.partial(final_body, bands),
        [
            ((rows, cols, chan), bf16), ((rows, cols, chan), f32), line, line, ((depth, 3 * chan), f32), line,
            line, ((depth, chan), f32), line, line, line, ((depth, wide), f32), ((1, depth * ups), f32),
            ((depth * ups, chan), f32), line, ((HEADS, TABLE), f32),
        ],
        me, bo, tg, last, *arrived, smem=1, name="finish",
    )
    outs = [out.reshape(-1) if out.shape[0] == 1 else out for out in outs]
    return (outs[0][None], outs[1][None], *outs[2:15], outs[15].T)


def solution(mesh):
    placed = (
        P("fsdp", "seq", None, None),
        P("fsdp"),
        P("fsdp"),
        P("fsdp", None),
        P("fsdp"),
        P("fsdp"),
        P("fsdp", None),
        P("fsdp"),
        P("fsdp"),
        P("fsdp"),
        P("fsdp", None),
        P("fsdp"),
        P("fsdp", None),
        P("fsdp"),
        P(),
        P(),
        P("fsdp", "seq", None),
        P("fsdp", "seq", None, None),
    )
    return jax.shard_map(
        on_device,
        mesh=mesh,
        in_specs=placed,
        out_specs=(
            P("fsdp", "seq", None, None),
            P("fsdp", "seq", None, None),
            P("fsdp"),
            P("fsdp"),
            P("fsdp", None),
            P("fsdp"),
            P("fsdp"),
            P("fsdp", None),
            P("fsdp"),
            P("fsdp"),
            P("fsdp"),
            P("fsdp", None),
            P("fsdp"),
            P("fsdp", None),
            P("fsdp"),
            P(),
        ),
        check_vma=False,
    )
```

```python
import functools

import jax
import jax.numpy as jnp
from jax import lax
from jax.experimental import pallas as pl
from jax.experimental.pallas import tpu as pltpu
from jax.sharding import PartitionSpec as P

HEADS = 4
WIN = 7
SHIFT = 3
TABLE = 169
PADDED = 8
WTOK = WIN * PADDED
QPAD = 64
SMALL = 16
DIGIT = 16

norm_eps = 1e-05
masked_fill = -1e30
f32 = jnp.float32
bf16 = jnp.bfloat16
NT = (((1,), (1,)), ((), ()))
TN = (((0,), (0,)), ((), ()))
VMEM = pltpu.VMEM


def mm(left, right, dims=(((1,), (0,)), ((), ()))):
    return lax.dot_general(left, right, dims, preferred_element_type=f32)


def iota(shape, axis):
    return lax.broadcasted_iota(jnp.int32, shape, axis)


def place_matrix(cols, roll):
    spots = cols // WIN * PADDED
    spot, col = iota((spots, cols), 0), iota((spots, cols), 1)
    place = spot % PADDED
    target = spot // PADDED * WIN + place + roll
    target = jnp.where(target >= cols, target - cols, target)
    return jnp.where((place < WIN) & (col == target), 1.0, 0.0).astype(bf16)


def head_mask(shape, lane_axis=1):
    chans = shape[-1] // HEADS
    return jnp.where(iota(shape, len(shape) - 1) // chans == iota(shape, 0), 1.0, 0.0)


def expand_heads(tokens, hmask):
    zeros = jnp.zeros((QPAD - WTOK, tokens.shape[1]), f32)
    full = jnp.concatenate([tokens, zeros], axis=0)
    return (full[None] * hmask).reshape(HEADS * QPAD, tokens.shape[1]).astype(bf16)


def merge_heads(stacked, hmask):
    parts = stacked.reshape(HEADS, QPAD, stacked.shape[1]) * hmask
    return ((parts[0] + parts[1]) + (parts[2] + parts[3]))[:WTOK]


def one_hot_rows(row, tall):
    spots = iota((tall, row.shape[1]), 0).astype(f32)
    return jnp.where(spots == row, 1.0, 0.0).astype(bf16)


def lane_mean(values):
    return jnp.mean(values, axis=-1, keepdims=True)


def pack_body(*refs):
    given, (out, out_h), scratch, sems = refs[:15], refs[15:17], refs[17:-1], refs[-1]
    sources = list(given[:13]) + [ref.at[0:SHIFT] for ref in given[13:]]
    targets = list(scratch) + [out_h.at[0], out_h.at[1]]
    copies = [
        pltpu.make_async_copy(source, target, sems.at[i])
        for i, (source, target) in enumerate(zip(sources, targets))
    ]
    for copy in copies:
        copy.start()
    for copy in copies:
        copy.wait()
    vectors, (qkv, proj, up, down) = scratch[:9], scratch[9:]
    depth, chan = proj.shape
    blocks, ups = qkv.shape[1] // chan, up.shape[1] // chan
    small = jnp.concatenate(
        [jnp.pad(vector[...].astype(f32), ((0, 0), (0, chan - vector.shape[1]))) for vector in vectors]
        + [jnp.zeros((SMALL - 9, chan), f32)],
        axis=0,
    ).astype(bf16)
    parts = [proj[...]]
    parts += [up[:, col * chan : (col + 1) * chan] for col in range(ups)]
    parts += [down[...]]
    parts += [qkv[:, col * chan : (col + 1) * chan] for col in range(blocks)]
    parts += [small]
    at = 0
    for part in parts:
        out[at : at + part.shape[0]] = part
        at += part.shape[0]


def join_body(*refs):
    for i, piece in enumerate(refs[:-1]):
        refs[-1][i] = piece[...]


def bias_body(region, table, index, out_bm, out_idx, tab, rel, ident):
    rows, _, cols = region.shape
    tokens = index.shape[0]
    wide = HEADS * QPAD
    tall = (TABLE + 15) // 16 * 16
    token_a, spot_a = iota((tokens, WTOK), 0), iota((tokens, WTOK), 1)
    keys_at = jnp.where(token_a // WIN * PADDED + token_a % WIN == spot_a, 1.0, 0.0).astype(bf16)
    token_b, lane_b = iota((tokens, wide), 0), iota((tokens, wide), 1)
    queries_at = jnp.where(token_b // WIN * PADDED + token_b % WIN == lane_b % QPAD, 1.0, 0.0).astype(bf16)
    half = mm(index[...].astype(f32).astype(bf16), keys_at).astype(bf16)
    out_idx[...] = mm(half, queries_at, TN)
    tab[...] = jnp.zeros_like(tab)
    whole = table[...]
    first = whole.astype(bf16).astype(f32)
    second = (whole - first).astype(bf16).astype(f32)
    third = whole - first - second
    tab[0:HEADS, 0:TABLE] = first
    tab[HEADS : 2 * HEADS, 0:TABLE] = second
    tab[2 * HEADS : 3 * HEADS, 0:TABLE] = third
    terms = tab[...][:, :tall].astype(bf16)
    own = jnp.where(iota((SMALL, wide), 0) % HEADS == iota((SMALL, wide), 1) // QPAD, 1.0, 0.0)

    def one_key(key, carry):
        hot = one_hot_rows(out_idx[pl.ds(key, 1), :], tall)
        rel[pl.ds(key, 1), :] = jnp.sum(mm(terms, hot) * own, axis=0, keepdims=True)
        return carry

    lax.fori_loop(0, WTOK, one_key, 0, unroll=8)
    place = place_matrix(cols, 0)
    across = cols // WIN
    for row in range(rows):
        classes = jnp.where(iota((128, cols), 0) == region[row], 1.0, 0.0).astype(bf16)
        at = row // WIN * across
        down = row % WIN * PADDED
        ident[at : at + across, down : down + PADDED, :] = mm(place, classes, NT).reshape(
            across, PADDED, 128
        )
    bias = rel[...]
    for win in range(rows // WIN * across):
        here = ident[win]
        other = jnp.concatenate([here, jnp.zeros((QPAD - WTOK, 128), f32)], axis=0)
        other = jnp.broadcast_to(other[None], (HEADS, QPAD, 128)).reshape(wide, 128).astype(bf16)
        out_bm[win] = jnp.where(mm(here.astype(bf16), other, NT) > 0.5, bias, masked_fill)


def assemble_vectors(pieces, sources, count, offset, out_small):
    chan = pieces[0].shape[1]
    per, per_up = chan // count, 4 * chan // count
    row = iota((8, chan), 0)
    vecs, ups = jnp.zeros((8, chan), f32), jnp.zeros((8, chan), f32)
    for piece, source in zip(pieces, sources):
        block = piece[offset : offset + SMALL].astype(f32)
        vecs += pltpu.roll(block[0:8], source * per, 1)
        at = source * per_up
        line = pltpu.roll(jnp.broadcast_to(block[8:9], (8, chan)), at % chan, 1)
        ups += jnp.where(row == at // chan, line, 0.0)
    out_small[0:8] = vecs
    out_small[8:16] = ups


def gelu_parts(hidden):
    base = 1.0 + (0.3275911 * 0.5**0.5) * jnp.abs(hidden)
    term = pl.reciprocal(base, approx=True)
    term = term * (2.0 - base * term)
    bell = jnp.exp(-0.5 * (hidden * hidden))
    poly = (0.5 * 1.061405429) * term - (0.5 * 1.453152027)
    poly = poly * term + (0.5 * 1.421413741)
    poly = poly * term - (0.5 * 0.284496736)
    poly = poly * term + (0.5 * 0.254829592)
    tail = poly * term * bell
    cdf = jnp.where(hidden >= 0, 1.0 - tail, tail)
    return cdf, cdf + hidden * (bell * 0.3989422804014327)


def layer_stats(values):
    centred = values - lane_mean(values)
    rstd = lax.rsqrt(lane_mean(centred * centred) + norm_eps)
    return centred * rstd, rstd


def layer_back(d_unit, unit, rstd):
    return rstd * (d_unit - lane_mean(d_unit) - unit * lane_mean(d_unit * unit))


def my_images(me_ref, band_ref, count):
    near = count // 2
    return [me_ref[0] ^ ((band_ref[0] % 2 ^ core) * near + i) for core in range(2) for i in range(near)]


def prepare_body(tok, cot, halo, out_xw, out_cw, out_unit, out_rstd):
    rows, cols, chan = tok.shape
    across = cols // WIN
    place = place_matrix(cols, SHIFT)
    for which, source, target in ((0, tok, out_xw), (1, cot, out_cw)):
        for row in range(rows):
            line = source[row + SHIFT] if row + SHIFT < rows else halo[which, row + SHIFT - rows]
            at, down = row // WIN * across, row % WIN * PADDED
            target[at : at + across, down : down + PADDED, :] = mm(place, line).reshape(across, PADDED, chan)
    step_wins = 4
    for at in range(0, out_xw.shape[0], step_wins):
        span = slice(at, at + step_wins)
        unit, rstd = layer_stats(out_xw[span])
        out_unit[span] = unit
        out_rstd[span] = jnp.broadcast_to(rstd, unit.shape)


def attend_body(count, me_ref, band_ref, unit, bm, *refs):
    inputs = 2 if count else 5
    weights, outs = refs[:inputs], refs[inputs:]
    out_nb, out_qx, out_k, out_v, out_p, out_att, out_small, w_qkv, w_proj, w_up, w_down, mixed = outs
    wins, _, chan = unit.shape
    if count:
        sources = my_images(me_ref, band_ref, count)
        pieces = [weights[core].at[i] for core in range(2) for i in range(count // 2)]
        depth, ups = chan // count, w_up.shape[1] // chan
        deep = ups * depth
        first = (1 + 2 * ups) * depth
        for piece, source in zip(pieces, sources):
            here = pl.ds(pl.multiple_of(source * depth, depth), depth)
            for col in range(3):
                w_qkv[here, col * chan : (col + 1) * chan] = piece[first + col * depth : first + (col + 1) * depth]
            w_proj[here] = piece[0:depth]
            for col in range(ups):
                w_up[here, col * chan : (col + 1) * chan] = piece[(1 + col) * depth : (2 + col) * depth]
            w_down[pl.ds(pl.multiple_of(source * deep, deep), deep)] = piece[(1 + ups) * depth : first]
        assemble_vectors(pieces, sources, count, first + 3 * depth, out_small)
    else:
        for source, target in zip(weights, (w_qkv, out_small, w_proj, w_up, w_down)):
            target[...] = source[...]
    small = out_small[...]
    gain, shift, bias_q, bias_v = small[0:1], small[1:2], small[2:3], small[3:4]
    hmask = head_mask((HEADS, QPAD, chan))
    scale = (chan // HEADS) ** -0.5
    step_wins = 4
    weight = w_qkv[...]
    for at in range(0, wins, step_wins):
        normed = (unit[at : at + step_wins].reshape(step_wins * WTOK, chan) * gain + shift).astype(bf16)
        out_nb[at * WTOK : (at + step_wins) * WTOK] = normed
    mixed[...] = mm(out_nb[...], weight)
    for at in range(0, wins, step_wins):
        three = mixed[at * WTOK : (at + step_wins) * WTOK]
        query = three[:, :chan] + bias_q
        key = three[:, chan : 2 * chan]
        value = three[:, 2 * chan :] + bias_v
        for win in range(step_wins):
            span = slice(win * WTOK, (win + 1) * WTOK)
            out_qx[at + win] = expand_heads(query[span].astype(bf16).astype(f32), hmask)
            out_k[at + win] = key[span].astype(bf16)
            out_v[at + win] = value[span].astype(bf16)
    for at in range(0, wins, step_wins):
        group = range(at, at + step_wins)
        scores = [mm(out_k[win], out_qx[win], NT) * scale + bm[win] for win in group]
        expos = [jnp.exp(one - jnp.max(one, axis=0, keepdims=True)) for one in scores]
        probs = [one * (1.0 / jnp.sum(one, axis=0, keepdims=True)) for one in expos]
        for win, one in zip(group, probs):
            out_p[win] = one
        parts = [mm(one.astype(bf16), out_v[win], TN) for win, one in zip(group, probs)]
        for win, one in zip(group, parts):
            out_att[win] = merge_heads(one, hmask)


def mlp_body(xw, cw, att, small_ref, w_proj, w_up, w_down, *refs):
    out_bw, out_dmid, out_datt, g_proj, g_up, g_down, g_one, *scratch = refs
    att_b, n2_b, dbr_b, dy_b, act_b, dh_b, hid, dact, mid, unit2, rstd2, back = scratch
    wins, _, chan = xw.shape
    wide = w_up.shape[1]
    ups = wide // chan
    small = small_ref[...]
    bias_p, gain, shift, bias_d = small[4:5], small[5:6], small[6:7], small[7:8]
    bias_u = jnp.concatenate([small[8 + i : 9 + i] for i in range(ups)], axis=1)
    weight_p, weight_u, weight_d = w_proj[...], w_up[...], w_down[...]
    half = wins // 2
    few = 4
    full, split = (few * WTOK, chan), (few, WTOK, chan)
    sums = [jnp.zeros((1, chan), f32) for _ in range(4)]
    sum_up = jnp.zeros((8, wide), f32)

    def rows_of(at, many):
        return slice(at, at + many), slice(at * WTOK, (at + many) * WTOK)

    def enter(at):
        span, flat = rows_of(at, half)
        dy_b[flat] = cw[span].reshape(half * WTOK, chan).astype(bf16)
        dact[flat] = mm(dy_b[flat], weight_d, NT)
        att_b[flat] = att[span].reshape(half * WTOK, chan).astype(bf16)
        mid[flat] = mm(att_b[flat], weight_p)
        for some in range(at, at + half, few):
            here, line = rows_of(some, few)
            middle = xw[here].reshape(full) + (mid[line] + bias_p)
            mid[line] = middle
            unit, rstd = layer_stats(middle)
            unit2[line] = unit
            rstd2[line] = jnp.broadcast_to(rstd, full)
            n2_b[line] = (unit * gain + shift).astype(bf16)
        hid[flat] = mm(n2_b[flat], weight_u)

    def tiles(at, have):
        for row in range(at * WTOK, (at + half) * WTOK, 16):
            line = slice(row, row + 16)
            hidden = hid[line] + bias_u
            cdf, slope = gelu_parts(hidden)
            act_b[line] = (hidden * cdf).astype(bf16)
            d_hidden = dact[line] * slope
            dh_b[line] = d_hidden.astype(bf16)
            have = have + (d_hidden[0:8] + d_hidden[8:16])
        return have

    def leave(at, have):
        span, flat = rows_of(at, half)
        out_bw[span] = (mid[flat] + mm(act_b[flat], weight_d) + bias_d).reshape(half, WTOK, chan)
        back[flat] = mm(dh_b[flat], weight_u, NT)
        for some in range(at, at + half, few):
            here, line = rows_of(some, few)
            d_normed = back[line]
            unit = unit2[line]
            grad = cw[here].reshape(full)
            d_middle = grad + layer_back(d_normed * gain, unit, rstd2[line])
            out_dmid[here] = d_middle.reshape(split)
            dbr_b[line] = d_middle.astype(bf16)
            terms = (d_middle, d_normed * unit, d_normed, grad)
            have = [one + jnp.sum(term, axis=0, keepdims=True) for one, term in zip(have, terms)]
        out_datt[span] = mm(dbr_b[flat], weight_p, NT).reshape(half, WTOK, chan)
        return have

    enter(0)
    enter(half)
    sum_up = tiles(0, sum_up)
    sums = leave(0, sums)
    sum_up = tiles(half, sum_up)
    sums = leave(half, sums)
    g_one[...] = jnp.zeros_like(g_one)
    for row in range(4):
        g_one[row : row + 1] = sums[row]
    total_up = jnp.sum(sum_up, axis=0, keepdims=True)
    for col in range(ups):
        g_one[4 + col : 5 + col] = total_up[:, col * chan : (col + 1) * chan]
    g_down[...] = mm(dy_b[...], act_b[...], TN).T
    g_up[...] = mm(n2_b[...], dh_b[...], TN)
    g_proj[...] = mm(att_b[...], dbr_b[...], TN)


def back_body(count, band_ref, qx, k_ref, v_ref, p_ref, datt, dmid, nb, unit_ref, rstd_ref, *refs):
    small_ref, w_qkv, idx, g_proj, g_up, g_down, g_one, out_tw, *refs = refs
    outs, scratch = refs[:2], refs[2:]
    dq, dk, dv, mixed, d_one, drel, spread, g_qkv, g_two, g_all = scratch
    wins, _, chan = dmid.shape
    hmask = head_mask((HEADS, QPAD, chan))
    scale = (chan // HEADS) ** -0.5
    step_wins = 4
    drel[...] = jnp.zeros_like(drel)
    for at in range(0, wins, step_wins):
        group = range(at, at + step_wins)
        grads = [expand_heads(datt[win].astype(bf16).astype(f32), hmask) for win in group]
        d_probs = [mm(v_ref[win], one, NT) for win, one in zip(group, grads)]
        for win, one in zip(group, grads):
            dv[win] = mm(p_ref[win].astype(bf16), one)
        weighted = [p_ref[win] * one for win, one in zip(group, d_probs)]
        d_scores = [
            (one - p_ref[win] * jnp.sum(one, axis=0, keepdims=True)).astype(bf16) for win, one in zip(group, weighted)
        ]
        four = [one.astype(f32) for one in d_scores]
        drel[...] += (four[0] + four[1]) + (four[2] + four[3])
        for win, one in zip(group, d_scores):
            dk[win] = mm(one, qx[win]) * scale
        parts = [mm(one, k_ref[win], TN) for win, one in zip(group, d_scores)]
        for win, one in zip(group, parts):
            dq[win] = merge_heads(one, hmask) * scale
    sums = []
    for col, ref in enumerate((dq, dk, dv)):
        part = ref[...].reshape(wins * WTOK, chan).astype(bf16)
        mixed[:, col * chan : (col + 1) * chan] = part
        if col != 1:
            sums.append(jnp.sum(ref[...].reshape(wins * WTOK, chan), axis=0, keepdims=True))
    g_two[...] = jnp.zeros_like(g_two)
    g_two[2:3] = sums[0]
    g_two[3:4] = sums[1]
    g_qkv[...] = mm(nb[...], mixed[...], TN)
    weight = w_qkv[...]
    gain = small_ref[0:1]
    full = (step_wins * WTOK, chan)
    sum_gain, sum_shift = jnp.zeros((1, chan), f32), jnp.zeros((1, chan), f32)
    d_one[...] = mm(mixed[...], weight, NT)
    for at in range(0, wins, step_wins):
        span = slice(at, at + step_wins)
        d_normed = d_one[at * WTOK : (at + step_wins) * WTOK]
        unit = unit_ref[span].reshape(full)
        grad = dmid[span].reshape(full) + layer_back(d_normed * gain, unit, rstd_ref[span].reshape(full))
        out_tw[span] = grad.reshape(step_wins, WTOK, chan)
        sum_gain += jnp.sum(d_normed * unit, axis=0, keepdims=True)
        sum_shift += jnp.sum(d_normed, axis=0, keepdims=True)
    g_two[0:1] = sum_gain
    g_two[1:2] = sum_shift

    lanes = HEADS * QPAD
    row_a, row_b = iota((2 * DIGIT, lanes), 0), iota((HEADS * DIGIT, lanes), 0).astype(f32)
    digit_a = (row_a % DIGIT).astype(f32)
    head_of = (iota((1, lanes), 1) // QPAD * DIGIT).astype(f32)

    def one_key(key, carry):
        line = drel[pl.ds(key, 1), :]
        entry = idx[pl.ds(key, 1), :]
        high_digit = jnp.floor(entry * (1.0 / DIGIT))
        low_digit = entry - high_digit * DIGIT + head_of
        high = line.astype(bf16).astype(f32)
        value = jnp.where(row_a < DIGIT, high, line - high)
        left = jnp.where(digit_a == high_digit, value, 0.0).astype(bf16)
        right = jnp.where(row_b == low_digit, 1.0, 0.0).astype(bf16)
        spread[key] = mm(left, right, NT)
        return carry

    lax.fori_loop(0, WTOK, one_key, 0, unroll=8)
    table = jnp.sum(spread[...], axis=0)
    table = table[0:DIGIT] + table[DIGIT:]
    g_two[4:SMALL, 0 : HEADS * DIGIT] = table[0 : SMALL - 4]
    if not count:
        outs[0][...] = g_qkv[...]
        outs[1][...] = g_two[...]
        return
    depth, ups = chan // count, g_up.shape[1] // chan
    deep = ups * depth
    first = (1 + 2 * ups) * depth
    for dest in range(count):
        at = dest * depth
        g_all[dest, 0:depth] = g_proj[at : at + depth].astype(bf16)
        for col in range(ups):
            part = g_up[at : at + depth, col * chan : (col + 1) * chan]
            g_all[dest, (1 + col) * depth : (2 + col) * depth] = part.astype(bf16)
        g_all[dest, (1 + ups) * depth : first] = g_down[dest * deep : (dest + 1) * deep].astype(bf16)
        for col in range(3):
            part = g_qkv[at : at + depth, col * chan : (col + 1) * chan]
            g_all[dest, first + col * depth : first + (col + 1) * depth] = part.astype(bf16)
        g_all[dest, first + 3 * depth : first + 3 * depth + SMALL] = g_one[...].astype(bf16)
        g_all[dest, first + 3 * depth + SMALL :] = g_two[...].astype(bf16)
    side = band_ref[0] % 2
    many = g_all.shape[1] // 2
    outs[0][...] = g_all[:, pl.ds(pl.multiple_of(side * many, many), many), :]
    outs[1][...] = g_all[:, pl.ds(pl.multiple_of((1 - side) * many, many), many), :]


def rows_body(bw, tw, out_bo, out_tg, out_halo):
    rows, cols, chan = out_bo.shape
    across = cols // WIN
    place = place_matrix(cols, SHIFT)
    twice = jnp.concatenate([place, place], axis=0)
    for row in range(rows):
        at, down = row // WIN * across, row % WIN * PADDED
        block = bw[at : at + across, down : down + PADDED, :].reshape(across * PADDED, chan).astype(bf16)
        block = mm(place, block, TN).astype(bf16)
        grad = tw[at : at + across, down : down + PADDED, :].reshape(across * PADDED, chan)
        high = grad.astype(bf16)
        low = (grad - high.astype(f32)).astype(bf16)
        grad = mm(twice, jnp.concatenate([high, low], axis=0), TN)
        if row + SHIFT < rows:
            out_bo[row + SHIFT] = block
            out_tg[row + SHIFT] = grad
        else:
            out_halo[0, row + SHIFT - rows] = block
            out_halo[1, row + SHIFT - rows] = grad.astype(bf16)
    for row in range(SHIFT):
        out_bo[row] = jnp.zeros((cols, chan), bf16)
        out_tg[row] = jnp.zeros((cols, chan), f32)


def total(refs):
    parts = [refs[source][...].astype(f32) for source in range(len(refs))]
    while len(parts) > 1:
        parts = [parts[i] + parts[i + 1] for i in range(0, len(parts), 2)]
    return parts[0]


def pair_body(mine, other, out):
    out[...] = (mine[...].astype(f32) + other[...].astype(f32)).astype(bf16)


def sum_body(pieces, out):
    out[...] = total([pieces.at[i] for i in range(pieces.shape[0])]).astype(bf16)


def final_body(bands, me_ref, band_ref, bo, tg, halo, *refs):
    both, outs, (rows_f, sems) = refs[:bands], refs[bands:-2], refs[-2:]
    (
        out_bo, out_tg, o_gain_one, o_shift_one, o_qkv, o_query, o_value, o_proj, o_bias_proj,
        o_gain_two, o_shift_two, o_up, o_bias_up, o_down, o_bias_down, o_table,
    ) = outs
    rows_f[...] = halo[1].astype(f32)
    copies = [
        pltpu.make_async_copy(halo.at[0], out_bo.at[0:SHIFT], sems.at[0]),
        pltpu.make_async_copy(rows_f, out_tg.at[0:SHIFT], sems.at[1]),
    ]
    for copy in copies:
        copy.start()
    me = me_ref[0]
    depth, chan = o_proj.shape
    ups = o_up.shape[1] // chan
    mine = total([both[step] for step in range(0, bands, 2)])
    other = total([both[step] for step in range(1, bands, 2)])
    even = band_ref[0] % 2 == 0
    summed = jnp.concatenate([jnp.where(even, mine, other), jnp.where(even, other, mine)], axis=0)
    first = (1 + 2 * ups) * depth
    o_proj[...] = summed[0:depth]
    for col in range(ups):
        o_up[:, col * chan : (col + 1) * chan] = summed[(1 + col) * depth : (2 + col) * depth]
    o_down[...] = summed[(1 + ups) * depth : first]
    for col in range(3):
        o_qkv[:, col * chan : (col + 1) * chan] = summed[first + col * depth : first + (col + 1) * depth]
    early = summed[first + 3 * depth : first + 3 * depth + SMALL]
    late = summed[first + 3 * depth + SMALL :]
    mine = jnp.concatenate([early[0:8], late[0:8]], axis=0)
    turned = pltpu.roll(mine, (chan - me * depth) % chan, 1)
    o_bias_proj[...] = turned[0:1, :depth]
    o_gain_two[...] = turned[1:2, :depth]
    o_shift_two[...] = turned[2:3, :depth]
    o_bias_down[...] = turned[3:4, :depth]
    o_gain_one[...] = turned[8:9, :depth]
    o_shift_one[...] = turned[9:10, :depth]
    o_query[...] = turned[10:11, :depth]
    o_value[...] = turned[11:12, :depth]
    at = me * depth * ups
    chosen = jnp.where(iota((8, chan), 0) == 4 + at // chan, early[0:8], 0.0)
    chosen = jnp.broadcast_to(jnp.sum(chosen, axis=0, keepdims=True), (8, chan))
    chosen = pltpu.roll(chosen, (chan - at % chan) % chan, 1)
    o_bias_up[...] = chosen[0:1, : depth * ups]
    for head in range(HEADS):
        for digit in range((TABLE + DIGIT - 1) // DIGIT):
            width = min(DIGIT, TABLE - digit * DIGIT)
            o_table[head : head + 1, digit * DIGIT : digit * DIGIT + width] = late[
                4 + digit : 5 + digit, head * DIGIT : head * DIGIT + width
            ]
    for copy in copies:
        copy.wait()


def call(body, outs, *args, scratch=(), ins=None, outs_at=None, name=None, limit=16, micros=1, aliases=None):
    at = lambda space: pl.BlockSpec(memory_space=space)
    return pl.pallas_call(
        body,
        out_shape=[jax.ShapeDtypeStruct(shape, dtype) for shape, dtype in outs],
        in_specs=[at(space) for space in (ins or [VMEM] * len(args))],
        out_specs=[at(space) for space in (outs_at or [VMEM] * len(outs))],
        scratch_shapes=[VMEM(*one) if isinstance(one, tuple) else one for one in scratch],
        input_output_aliases=aliases or {},
        compiler_params=pltpu.CompilerParams(vmem_limit_bytes=limit << 20),
        cost_estimate=pl.CostEstimate(flops=micros * 10**9, bytes_accessed=micros * 3 * 10**6, transcendentals=0),
        name=name,
    )(*args)


def shifted(value, axis, steps):
    count = lax.axis_size(axis)
    return lax.ppermute(value, axis, [(source, (source + steps) % count) for source in range(count)])


def swap(value, axis, step):
    count = lax.axis_size(axis)
    return lax.ppermute(value, axis, [(source, source ^ step) for source in range(count)])


def spread_out(value, i):
    bands, images = lax.axis_size("seq"), lax.axis_size("fsdp")
    pairs = [
        (band * images + image, band * images + (image ^ (band % 2 * (images // 2) + i)))
        for band in range(bands)
        for image in range(images)
    ]
    return lax.ppermute(value, ("seq", "fsdp"), pairs)


def on_device(
    tokens_in, first_gain, first_shift, qkv_weight, query_bias, value_bias, proj_weight, proj_bias,
    second_gain, second_shift, up_weight, up_bias, down_weight, down_bias, bias_table, table_index,
    region_ids, cotangent,
):
    images, rows, cols, chan = tokens_in.shape
    assert images == 1
    fsdp, bands = lax.axis_size("fsdp"), lax.axis_size("seq")
    wide = up_weight.shape[1]
    depth = proj_weight.shape[0]
    wins = rows // WIN * (cols // WIN)
    direct = depth % 16 == 0
    count = fsdp if direct else 0
    tok, cot = tokens_in[0], cotangent[0]
    region = region_ids.reshape(rows, 1, cols)
    vectors = (
        first_gain, first_shift, query_bias, value_bias, proj_bias, second_gain, second_shift, down_bias, up_bias,
    )
    tokw = (wins, WTOK, chan)
    flatw = (wins * WTOK, chan)
    flatu = (wins * WTOK, wide)
    ups = wide // chan
    piece_rows = (1 + 2 * ups) * depth + 3 * depth + SMALL
    wide_scores = (wins, WTOK, HEADS * QPAD)
    sems = lambda many: pltpu.SemaphoreType.DMA((many,))
    near = fsdp // 2
    me = lax.axis_index("fsdp").astype(jnp.int32).reshape(1)
    band = lax.axis_index("seq").astype(jnp.int32).reshape(1)
    if direct:
        held = [vector.reshape(1, -1) for vector in vectors] + [qkv_weight, proj_weight, up_weight, down_weight]
        piece, halo = call(
            pack_body,
            [((piece_rows, chan), bf16), ((2, SHIFT, cols, chan), bf16)],
            *held, tok, cot, name="pack", limit=58, ins=[pl.ANY] * 15,
            scratch=[(array.shape, bf16) for array in held] + [sems(15)],
        )
        fetched = [spread_out(piece, i) for i in range(near)]
    else:
        halo = jnp.stack([tok[:SHIFT], cot[:SHIFT]])
        gather = functools.partial(lax.all_gather, axis_name="fsdp", axis=0, tiled=True)
        full = [gather(vector).astype(f32).reshape(-1, chan) for vector in vectors]
        full.append(jnp.zeros((SMALL - 8 - ups, chan), f32))
        weights = [
            gather(qkv_weight), jnp.concatenate(full, axis=0), gather(proj_weight), gather(up_weight),
            gather(down_weight),
        ]
    halo = shifted(halo, "seq", -1)
    bm, idx = call(
        bias_body,
        [(wide_scores, f32), ((WTOK, HEADS * QPAD), f32)],
        region, bias_table.T, table_index,
        scratch=[((SMALL, 256), f32), ((WTOK, HEADS * QPAD), f32), ((wins, WTOK, 128), f32)],
        name="score_bias", micros=3,
    )
    if direct:
        *fetched, bm, idx = lax.optimization_barrier((*fetched, bm, idx))
        (pair,) = call(join_body, [((near, piece_rows, chan), bf16)], *fetched, name="join")
        weights = [pair, swap(pair, "seq", 1)]
    xw, cw, unit, rstd = call(prepare_body, [(tokw, f32)] * 4, tok, cot, halo, name="prepare", micros=2)
    big = dict(limit=32)
    place = [pltpu.SMEM] * 2
    nb, qx, k_b, v_b, probs, att, small, w_qkv, w_proj, w_up, w_down = call(
        functools.partial(attend_body, count),
        [
            (flatw, bf16), ((wins, HEADS * QPAD, chan), bf16), (tokw, bf16), (tokw, bf16), (wide_scores, f32),
            (tokw, f32), ((SMALL, chan), f32), ((chan, 3 * chan), bf16), ((chan, chan), bf16), ((chan, wide), bf16),
            ((wide, chan), bf16),
        ],
        me, band, unit, bm, *weights, name="attention", micros=3, ins=place + [VMEM] * (2 + len(weights)), **big,
        scratch=[((wins * WTOK, 3 * chan), f32)],
    )
    bw, dmid, datt, g_proj, g_up, g_down, g_one = call(
        mlp_body,
        [
            (tokw, f32), (tokw, f32), (tokw, f32), ((chan, chan), f32), ((chan, wide), f32), ((wide, chan), f32),
            ((SMALL, chan), f32),
        ],
        xw, cw, att, small, w_proj, w_up, w_down, name="feed_forward", micros=5, **big,
        scratch=[(flatw, bf16)] * 4 + [(flatu, bf16)] * 2 + [(flatu, f32)] * 2 + [(flatw, f32)] * 4,
    )
    if direct:
        halves = ((fsdp, (piece_rows + SMALL) // 2, chan), bf16)
        sent = [halves] * 2
    else:
        sent = [((chan, 3 * chan), f32), ((SMALL, chan), f32)]
    tw, *grads = call(
        functools.partial(back_body, count),
        [(tokw, f32)] + sent,
        band, qx, k_b, v_b, probs, datt, dmid, nb, unit, rstd, small, w_qkv, idx, g_proj, g_up, g_down, g_one,
        name="attention_back", micros=5, ins=place[:1] + [VMEM] * 16, **big,
        scratch=[
            (tokw, f32), (tokw, f32), (tokw, f32), ((wins * WTOK, 3 * chan), bf16), (flatw, f32),
            ((WTOK, HEADS * QPAD), f32), ((WTOK, 2 * DIGIT, HEADS * DIGIT), f32), ((chan, 3 * chan), f32), ((SMALL, chan), f32),
            ((max(count, 1), piece_rows + SMALL, chan), bf16),
        ],
    )
    bo, tg, last = call(
        rows_body,
        [((rows, cols, chan), bf16), ((rows, cols, chan), f32), ((2, SHIFT, cols, chan), bf16)],
        bw, tw, name="rows", micros=2,
    )
    if not direct:
        last = shifted(last, "seq", 1)
        g_proj, g_up, g_down, early, g_qkv, late = lax.psum((g_proj, g_up, g_down, g_one, *grads), "seq")
        digits = (TABLE + DIGIT - 1) // DIGIT
        table = lax.psum(late[4 : 4 + digits, : HEADS * DIGIT], "fsdp").reshape(digits, HEADS, DIGIT)
        table = table.transpose(1, 0, 2).reshape(HEADS, digits * DIGIT)[:, :TABLE]
        scatter = functools.partial(lax.psum_scatter, axis_name="fsdp", scatter_dimension=0, tiled=True)
        block_out = jnp.concatenate([last[0], bo[SHIFT:]], axis=0)
        tokens_grad = jnp.concatenate([last[1].astype(f32), tg[SHIFT:]], axis=0)
        return (
            block_out[None], tokens_grad[None], scatter(late[0]), scatter(late[1]), scatter(g_qkv),
            scatter(late[2]), scatter(late[3]), scatter(g_proj), scatter(early[0]), scatter(early[1]),
            scatter(early[2]), scatter(g_up), scatter(early[4 : 4 + ups].reshape(-1)),
            scatter(g_down), scatter(early[3]), table.T,
        )
    kept, given = grads[0], swap(grads[1], "seq", 1)
    kept, given, last = lax.optimization_barrier((kept, given, last))
    last = shifted(last, "seq", 1)
    (kept,) = call(pair_body, [halves], kept, given, name="sum_cores")
    pieces = lax.all_to_all(kept, "fsdp", 0, 0, tiled=True)
    (both,) = call(sum_body, [(halves[0][1:], bf16)], pieces, name="sum_images")
    arrived = [both] + [swap(both, "seq", step) for step in range(1, bands)]
    line = ((1, depth), f32)
    outs = call(
        functools.partial(final_body, bands),
        [
            ((rows, cols, chan), bf16), ((rows, cols, chan), f32), line, line, ((depth, 3 * chan), f32), line,
            line, ((depth, chan), f32), line, line, line, ((depth, wide), f32), ((1, depth * ups), f32),
            ((depth * ups, chan), f32), line, ((HEADS, TABLE), f32),
        ],
        me, band, bo, tg, last, *arrived, name="finish", aliases={2: 0, 3: 1},
        ins=[pltpu.SMEM] * 2 + [pl.ANY] * 2 + [VMEM] * (1 + bands), outs_at=[pl.ANY, pl.ANY] + [VMEM] * 14,
        scratch=[((SHIFT, cols, chan), f32), sems(2)],
    )
    outs = [out.reshape(-1) if out.shape[0] == 1 else out for out in outs]
    return (outs[0][None], outs[1][None], *outs[2:15], outs[15].T)


def solution(mesh):
    placed = (
        P("fsdp", "seq", None, None),
        P("fsdp"),
        P("fsdp"),
        P("fsdp", None),
        P("fsdp"),
        P("fsdp"),
        P("fsdp", None),
        P("fsdp"),
        P("fsdp"),
        P("fsdp"),
        P("fsdp", None),
        P("fsdp"),
        P("fsdp", None),
        P("fsdp"),
        P(),
        P(),
        P("fsdp", "seq", None),
        P("fsdp", "seq", None, None),
    )
    return jax.shard_map(
        on_device,
        mesh=mesh,
        in_specs=placed,
        out_specs=(
            P("fsdp", "seq", None, None),
            P("fsdp", "seq", None, None),
            P("fsdp"),
            P("fsdp"),
            P("fsdp", None),
            P("fsdp"),
            P("fsdp"),
            P("fsdp", None),
            P("fsdp"),
            P("fsdp"),
            P("fsdp"),
            P("fsdp", None),
            P("fsdp"),
            P("fsdp", None),
            P("fsdp"),
            P(),
        ),
        check_vma=False,
    )
```

```python
import functools

import jax
import jax.numpy as jnp
from jax import lax
from jax.experimental import pallas as pl
from jax.experimental.pallas import tpu as pltpu
from jax.sharding import PartitionSpec as P

HEADS = 4
WIN = 7
SHIFT = 3
TABLE = 169
PADDED = 8
WTOK = WIN * PADDED
QPAD = 64
SMALL = 16
DIGIT = 16

norm_eps = 1e-05
masked_fill = -1e30
f32 = jnp.float32
bf16 = jnp.bfloat16
NT = (((1,), (1,)), ((), ()))
TN = (((0,), (0,)), ((), ()))
VMEM = pltpu.VMEM


def mm(left, right, dims=(((1,), (0,)), ((), ()))):
    return lax.dot_general(left, right, dims, preferred_element_type=f32)


def iota(shape, axis):
    return lax.broadcasted_iota(jnp.int32, shape, axis)


def place_matrix(cols, roll):
    spots = cols // WIN * PADDED
    spot, col = iota((spots, cols), 0), iota((spots, cols), 1)
    place = spot % PADDED
    target = spot // PADDED * WIN + place + roll
    target = jnp.where(target >= cols, target - cols, target)
    return jnp.where((place < WIN) & (col == target), 1.0, 0.0).astype(bf16)


def head_mask(shape, lane_axis=1):
    chans = shape[-1] // HEADS
    return jnp.where(iota(shape, len(shape) - 1) // chans == iota(shape, 0), 1.0, 0.0)


def expand_heads(tokens, hmask):
    zeros = jnp.zeros((QPAD - WTOK, tokens.shape[1]), f32)
    full = jnp.concatenate([tokens, zeros], axis=0)
    return (full[None] * hmask).reshape(HEADS * QPAD, tokens.shape[1]).astype(bf16)


def merge_heads(stacked, hmask):
    parts = stacked.reshape(HEADS, QPAD, stacked.shape[1]) * hmask
    return ((parts[0] + parts[1]) + (parts[2] + parts[3]))[:WTOK]


def lane_mean(values):
    return jnp.mean(values, axis=-1, keepdims=True)


def pack_body(*refs):
    given, (out, out_h), scratch, sems = refs[:15], refs[15:17], refs[17:-1], refs[-1]
    sources = list(given[:13]) + [ref.at[0:SHIFT] for ref in given[13:]]
    targets = list(scratch) + [out_h.at[0], out_h.at[1]]
    copies = [
        pltpu.make_async_copy(source, target, sems.at[i])
        for i, (source, target) in enumerate(zip(sources, targets))
    ]
    for copy in copies:
        copy.start()
    for copy in copies:
        copy.wait()
    vectors, (qkv, proj, up, down) = scratch[:9], scratch[9:]
    depth, chan = proj.shape
    blocks, ups = qkv.shape[1] // chan, up.shape[1] // chan
    small = jnp.concatenate(
        [jnp.pad(vector[...].astype(f32), ((0, 0), (0, chan - vector.shape[1]))) for vector in vectors]
        + [jnp.zeros((SMALL - 9, chan), f32)],
        axis=0,
    ).astype(bf16)
    parts = [proj[...]]
    parts += [up[:, col * chan : (col + 1) * chan] for col in range(ups)]
    parts += [down[...]]
    parts += [qkv[:, col * chan : (col + 1) * chan] for col in range(blocks)]
    parts += [small]
    at = 0
    for part in parts:
        out[at : at + part.shape[0]] = part
        at += part.shape[0]


def join_body(*refs):
    for i, piece in enumerate(refs[:-1]):
        refs[-1][i] = piece[...]


def bias_body(region, table, index, tok, cot, out_bm, out_idx, tab, rel, ident):
    rows, _, cols = region.shape
    tokens = index.shape[0]
    wide = HEADS * QPAD
    token_a, spot_a = iota((tokens, WTOK), 0), iota((tokens, WTOK), 1)
    keys_at = jnp.where(token_a // WIN * PADDED + token_a % WIN == spot_a, 1.0, 0.0).astype(bf16)
    token_b, lane_b = iota((tokens, wide), 0), iota((tokens, wide), 1)
    queries_at = jnp.where(token_b // WIN * PADDED + token_b % WIN == lane_b % QPAD, 1.0, 0.0).astype(bf16)
    half = mm(index[...].astype(f32).astype(bf16), keys_at).astype(bf16)
    out_idx[...] = mm(half, queries_at, TN)
    tab[...] = jnp.zeros_like(tab)
    for head in range(HEADS):
        for digit in range((TABLE + DIGIT - 1) // DIGIT):
            width = min(DIGIT, TABLE - digit * DIGIT)
            tab[digit : digit + 1, head * DIGIT : head * DIGIT + width] = table[
                head : head + 1, digit * DIGIT : digit * DIGIT + width
            ]
    entries = tab[...]
    first = entries.astype(bf16).astype(f32)
    second = (entries - first).astype(bf16).astype(f32)
    terms = jnp.concatenate([first, second, entries - first - second], axis=0).astype(bf16)
    digit_a = (iota((3 * DIGIT, wide), 0) % DIGIT).astype(f32)
    row_b = iota((HEADS * DIGIT, wide), 0).astype(f32)
    head_of = (iota((1, wide), 1) // QPAD * DIGIT).astype(f32)

    def one_key(key, carry):
        entry = out_idx[pl.ds(key, 1), :]
        high_digit = jnp.floor(entry * (1.0 / DIGIT))
        low_digit = entry - high_digit * DIGIT + head_of
        hot = jnp.where(row_b == low_digit, 1.0, 0.0).astype(bf16)
        found = jnp.where(digit_a == high_digit, mm(terms, hot), 0.0)
        rel[pl.ds(key, 1), :] = jnp.sum(found, axis=0, keepdims=True)
        return carry

    lax.fori_loop(0, WTOK, one_key, 0, unroll=8)
    place = place_matrix(cols, 0)
    across = cols // WIN
    for row in range(rows):
        classes = jnp.where(iota((128, cols), 0) == region[row], 1.0, 0.0).astype(bf16)
        at = row // WIN * across
        down = row % WIN * PADDED
        ident[at : at + across, down : down + PADDED, :] = mm(place, classes, NT).reshape(
            across, PADDED, 128
        )
    bias = rel[...]
    for win in range(rows // WIN * across):
        here = ident[win]
        other = jnp.concatenate([here, jnp.zeros((QPAD - WTOK, 128), f32)], axis=0)
        other = jnp.broadcast_to(other[None], (HEADS, QPAD, 128)).reshape(wide, 128).astype(bf16)
        out_bm[win] = jnp.where(mm(here.astype(bf16), other, NT) > 0.5, bias, masked_fill)


def assemble_vectors(pieces, sources, count, offset, out_small):
    chan = pieces[0].shape[1]
    per, per_up = chan // count, 4 * chan // count
    row = iota((8, chan), 0)
    vecs, ups = jnp.zeros((8, chan), f32), jnp.zeros((8, chan), f32)
    for piece, source in zip(pieces, sources):
        block = piece[offset : offset + SMALL].astype(f32)
        vecs += pltpu.roll(block[0:8], source * per, 1)
        at = source * per_up
        line = pltpu.roll(jnp.broadcast_to(block[8:9], (8, chan)), at % chan, 1)
        ups += jnp.where(row == at // chan, line, 0.0)
    out_small[0:8] = vecs
    out_small[8:16] = ups


def gelu_parts(hidden):
    base = 1.0 + (0.3275911 * 0.5**0.5) * jnp.abs(hidden)
    term = pl.reciprocal(base, approx=True)
    term = term * (2.0 - base * term)
    bell = jnp.exp(-0.5 * (hidden * hidden))
    poly = (0.5 * 1.061405429) * term - (0.5 * 1.453152027)
    poly = poly * term + (0.5 * 1.421413741)
    poly = poly * term - (0.5 * 0.284496736)
    poly = poly * term + (0.5 * 0.254829592)
    tail = poly * term * bell
    cdf = jnp.where(hidden >= 0, 1.0 - tail, tail)
    return cdf, cdf + hidden * (bell * 0.3989422804014327)


def layer_stats(values):
    centred = values - lane_mean(values)
    rstd = lax.rsqrt(lane_mean(centred * centred) + norm_eps)
    return centred * rstd, rstd


def layer_back(d_unit, unit, rstd):
    return rstd * (d_unit - lane_mean(d_unit) - unit * lane_mean(d_unit * unit))


def my_images(me_ref, band_ref, count):
    near = count // 2
    return [me_ref[0] ^ ((band_ref[0] % 2 ^ core) * near + i) for core in range(2) for i in range(near)]


def prepare_body(tok, cot, halo, out_xw, out_cw, out_unit, out_rstd):
    rows, cols, chan = tok.shape
    across = cols // WIN
    place = place_matrix(cols, SHIFT)
    for which, source, target in ((0, tok, out_xw), (1, cot, out_cw)):
        for row in range(rows):
            line = source[row + SHIFT] if row + SHIFT < rows else halo[which, row + SHIFT - rows]
            at, down = row // WIN * across, row % WIN * PADDED
            target[at : at + across, down : down + PADDED, :] = mm(place, line).reshape(across, PADDED, chan)
    step_wins = 4
    for at in range(0, out_xw.shape[0], step_wins):
        span = slice(at, at + step_wins)
        unit, rstd = layer_stats(out_xw[span])
        out_unit[span] = unit
        out_rstd[span] = jnp.broadcast_to(rstd, unit.shape)


def attend_body(count, me_ref, band_ref, unit, bm, *refs):
    inputs = 2 if count else 5
    weights, outs = refs[:inputs], refs[inputs:]
    out_nb, out_qx, out_k, out_v, out_p, out_att, out_small, w_qkv, w_proj, w_up, w_down, mixed = outs
    wins, _, chan = unit.shape
    if count:
        sources = my_images(me_ref, band_ref, count)
        pieces = [weights[core].at[i] for core in range(2) for i in range(count // 2)]
        depth, ups = chan // count, w_up.shape[1] // chan
        deep = ups * depth
        first = (1 + 2 * ups) * depth
        for piece, source in zip(pieces, sources):
            here = pl.ds(pl.multiple_of(source * depth, depth), depth)
            for col in range(3):
                w_qkv[here, col * chan : (col + 1) * chan] = piece[first + col * depth : first + (col + 1) * depth]
            w_proj[here] = piece[0:depth]
            for col in range(ups):
                w_up[here, col * chan : (col + 1) * chan] = piece[(1 + col) * depth : (2 + col) * depth]
            w_down[pl.ds(pl.multiple_of(source * deep, deep), deep)] = piece[(1 + ups) * depth : first]
        assemble_vectors(pieces, sources, count, first + 3 * depth, out_small)
    else:
        for source, target in zip(weights, (w_qkv, out_small, w_proj, w_up, w_down)):
            target[...] = source[...]
    small = out_small[...]
    gain, shift, bias_q, bias_v = small[0:1], small[1:2], small[2:3], small[3:4]
    hmask = head_mask((HEADS, QPAD, chan))
    scale = (chan // HEADS) ** -0.5
    step_wins = 4
    weight = w_qkv[...]
    for at in range(0, wins, step_wins):
        normed = (unit[at : at + step_wins].reshape(step_wins * WTOK, chan) * gain + shift).astype(bf16)
        out_nb[at * WTOK : (at + step_wins) * WTOK] = normed
    mixed[...] = mm(out_nb[...], weight)
    for at in range(0, wins, step_wins):
        three = mixed[at * WTOK : (at + step_wins) * WTOK]
        query = three[:, :chan] + bias_q
        key = three[:, chan : 2 * chan]
        value = three[:, 2 * chan :] + bias_v
        for win in range(step_wins):
            span = slice(win * WTOK, (win + 1) * WTOK)
            out_qx[at + win] = expand_heads(query[span].astype(bf16).astype(f32), hmask)
            out_k[at + win] = key[span].astype(bf16)
            out_v[at + win] = value[span].astype(bf16)
    for at in range(0, wins, step_wins):
        group = range(at, at + step_wins)
        scores = [mm(out_k[win], out_qx[win], NT) * scale + bm[win] for win in group]
        expos = [jnp.exp(one - jnp.max(one, axis=0, keepdims=True)) for one in scores]
        probs = [one * (1.0 / jnp.sum(one, axis=0, keepdims=True)) for one in expos]
        for win, one in zip(group, probs):
            out_p[win] = one
        parts = [mm(one.astype(bf16), out_v[win], TN) for win, one in zip(group, probs)]
        for win, one in zip(group, parts):
            out_att[win] = merge_heads(one, hmask)


def mlp_body(xw, cw, att, small_ref, w_proj, w_up, w_down, *refs):
    out_bw, out_dmid, out_datt, g_proj, g_up, g_down, g_one, *scratch = refs
    att_b, n2_b, dbr_b, dy_b, act_b, dh_b, hid, dact, mid, unit2, rstd2, back = scratch
    wins, _, chan = xw.shape
    wide = w_up.shape[1]
    ups = wide // chan
    small = small_ref[...]
    bias_p, gain, shift, bias_d = small[4:5], small[5:6], small[6:7], small[7:8]
    bias_u = jnp.concatenate([small[8 + i : 9 + i] for i in range(ups)], axis=1)
    weight_p, weight_u, weight_d = w_proj[...], w_up[...], w_down[...]
    half = wins // 2
    few = 4
    full, split = (few * WTOK, chan), (few, WTOK, chan)
    sums = [jnp.zeros((1, chan), f32) for _ in range(4)]
    sum_up = jnp.zeros((8, wide), f32)

    def rows_of(at, many):
        return slice(at, at + many), slice(at * WTOK, (at + many) * WTOK)

    def enter(at):
        span, flat = rows_of(at, half)
        dy_b[flat] = cw[span].reshape(half * WTOK, chan).astype(bf16)
        dact[flat] = mm(dy_b[flat], weight_d, NT)
        att_b[flat] = att[span].reshape(half * WTOK, chan).astype(bf16)
        mid[flat] = mm(att_b[flat], weight_p)
        for some in range(at, at + half, few):
            here, line = rows_of(some, few)
            middle = xw[here].reshape(full) + (mid[line] + bias_p)
            mid[line] = middle
            unit, rstd = layer_stats(middle)
            unit2[line] = unit
            rstd2[line] = jnp.broadcast_to(rstd, full)
            n2_b[line] = (unit * gain + shift).astype(bf16)
        hid[flat] = mm(n2_b[flat], weight_u)

    def tiles(at, have):
        for row in range(at * WTOK, (at + half) * WTOK, 16):
            line = slice(row, row + 16)
            hidden = hid[line] + bias_u
            cdf, slope = gelu_parts(hidden)
            act_b[line] = (hidden * cdf).astype(bf16)
            d_hidden = dact[line] * slope
            dh_b[line] = d_hidden.astype(bf16)
            have = have + (d_hidden[0:8] + d_hidden[8:16])
        return have

    def leave(at, have):
        span, flat = rows_of(at, half)
        out_bw[span] = (mid[flat] + mm(act_b[flat], weight_d) + bias_d).reshape(half, WTOK, chan)
        back[flat] = mm(dh_b[flat], weight_u, NT)
        for some in range(at, at + half, few):
            here, line = rows_of(some, few)
            d_normed = back[line]
            unit = unit2[line]
            grad = cw[here].reshape(full)
            d_middle = grad + layer_back(d_normed * gain, unit, rstd2[line])
            out_dmid[here] = d_middle.reshape(split)
            dbr_b[line] = d_middle.astype(bf16)
            terms = (d_middle, d_normed * unit, d_normed, grad)
            have = [one + jnp.sum(term, axis=0, keepdims=True) for one, term in zip(have, terms)]
        out_datt[span] = mm(dbr_b[flat], weight_p, NT).reshape(half, WTOK, chan)
        return have

    enter(0)
    enter(half)
    sum_up = tiles(0, sum_up)
    sums = leave(0, sums)
    sum_up = tiles(half, sum_up)
    sums = leave(half, sums)
    g_one[...] = jnp.zeros_like(g_one)
    for row in range(4):
        g_one[row : row + 1] = sums[row]
    total_up = jnp.sum(sum_up, axis=0, keepdims=True)
    for col in range(ups):
        g_one[4 + col : 5 + col] = total_up[:, col * chan : (col + 1) * chan]
    g_down[...] = mm(dy_b[...], act_b[...], TN).T
    g_up[...] = mm(n2_b[...], dh_b[...], TN)
    g_proj[...] = mm(att_b[...], dbr_b[...], TN)


def back_body(count, band_ref, qx, k_ref, v_ref, p_ref, datt, dmid, nb, unit_ref, rstd_ref, *refs):
    small_ref, w_qkv, idx, g_proj, g_up, g_down, g_one, out_tw, *refs = refs
    outs, scratch = refs[:2], refs[2:]
    dq, dk, dv, mixed, d_one, drel, spread, g_qkv, g_two, g_all = scratch
    wins, _, chan = dmid.shape
    hmask = head_mask((HEADS, QPAD, chan))
    scale = (chan // HEADS) ** -0.5
    step_wins = 4
    drel[...] = jnp.zeros_like(drel)
    for at in range(0, wins, step_wins):
        group = range(at, at + step_wins)
        grads = [expand_heads(datt[win].astype(bf16).astype(f32), hmask) for win in group]
        d_probs = [mm(v_ref[win], one, NT) for win, one in zip(group, grads)]
        for win, one in zip(group, grads):
            dv[win] = mm(p_ref[win].astype(bf16), one)
        weighted = [p_ref[win] * one for win, one in zip(group, d_probs)]
        d_scores = [
            (one - p_ref[win] * jnp.sum(one, axis=0, keepdims=True)).astype(bf16) for win, one in zip(group, weighted)
        ]
        four = [one.astype(f32) for one in d_scores]
        drel[...] += (four[0] + four[1]) + (four[2] + four[3])
        for win, one in zip(group, d_scores):
            dk[win] = mm(one, qx[win]) * scale
        parts = [mm(one, k_ref[win], TN) for win, one in zip(group, d_scores)]
        for win, one in zip(group, parts):
            dq[win] = merge_heads(one, hmask) * scale
    sums = []
    for col, ref in enumerate((dq, dk, dv)):
        part = ref[...].reshape(wins * WTOK, chan).astype(bf16)
        mixed[:, col * chan : (col + 1) * chan] = part
        if col != 1:
            sums.append(jnp.sum(ref[...].reshape(wins * WTOK, chan), axis=0, keepdims=True))
    g_two[...] = jnp.zeros_like(g_two)
    g_two[2:3] = sums[0]
    g_two[3:4] = sums[1]
    g_qkv[...] = mm(nb[...], mixed[...], TN)
    weight = w_qkv[...]
    gain = small_ref[0:1]
    full = (step_wins * WTOK, chan)
    sum_gain, sum_shift = jnp.zeros((1, chan), f32), jnp.zeros((1, chan), f32)
    d_one[...] = mm(mixed[...], weight, NT)
    for at in range(0, wins, step_wins):
        span = slice(at, at + step_wins)
        d_normed = d_one[at * WTOK : (at + step_wins) * WTOK]
        unit = unit_ref[span].reshape(full)
        grad = dmid[span].reshape(full) + layer_back(d_normed * gain, unit, rstd_ref[span].reshape(full))
        out_tw[span] = grad.reshape(step_wins, WTOK, chan)
        sum_gain += jnp.sum(d_normed * unit, axis=0, keepdims=True)
        sum_shift += jnp.sum(d_normed, axis=0, keepdims=True)
    g_two[0:1] = sum_gain
    g_two[1:2] = sum_shift

    lanes = HEADS * QPAD
    row_a, row_b = iota((DIGIT, lanes), 0).astype(f32), iota((HEADS * DIGIT, lanes), 0).astype(f32)
    head_of = (iota((1, lanes), 1) // QPAD * DIGIT).astype(f32)

    def one_key(key, carry):
        line = drel[pl.ds(key, 1), :]
        entry = idx[pl.ds(key, 1), :]
        high_digit = jnp.floor(entry * (1.0 / DIGIT))
        low_digit = entry - high_digit * DIGIT + head_of
        left = jnp.where(row_a == high_digit, line, 0.0).astype(bf16)
        right = jnp.where(row_b == low_digit, 1.0, 0.0).astype(bf16)
        spread[key] = mm(left, right, NT)
        return carry

    lax.fori_loop(0, WTOK, one_key, 0, unroll=8)
    table = jnp.sum(spread[...], axis=0)
    g_two[4:SMALL, 0 : HEADS * DIGIT] = table[0 : SMALL - 4]
    if not count:
        outs[0][...] = g_qkv[...]
        outs[1][...] = g_two[...]
        return
    depth, ups = chan // count, g_up.shape[1] // chan
    deep = ups * depth
    first = (1 + 2 * ups) * depth
    for dest in range(count):
        at = dest * depth
        g_all[dest, 0:depth] = g_proj[at : at + depth].astype(bf16)
        for col in range(ups):
            part = g_up[at : at + depth, col * chan : (col + 1) * chan]
            g_all[dest, (1 + col) * depth : (2 + col) * depth] = part.astype(bf16)
        g_all[dest, (1 + ups) * depth : first] = g_down[dest * deep : (dest + 1) * deep].astype(bf16)
        for col in range(3):
            part = g_qkv[at : at + depth, col * chan : (col + 1) * chan]
            g_all[dest, first + col * depth : first + (col + 1) * depth] = part.astype(bf16)
        g_all[dest, first + 3 * depth : first + 3 * depth + SMALL] = g_one[...].astype(bf16)
        g_all[dest, first + 3 * depth + SMALL :] = g_two[...].astype(bf16)
    side = band_ref[0] % 2
    many = g_all.shape[1] // 2
    outs[0][...] = g_all[:, pl.ds(pl.multiple_of(side * many, many), many), :]
    outs[1][...] = g_all[:, pl.ds(pl.multiple_of((1 - side) * many, many), many), :]


def rows_body(bw, tw, out_bo, out_tg, out_halo):
    rows, cols, chan = out_bo.shape
    across = cols // WIN
    place = place_matrix(cols, SHIFT)
    twice = jnp.concatenate([place, place], axis=0)
    for row in range(rows):
        at, down = row // WIN * across, row % WIN * PADDED
        block = bw[at : at + across, down : down + PADDED, :].reshape(across * PADDED, chan).astype(bf16)
        block = mm(place, block, TN).astype(bf16)
        grad = tw[at : at + across, down : down + PADDED, :].reshape(across * PADDED, chan)
        high = grad.astype(bf16)
        low = (grad - high.astype(f32)).astype(bf16)
        grad = mm(twice, jnp.concatenate([high, low], axis=0), TN)
        if row + SHIFT < rows:
            out_bo[row + SHIFT] = block
            out_tg[row + SHIFT] = grad
        else:
            out_halo[0, row + SHIFT - rows] = block
            out_halo[1, row + SHIFT - rows] = grad.astype(bf16)
    for row in range(SHIFT):
        out_bo[row] = jnp.zeros((cols, chan), bf16)
        out_tg[row] = jnp.zeros((cols, chan), f32)


def total(refs):
    parts = [refs[source][...].astype(f32) for source in range(len(refs))]
    while len(parts) > 1:
        parts = [parts[i] + parts[i + 1] for i in range(0, len(parts), 2)]
    return parts[0]


def pair_body(mine, other, out):
    out[...] = (mine[...].astype(f32) + other[...].astype(f32)).astype(bf16)


def sum_body(pieces, out):
    out[...] = total([pieces.at[i] for i in range(pieces.shape[0])]).astype(bf16)


def final_body(bands, me_ref, band_ref, bo, tg, halo, *refs):
    both, outs, (rows_f, sems) = refs[:bands], refs[bands:-2], refs[-2:]
    (
        out_bo, out_tg, o_gain_one, o_shift_one, o_qkv, o_query, o_value, o_proj, o_bias_proj,
        o_gain_two, o_shift_two, o_up, o_bias_up, o_down, o_bias_down, o_table,
    ) = outs
    rows_f[...] = halo[1].astype(f32)
    copies = [
        pltpu.make_async_copy(halo.at[0], out_bo.at[0:SHIFT], sems.at[0]),
        pltpu.make_async_copy(rows_f, out_tg.at[0:SHIFT], sems.at[1]),
    ]
    for copy in copies:
        copy.start()
    me = me_ref[0]
    depth, chan = o_proj.shape
    ups = o_up.shape[1] // chan
    mine = total([both[step] for step in range(0, bands, 2)])
    other = total([both[step] for step in range(1, bands, 2)])
    even = band_ref[0] % 2 == 0
    summed = jnp.concatenate([jnp.where(even, mine, other), jnp.where(even, other, mine)], axis=0)
    first = (1 + 2 * ups) * depth
    o_proj[...] = summed[0:depth]
    for col in range(ups):
        o_up[:, col * chan : (col + 1) * chan] = summed[(1 + col) * depth : (2 + col) * depth]
    o_down[...] = summed[(1 + ups) * depth : first]
    for col in range(3):
        o_qkv[:, col * chan : (col + 1) * chan] = summed[first + col * depth : first + (col + 1) * depth]
    early = summed[first + 3 * depth : first + 3 * depth + SMALL]
    late = summed[first + 3 * depth + SMALL :]
    mine = jnp.concatenate([early[0:8], late[0:8]], axis=0)
    turned = pltpu.roll(mine, (chan - me * depth) % chan, 1)
    o_bias_proj[...] = turned[0:1, :depth]
    o_gain_two[...] = turned[1:2, :depth]
    o_shift_two[...] = turned[2:3, :depth]
    o_bias_down[...] = turned[3:4, :depth]
    o_gain_one[...] = turned[8:9, :depth]
    o_shift_one[...] = turned[9:10, :depth]
    o_query[...] = turned[10:11, :depth]
    o_value[...] = turned[11:12, :depth]
    at = me * depth * ups
    chosen = jnp.where(iota((8, chan), 0) == 4 + at // chan, early[0:8], 0.0)
    chosen = jnp.broadcast_to(jnp.sum(chosen, axis=0, keepdims=True), (8, chan))
    chosen = pltpu.roll(chosen, (chan - at % chan) % chan, 1)
    o_bias_up[...] = chosen[0:1, : depth * ups]
    for head in range(HEADS):
        for digit in range((TABLE + DIGIT - 1) // DIGIT):
            width = min(DIGIT, TABLE - digit * DIGIT)
            o_table[head : head + 1, digit * DIGIT : digit * DIGIT + width] = late[
                4 + digit : 5 + digit, head * DIGIT : head * DIGIT + width
            ]
    for copy in copies:
        copy.wait()


def call(body, outs, *args, scratch=(), ins=None, outs_at=None, name=None, limit=16, micros=1, aliases=None):
    at = lambda space: pl.BlockSpec(memory_space=space)
    return pl.pallas_call(
        body,
        out_shape=[jax.ShapeDtypeStruct(shape, dtype) for shape, dtype in outs],
        in_specs=[at(space) for space in (ins or [VMEM] * len(args))],
        out_specs=[at(space) for space in (outs_at or [VMEM] * len(outs))],
        scratch_shapes=[VMEM(*one) if isinstance(one, tuple) else one for one in scratch],
        input_output_aliases=aliases or {},
        compiler_params=pltpu.CompilerParams(vmem_limit_bytes=limit << 20),
        cost_estimate=pl.CostEstimate(flops=micros * 10**9, bytes_accessed=micros * 3 * 10**6, transcendentals=0),
        name=name,
    )(*args)


def shifted(value, axis, steps):
    count = lax.axis_size(axis)
    return lax.ppermute(value, axis, [(source, (source + steps) % count) for source in range(count)])


def swap(value, axis, step):
    count = lax.axis_size(axis)
    return lax.ppermute(value, axis, [(source, source ^ step) for source in range(count)])


def spread_out(value, i):
    bands, images = lax.axis_size("seq"), lax.axis_size("fsdp")
    pairs = [
        (band * images + image, band * images + (image ^ (band % 2 * (images // 2) + i)))
        for band in range(bands)
        for image in range(images)
    ]
    return lax.ppermute(value, ("seq", "fsdp"), pairs)


def on_device(
    tokens_in, first_gain, first_shift, qkv_weight, query_bias, value_bias, proj_weight, proj_bias,
    second_gain, second_shift, up_weight, up_bias, down_weight, down_bias, bias_table, table_index,
    region_ids, cotangent,
):
    images, rows, cols, chan = tokens_in.shape
    assert images == 1
    fsdp, bands = lax.axis_size("fsdp"), lax.axis_size("seq")
    wide = up_weight.shape[1]
    depth = proj_weight.shape[0]
    wins = rows // WIN * (cols // WIN)
    direct = depth % 16 == 0
    count = fsdp if direct else 0
    tok, cot = tokens_in[0], cotangent[0]
    region = region_ids.reshape(rows, 1, cols)
    vectors = (
        first_gain, first_shift, query_bias, value_bias, proj_bias, second_gain, second_shift, down_bias, up_bias,
    )
    tokw = (wins, WTOK, chan)
    flatw = (wins * WTOK, chan)
    flatu = (wins * WTOK, wide)
    ups = wide // chan
    piece_rows = (1 + 2 * ups) * depth + 3 * depth + SMALL
    wide_scores = (wins, WTOK, HEADS * QPAD)
    sems = lambda many: pltpu.SemaphoreType.DMA((many,))
    near = fsdp // 2
    me = lax.axis_index("fsdp").astype(jnp.int32).reshape(1)
    band = lax.axis_index("seq").astype(jnp.int32).reshape(1)
    if direct:
        held = [vector.reshape(1, -1) for vector in vectors] + [qkv_weight, proj_weight, up_weight, down_weight]
        piece, halo = call(
            pack_body,
            [((piece_rows, chan), bf16), ((2, SHIFT, cols, chan), bf16)],
            *held, tok, cot, name="pack", limit=58, ins=[pl.ANY] * 15,
            scratch=[(array.shape, bf16) for array in held] + [sems(15)],
        )
        fetched = [spread_out(piece, i) for i in range(near)]
    else:
        halo = jnp.stack([tok[:SHIFT], cot[:SHIFT]])
        gather = functools.partial(lax.all_gather, axis_name="fsdp", axis=0, tiled=True)
        full = [gather(vector).astype(f32).reshape(-1, chan) for vector in vectors]
        full.append(jnp.zeros((SMALL - 8 - ups, chan), f32))
        weights = [
            gather(qkv_weight), jnp.concatenate(full, axis=0), gather(proj_weight), gather(up_weight),
            gather(down_weight),
        ]
    halo = shifted(halo, "seq", -1)
    bm, idx = call(
        bias_body,
        [(wide_scores, f32), ((WTOK, HEADS * QPAD), f32)],
        region, bias_table.T, table_index, tok, cot,
        scratch=[((DIGIT, HEADS * DIGIT), f32), ((WTOK, HEADS * QPAD), f32), ((wins, WTOK, 128), f32)],
        name="score_bias", micros=3,
    )
    if direct:
        *fetched, bm, idx = lax.optimization_barrier((*fetched, bm, idx))
        (pair,) = call(join_body, [((near, piece_rows, chan), bf16)], *fetched, name="join")
        weights = [pair, swap(pair, "seq", 1)]
    xw, cw, unit, rstd = call(prepare_body, [(tokw, f32)] * 4, tok, cot, halo, name="prepare", micros=2)
    big = dict(limit=32)
    place = [pltpu.SMEM] * 2
    nb, qx, k_b, v_b, probs, att, small, w_qkv, w_proj, w_up, w_down = call(
        functools.partial(attend_body, count),
        [
            (flatw, bf16), ((wins, HEADS * QPAD, chan), bf16), (tokw, bf16), (tokw, bf16), (wide_scores, f32),
            (tokw, f32), ((SMALL, chan), f32), ((chan, 3 * chan), bf16), ((chan, chan), bf16), ((chan, wide), bf16),
            ((wide, chan), bf16),
        ],
        me, band, unit, bm, *weights, name="attention", micros=3, ins=place + [VMEM] * (2 + len(weights)), **big,
        scratch=[((wins * WTOK, 3 * chan), f32)],
    )
    bw, dmid, datt, g_proj, g_up, g_down, g_one = call(
        mlp_body,
        [
            (tokw, f32), (tokw, f32), (tokw, f32), ((chan, chan), f32), ((chan, wide), f32), ((wide, chan), f32),
            ((SMALL, chan), f32),
        ],
        xw, cw, att, small, w_proj, w_up, w_down, name="feed_forward", micros=5, **big,
        scratch=[(flatw, bf16)] * 4 + [(flatu, bf16)] * 2 + [(flatu, f32)] * 2 + [(flatw, f32)] * 4,
    )
    if direct:
        halves = ((fsdp, (piece_rows + SMALL) // 2, chan), bf16)
        sent = [halves] * 2
    else:
        sent = [((chan, 3 * chan), f32), ((SMALL, chan), f32)]
    tw, *grads = call(
        functools.partial(back_body, count),
        [(tokw, f32)] + sent,
        band, qx, k_b, v_b, probs, datt, dmid, nb, unit, rstd, small, w_qkv, idx, g_proj, g_up, g_down, g_one,
        name="attention_back", micros=5, ins=place[:1] + [VMEM] * 16, **big,
        scratch=[
            (tokw, f32), (tokw, f32), (tokw, f32), ((wins * WTOK, 3 * chan), bf16), (flatw, f32),
            ((WTOK, HEADS * QPAD), f32), ((WTOK, DIGIT, HEADS * DIGIT), f32), ((chan, 3 * chan), f32), ((SMALL, chan), f32),
            ((max(count, 1), piece_rows + SMALL, chan), bf16),
        ],
    )
    bo, tg, last = call(
        rows_body,
        [((rows, cols, chan), bf16), ((rows, cols, chan), f32), ((2, SHIFT, cols, chan), bf16)],
        bw, tw, name="rows", micros=2,
    )
    if not direct:
        last = shifted(last, "seq", 1)
        g_proj, g_up, g_down, early, g_qkv, late = lax.psum((g_proj, g_up, g_down, g_one, *grads), "seq")
        digits = (TABLE + DIGIT - 1) // DIGIT
        table = lax.psum(late[4 : 4 + digits, : HEADS * DIGIT], "fsdp").reshape(digits, HEADS, DIGIT)
        table = table.transpose(1, 0, 2).reshape(HEADS, digits * DIGIT)[:, :TABLE]
        scatter = functools.partial(lax.psum_scatter, axis_name="fsdp", scatter_dimension=0, tiled=True)
        block_out = jnp.concatenate([last[0], bo[SHIFT:]], axis=0)
        tokens_grad = jnp.concatenate([last[1].astype(f32), tg[SHIFT:]], axis=0)
        return (
            block_out[None], tokens_grad[None], scatter(late[0]), scatter(late[1]), scatter(g_qkv),
            scatter(late[2]), scatter(late[3]), scatter(g_proj), scatter(early[0]), scatter(early[1]),
            scatter(early[2]), scatter(g_up), scatter(early[4 : 4 + ups].reshape(-1)),
            scatter(g_down), scatter(early[3]), table.T,
        )
    kept, given = grads[0], swap(grads[1], "seq", 1)
    kept, given, last = lax.optimization_barrier((kept, given, last))
    last = shifted(last, "seq", 1)
    (kept,) = call(pair_body, [halves], kept, given, name="sum_cores")
    pieces = lax.all_to_all(kept, "fsdp", 0, 0, tiled=True)
    (both,) = call(sum_body, [(halves[0][1:], bf16)], pieces, name="sum_images")
    arrived = [both] + [swap(both, "seq", step) for step in range(1, bands)]
    line = ((1, depth), f32)
    outs = call(
        functools.partial(final_body, bands),
        [
            ((rows, cols, chan), bf16), ((rows, cols, chan), f32), line, line, ((depth, 3 * chan), f32), line,
            line, ((depth, chan), f32), line, line, line, ((depth, wide), f32), ((1, depth * ups), f32),
            ((depth * ups, chan), f32), line, ((HEADS, TABLE), f32),
        ],
        me, band, bo, tg, last, *arrived, name="finish", aliases={2: 0, 3: 1},
        ins=[pltpu.SMEM] * 2 + [pl.ANY] * 2 + [VMEM] * (1 + bands), outs_at=[pl.ANY, pl.ANY] + [VMEM] * 14,
        scratch=[((SHIFT, cols, chan), f32), sems(2)],
    )
    outs = [out.reshape(-1) if out.shape[0] == 1 else out for out in outs]
    return (outs[0][None], outs[1][None], *outs[2:15], outs[15].T)


def solution(mesh):
    placed = (
        P("fsdp", "seq", None, None),
        P("fsdp"),
        P("fsdp"),
        P("fsdp", None),
        P("fsdp"),
        P("fsdp"),
        P("fsdp", None),
        P("fsdp"),
        P("fsdp"),
        P("fsdp"),
        P("fsdp", None),
        P("fsdp"),
        P("fsdp", None),
        P("fsdp"),
        P(),
        P(),
        P("fsdp", "seq", None),
        P("fsdp", "seq", None, None),
    )
    return jax.shard_map(
        on_device,
        mesh=mesh,
        in_specs=placed,
        out_specs=(
            P("fsdp", "seq", None, None),
            P("fsdp", "seq", None, None),
            P("fsdp"),
            P("fsdp"),
            P("fsdp", None),
            P("fsdp"),
            P("fsdp"),
            P("fsdp", None),
            P("fsdp"),
            P("fsdp"),
            P("fsdp"),
            P("fsdp", None),
            P("fsdp"),
            P("fsdp", None),
            P("fsdp"),
            P(),
        ),
        check_vma=False,
    )
```

```python
import functools

import jax
import jax.numpy as jnp
from jax import lax
from jax.experimental import pallas as pl
from jax.experimental.pallas import tpu as pltpu
from jax.sharding import PartitionSpec as P

HEADS = 4
WIN = 7
SHIFT = 3
TABLE = 169
PADDED = 8
WTOK = WIN * PADDED
QPAD = 64
SMALL = 16
DIGIT = 16

norm_eps = 1e-05
masked_fill = -1e30
f32 = jnp.float32
bf16 = jnp.bfloat16
NT = (((1,), (1,)), ((), ()))
TN = (((0,), (0,)), ((), ()))
VMEM = pltpu.VMEM


def mm(left, right, dims=(((1,), (0,)), ((), ()))):
    return lax.dot_general(left, right, dims, preferred_element_type=f32)


def iota(shape, axis):
    return lax.broadcasted_iota(jnp.int32, shape, axis)


def place_matrix(cols, roll):
    spots = cols // WIN * PADDED
    spot, col = iota((spots, cols), 0), iota((spots, cols), 1)
    place = spot % PADDED
    target = spot // PADDED * WIN + place + roll
    target = jnp.where(target >= cols, target - cols, target)
    return jnp.where((place < WIN) & (col == target), 1.0, 0.0).astype(bf16)


def head_mask(shape, lane_axis=1):
    chans = shape[-1] // HEADS
    return jnp.where(iota(shape, len(shape) - 1) // chans == iota(shape, 0), 1.0, 0.0)


def expand_heads(tokens, hmask):
    zeros = jnp.zeros((QPAD - WTOK, tokens.shape[1]), f32)
    full = jnp.concatenate([tokens, zeros], axis=0)
    return (full[None] * hmask).reshape(HEADS * QPAD, tokens.shape[1]).astype(bf16)


def merge_heads(stacked, hmask):
    parts = stacked.reshape(HEADS, QPAD, stacked.shape[1]) * hmask
    return ((parts[0] + parts[1]) + (parts[2] + parts[3]))[:WTOK]


def lane_mean(values):
    return jnp.mean(values, axis=-1, keepdims=True)


def pack_body(*refs):
    given, (out, out_h), scratch, sems = refs[:15], refs[15:17], refs[17:-1], refs[-1]
    sources = list(given[:13]) + [ref.at[0:SHIFT] for ref in given[13:]]
    targets = list(scratch) + [out_h.at[0], out_h.at[1]]
    copies = [
        pltpu.make_async_copy(source, target, sems.at[i])
        for i, (source, target) in enumerate(zip(sources, targets))
    ]
    for copy in copies:
        copy.start()
    for copy in copies:
        copy.wait()
    vectors, (qkv, proj, up, down) = scratch[:9], scratch[9:]
    depth, chan = proj.shape
    blocks, ups = qkv.shape[1] // chan, up.shape[1] // chan
    small = jnp.concatenate(
        [jnp.pad(vector[...].astype(f32), ((0, 0), (0, chan - vector.shape[1]))) for vector in vectors]
        + [jnp.zeros((SMALL - 9, chan), f32)],
        axis=0,
    ).astype(bf16)
    parts = [proj[...]]
    parts += [up[:, col * chan : (col + 1) * chan] for col in range(ups)]
    parts += [down[...]]
    parts += [qkv[:, col * chan : (col + 1) * chan] for col in range(blocks)]
    parts += [small]
    at = 0
    for part in parts:
        out[at : at + part.shape[0]] = part
        at += part.shape[0]


def join_body(*refs):
    for i, piece in enumerate(refs[:-1]):
        refs[-1][i] = piece[...]


def bias_body(region, table, index, tok, cot, out_bm, out_idx, tab, rel, ident):
    rows, _, cols = region.shape
    tokens = index.shape[0]
    wide = HEADS * QPAD
    token_a, spot_a = iota((tokens, WTOK), 0), iota((tokens, WTOK), 1)
    keys_at = jnp.where(token_a // WIN * PADDED + token_a % WIN == spot_a, 1.0, 0.0).astype(bf16)
    token_b, lane_b = iota((tokens, wide), 0), iota((tokens, wide), 1)
    queries_at = jnp.where(token_b // WIN * PADDED + token_b % WIN == lane_b % QPAD, 1.0, 0.0).astype(bf16)
    half = mm(index[...].astype(f32).astype(bf16), keys_at).astype(bf16)
    out_idx[...] = mm(half, queries_at, TN)
    tab[...] = jnp.zeros_like(tab)
    for head in range(HEADS):
        for digit in range((TABLE + DIGIT - 1) // DIGIT):
            width = min(DIGIT, TABLE - digit * DIGIT)
            tab[digit : digit + 1, head * DIGIT : head * DIGIT + width] = table[
                head : head + 1, digit * DIGIT : digit * DIGIT + width
            ]
    entries = tab[...]
    first = entries.astype(bf16).astype(f32)
    second = (entries - first).astype(bf16).astype(f32)
    terms = jnp.concatenate([first, second, entries - first - second], axis=0).astype(bf16)
    digit_a = (iota((3 * DIGIT, wide), 0) % DIGIT).astype(f32)
    row_b = iota((HEADS * DIGIT, wide), 0).astype(f32)
    head_of = (iota((1, wide), 1) // QPAD * DIGIT).astype(f32)

    for start in range(0, WTOK, 8):
        keys = range(start, start + 8)
        lines = [out_idx[key : key + 1, :] for key in keys]
        highs = [jnp.floor(entry * (1.0 / DIGIT)) for entry in lines]
        lows = [entry - high * DIGIT + head_of for entry, high in zip(lines, highs)]
        found = [mm(terms, jnp.where(row_b == low, 1.0, 0.0).astype(bf16)) for low in lows]
        found = [jnp.where(digit_a == high, one, 0.0) for high, one in zip(highs, found)]
        for key, one in zip(keys, found):
            rel[key : key + 1, :] = jnp.sum(one, axis=0, keepdims=True)
    place = place_matrix(cols, 0)
    across = cols // WIN
    for row in range(rows):
        classes = jnp.where(iota((128, cols), 0) == region[row], 1.0, 0.0).astype(bf16)
        at = row // WIN * across
        down = row % WIN * PADDED
        ident[at : at + across, down : down + PADDED, :] = mm(place, classes, NT).reshape(
            across, PADDED, 128
        )
    bias = rel[...]
    for win in range(rows // WIN * across):
        here = ident[win]
        other = jnp.concatenate([here, jnp.zeros((QPAD - WTOK, 128), f32)], axis=0)
        other = jnp.broadcast_to(other[None], (HEADS, QPAD, 128)).reshape(wide, 128).astype(bf16)
        out_bm[win] = jnp.where(mm(here.astype(bf16), other, NT) > 0.5, bias, masked_fill)


def assemble_vectors(pieces, sources, count, offset, out_small):
    chan = pieces[0].shape[1]
    per, per_up = chan // count, 4 * chan // count
    row = iota((8, chan), 0)
    vecs, ups = jnp.zeros((8, chan), f32), jnp.zeros((8, chan), f32)
    for piece, source in zip(pieces, sources):
        block = piece[offset : offset + SMALL].astype(f32)
        vecs += pltpu.roll(block[0:8], source * per, 1)
        at = source * per_up
        line = pltpu.roll(jnp.broadcast_to(block[8:9], (8, chan)), at % chan, 1)
        ups += jnp.where(row == at // chan, line, 0.0)
    out_small[0:8] = vecs
    out_small[8:16] = ups


def gelu_parts(hidden):
    base = 1.0 + (0.3275911 * 0.5**0.5) * jnp.abs(hidden)
    term = pl.reciprocal(base, approx=True)
    term = term * (2.0 - base * term)
    bell = jnp.exp(-0.5 * (hidden * hidden))
    poly = (0.5 * 1.061405429) * term - (0.5 * 1.453152027)
    poly = poly * term + (0.5 * 1.421413741)
    poly = poly * term - (0.5 * 0.284496736)
    poly = poly * term + (0.5 * 0.254829592)
    tail = poly * term * bell
    cdf = jnp.where(hidden >= 0, 1.0 - tail, tail)
    return cdf, cdf + hidden * (bell * 0.3989422804014327)


def layer_stats(values):
    centred = values - lane_mean(values)
    rstd = lax.rsqrt(lane_mean(centred * centred) + norm_eps)
    return centred * rstd, rstd


def layer_back(d_unit, unit, rstd):
    return rstd * (d_unit - lane_mean(d_unit) - unit * lane_mean(d_unit * unit))


def my_images(me_ref, band_ref, count):
    near = count // 2
    return [me_ref[0] ^ ((band_ref[0] % 2 ^ core) * near + i) for core in range(2) for i in range(near)]


def prepare_body(tok, cot, halo_one, halo_two, out_xw, out_cw, out_unit, out_rstd):
    rows, cols, chan = tok.shape
    across = cols // WIN
    place = place_matrix(cols, SHIFT)
    for which, source, target in ((0, tok, out_xw), (1, cot, out_cw)):
        for row in range(rows):
            if row + SHIFT < rows:
                line = source[row + SHIFT]
            else:
                over = row + SHIFT - rows
                line = (halo_one[which, over].astype(f32) + halo_two[which, over].astype(f32)).astype(bf16)
            at, down = row // WIN * across, row % WIN * PADDED
            target[at : at + across, down : down + PADDED, :] = mm(place, line).reshape(across, PADDED, chan)
    step_wins = 4
    for at in range(0, out_xw.shape[0], step_wins):
        span = slice(at, at + step_wins)
        unit, rstd = layer_stats(out_xw[span])
        out_unit[span] = unit
        out_rstd[span] = jnp.broadcast_to(rstd, unit.shape)


def attend_body(count, me_ref, band_ref, unit, bm, *refs):
    inputs = 2 if count else 5
    weights, outs = refs[:inputs], refs[inputs:]
    out_nb, out_qx, out_k, out_v, out_p, out_att, out_small, w_qkv, w_proj, w_up, w_down, mixed = outs
    wins, _, chan = unit.shape
    if count:
        sources = my_images(me_ref, band_ref, count)
        pieces = [weights[core].at[i] for core in range(2) for i in range(count // 2)]
        depth, ups = chan // count, w_up.shape[1] // chan
        deep = ups * depth
        first = (1 + 2 * ups) * depth
        for piece, source in zip(pieces, sources):
            here = pl.ds(pl.multiple_of(source * depth, depth), depth)
            for col in range(3):
                w_qkv[here, col * chan : (col + 1) * chan] = piece[first + col * depth : first + (col + 1) * depth]
            w_proj[here] = piece[0:depth]
            for col in range(ups):
                w_up[here, col * chan : (col + 1) * chan] = piece[(1 + col) * depth : (2 + col) * depth]
            w_down[pl.ds(pl.multiple_of(source * deep, deep), deep)] = piece[(1 + ups) * depth : first]
        assemble_vectors(pieces, sources, count, first + 3 * depth, out_small)
    else:
        for source, target in zip(weights, (w_qkv, out_small, w_proj, w_up, w_down)):
            target[...] = source[...]
    small = out_small[...]
    gain, shift, bias_q, bias_v = small[0:1], small[1:2], small[2:3], small[3:4]
    hmask = head_mask((HEADS, QPAD, chan))
    scale = (chan // HEADS) ** -0.5
    step_wins = 4
    weight = w_qkv[...]
    for at in range(0, wins, step_wins):
        normed = (unit[at : at + step_wins].reshape(step_wins * WTOK, chan) * gain + shift).astype(bf16)
        out_nb[at * WTOK : (at + step_wins) * WTOK] = normed
    mixed[...] = mm(out_nb[...], weight)
    for at in range(0, wins, step_wins):
        three = mixed[at * WTOK : (at + step_wins) * WTOK]
        query = three[:, :chan] + bias_q
        key = three[:, chan : 2 * chan]
        value = three[:, 2 * chan :] + bias_v
        for win in range(step_wins):
            span = slice(win * WTOK, (win + 1) * WTOK)
            out_qx[at + win] = expand_heads(query[span].astype(bf16).astype(f32), hmask)
            out_k[at + win] = key[span].astype(bf16)
            out_v[at + win] = value[span].astype(bf16)
    for at in range(0, wins, step_wins):
        group = range(at, at + step_wins)
        scores = [mm(out_k[win], out_qx[win], NT) * scale + bm[win] for win in group]
        expos = [jnp.exp(one - jnp.max(one, axis=0, keepdims=True)) for one in scores]
        probs = [one * (1.0 / jnp.sum(one, axis=0, keepdims=True)) for one in expos]
        for win, one in zip(group, probs):
            out_p[win] = one
        parts = [mm(one.astype(bf16), out_v[win], TN) for win, one in zip(group, probs)]
        for win, one in zip(group, parts):
            out_att[win] = merge_heads(one, hmask)


def mlp_body(xw, cw, att, small_ref, w_proj, w_up, w_down, *refs):
    out_bw, out_dmid, out_datt, g_proj, g_up, g_down, g_one, *scratch = refs
    att_b, n2_b, dbr_b, dy_b, act_b, dh_b, hid, dact, mid, unit2, rstd2, back = scratch
    wins, _, chan = xw.shape
    wide = w_up.shape[1]
    ups = wide // chan
    small = small_ref[...]
    bias_p, gain, shift, bias_d = small[4:5], small[5:6], small[6:7], small[7:8]
    bias_u = jnp.concatenate([small[8 + i : 9 + i] for i in range(ups)], axis=1)
    weight_p, weight_u, weight_d = w_proj[...], w_up[...], w_down[...]
    half = wins // 2
    few = 4
    full, split = (few * WTOK, chan), (few, WTOK, chan)
    sums = [jnp.zeros((1, chan), f32) for _ in range(4)]
    sum_up = jnp.zeros((8, wide), f32)

    def rows_of(at, many):
        return slice(at, at + many), slice(at * WTOK, (at + many) * WTOK)

    def enter(at):
        span, flat = rows_of(at, half)
        dy_b[flat] = cw[span].reshape(half * WTOK, chan).astype(bf16)
        dact[flat] = mm(dy_b[flat], weight_d, NT)
        att_b[flat] = att[span].reshape(half * WTOK, chan).astype(bf16)
        mid[flat] = mm(att_b[flat], weight_p)
        for some in range(at, at + half, few):
            here, line = rows_of(some, few)
            middle = xw[here].reshape(full) + (mid[line] + bias_p)
            mid[line] = middle
            unit, rstd = layer_stats(middle)
            unit2[line] = unit
            rstd2[line] = jnp.broadcast_to(rstd, full)
            n2_b[line] = (unit * gain + shift).astype(bf16)
        hid[flat] = mm(n2_b[flat], weight_u)

    def tiles(at, have):
        for row in range(at * WTOK, (at + half) * WTOK, 16):
            line = slice(row, row + 16)
            hidden = hid[line] + bias_u
            cdf, slope = gelu_parts(hidden)
            act_b[line] = (hidden * cdf).astype(bf16)
            d_hidden = dact[line] * slope
            dh_b[line] = d_hidden.astype(bf16)
            have = have + (d_hidden[0:8] + d_hidden[8:16])
        return have

    def leave(at, have):
        span, flat = rows_of(at, half)
        out_bw[span] = (mid[flat] + mm(act_b[flat], weight_d) + bias_d).reshape(half, WTOK, chan)
        back[flat] = mm(dh_b[flat], weight_u, NT)
        for some in range(at, at + half, few):
            here, line = rows_of(some, few)
            d_normed = back[line]
            unit = unit2[line]
            grad = cw[here].reshape(full)
            d_middle = grad + layer_back(d_normed * gain, unit, rstd2[line])
            out_dmid[here] = d_middle.reshape(split)
            dbr_b[line] = d_middle.astype(bf16)
            terms = (d_middle, d_normed * unit, d_normed, grad)
            have = [one + jnp.sum(term, axis=0, keepdims=True) for one, term in zip(have, terms)]
        out_datt[span] = mm(dbr_b[flat], weight_p, NT).reshape(half, WTOK, chan)
        return have

    enter(0)
    enter(half)
    sum_up = tiles(0, sum_up)
    sums = leave(0, sums)
    sum_up = tiles(half, sum_up)
    sums = leave(half, sums)
    g_one[...] = jnp.zeros_like(g_one)
    for row in range(4):
        g_one[row : row + 1] = sums[row]
    total_up = jnp.sum(sum_up, axis=0, keepdims=True)
    for col in range(ups):
        g_one[4 + col : 5 + col] = total_up[:, col * chan : (col + 1) * chan]
    g_down[...] = mm(dy_b[...], act_b[...], TN).T
    g_up[...] = mm(n2_b[...], dh_b[...], TN)
    g_proj[...] = mm(att_b[...], dbr_b[...], TN)


def back_body(count, band_ref, qx, k_ref, v_ref, p_ref, datt, dmid, nb, unit_ref, rstd_ref, *refs):
    small_ref, w_qkv, idx, g_proj, g_up, g_down, g_one, out_tw, *refs = refs
    outs, scratch = refs[:2], refs[2:]
    dq, dk, dv, mixed, d_one, drel, spread, g_qkv, g_two, g_all = scratch
    wins, _, chan = dmid.shape
    hmask = head_mask((HEADS, QPAD, chan))
    scale = (chan // HEADS) ** -0.5
    step_wins = 4
    drel[...] = jnp.zeros_like(drel)
    for at in range(0, wins, step_wins):
        group = range(at, at + step_wins)
        grads = [expand_heads(datt[win].astype(bf16).astype(f32), hmask) for win in group]
        d_probs = [mm(v_ref[win], one, NT) for win, one in zip(group, grads)]
        for win, one in zip(group, grads):
            dv[win] = mm(p_ref[win].astype(bf16), one)
        weighted = [p_ref[win] * one for win, one in zip(group, d_probs)]
        d_scores = [
            (one - p_ref[win] * jnp.sum(one, axis=0, keepdims=True)).astype(bf16) for win, one in zip(group, weighted)
        ]
        four = [one.astype(f32) for one in d_scores]
        drel[...] += (four[0] + four[1]) + (four[2] + four[3])
        for win, one in zip(group, d_scores):
            dk[win] = mm(one, qx[win]) * scale
        parts = [mm(one, k_ref[win], TN) for win, one in zip(group, d_scores)]
        for win, one in zip(group, parts):
            dq[win] = merge_heads(one, hmask) * scale
    sums = []
    for col, ref in enumerate((dq, dk, dv)):
        part = ref[...].reshape(wins * WTOK, chan).astype(bf16)
        mixed[:, col * chan : (col + 1) * chan] = part
        if col != 1:
            sums.append(jnp.sum(ref[...].reshape(wins * WTOK, chan), axis=0, keepdims=True))
    g_two[...] = jnp.zeros_like(g_two)
    g_two[2:3] = sums[0]
    g_two[3:4] = sums[1]
    g_qkv[...] = mm(nb[...], mixed[...], TN)
    weight = w_qkv[...]
    gain = small_ref[0:1]
    full = (step_wins * WTOK, chan)
    sum_gain, sum_shift = jnp.zeros((1, chan), f32), jnp.zeros((1, chan), f32)
    d_one[...] = mm(mixed[...], weight, NT)
    for at in range(0, wins, step_wins):
        span = slice(at, at + step_wins)
        d_normed = d_one[at * WTOK : (at + step_wins) * WTOK]
        unit = unit_ref[span].reshape(full)
        grad = dmid[span].reshape(full) + layer_back(d_normed * gain, unit, rstd_ref[span].reshape(full))
        out_tw[span] = grad.reshape(step_wins, WTOK, chan)
        sum_gain += jnp.sum(d_normed * unit, axis=0, keepdims=True)
        sum_shift += jnp.sum(d_normed, axis=0, keepdims=True)
    g_two[0:1] = sum_gain
    g_two[1:2] = sum_shift

    lanes = HEADS * QPAD
    row_a, row_b = iota((DIGIT, lanes), 0).astype(f32), iota((HEADS * DIGIT, lanes), 0).astype(f32)
    head_of = (iota((1, lanes), 1) // QPAD * DIGIT).astype(f32)

    for start in range(0, WTOK, 8):
        keys = range(start, start + 8)
        entries = [idx[key : key + 1, :] for key in keys]
        highs = [jnp.floor(entry * (1.0 / DIGIT)) for entry in entries]
        lows = [entry - high * DIGIT + head_of for entry, high in zip(entries, highs)]
        lefts = [
            jnp.where(row_a == high, drel[key : key + 1, :], 0.0).astype(bf16) for key, high in zip(keys, highs)
        ]
        rights = [jnp.where(row_b == low, 1.0, 0.0).astype(bf16) for low in lows]
        for key, left, right in zip(keys, lefts, rights):
            spread[key] = mm(left, right, NT)
    table = jnp.sum(spread[...], axis=0)
    g_two[4:SMALL, 0 : HEADS * DIGIT] = table[0 : SMALL - 4]
    if not count:
        outs[0][...] = g_qkv[...]
        outs[1][...] = g_two[...]
        return
    depth, ups = chan // count, g_up.shape[1] // chan
    deep = ups * depth
    first = (1 + 2 * ups) * depth
    for dest in range(count):
        at = dest * depth
        g_all[dest, 0:depth] = g_proj[at : at + depth].astype(bf16)
        for col in range(ups):
            part = g_up[at : at + depth, col * chan : (col + 1) * chan]
            g_all[dest, (1 + col) * depth : (2 + col) * depth] = part.astype(bf16)
        g_all[dest, (1 + ups) * depth : first] = g_down[dest * deep : (dest + 1) * deep].astype(bf16)
        for col in range(3):
            part = g_qkv[at : at + depth, col * chan : (col + 1) * chan]
            g_all[dest, first + col * depth : first + (col + 1) * depth] = part.astype(bf16)
        g_all[dest, first + 3 * depth : first + 3 * depth + SMALL] = g_one[...].astype(bf16)
        g_all[dest, first + 3 * depth + SMALL :] = g_two[...].astype(bf16)
    side = band_ref[0] % 2
    many = g_all.shape[1] // 2
    outs[0][...] = g_all[:, pl.ds(pl.multiple_of(side * many, many), many), :]
    outs[1][...] = g_all[:, pl.ds(pl.multiple_of((1 - side) * many, many), many), :]


def rows_body(bw, tw, out_bo, out_tg, out_halo):
    rows, cols, chan = out_bo.shape
    across = cols // WIN
    place = place_matrix(cols, SHIFT)
    twice = jnp.concatenate([place, place], axis=0)
    for row in range(rows):
        at, down = row // WIN * across, row % WIN * PADDED
        block = bw[at : at + across, down : down + PADDED, :].reshape(across * PADDED, chan).astype(bf16)
        block = mm(place, block, TN).astype(bf16)
        grad = tw[at : at + across, down : down + PADDED, :].reshape(across * PADDED, chan)
        high = grad.astype(bf16)
        low = (grad - high.astype(f32)).astype(bf16)
        grad = mm(twice, jnp.concatenate([high, low], axis=0), TN)
        if row + SHIFT < rows:
            out_bo[row + SHIFT] = block
            out_tg[row + SHIFT] = grad
        else:
            out_halo[0, row + SHIFT - rows] = block
            out_halo[1, row + SHIFT - rows] = grad.astype(bf16)
    for row in range(SHIFT):
        out_bo[row] = jnp.zeros((cols, chan), bf16)
        out_tg[row] = jnp.zeros((cols, chan), f32)


def total(refs):
    parts = [refs[source][...].astype(f32) for source in range(len(refs))]
    while len(parts) > 1:
        parts = [parts[i] + parts[i + 1] for i in range(0, len(parts), 2)]
    return parts[0]


def pair_body(mine, other, out):
    out[...] = (mine[...].astype(f32) + other[...].astype(f32)).astype(bf16)


def sum_body(pieces, out):
    out[...] = total([pieces.at[i] for i in range(pieces.shape[0])]).astype(bf16)


def final_body(bands, me_ref, band_ref, bo, tg, halo, *refs):
    both, outs, (rows_f, sems) = refs[:bands], refs[bands:-2], refs[-2:]
    (
        out_bo, out_tg, o_gain_one, o_shift_one, o_qkv, o_query, o_value, o_proj, o_bias_proj,
        o_gain_two, o_shift_two, o_up, o_bias_up, o_down, o_bias_down, o_table,
    ) = outs
    rows_f[...] = halo[1].astype(f32)
    copies = [
        pltpu.make_async_copy(halo.at[0], out_bo.at[0:SHIFT], sems.at[0]),
        pltpu.make_async_copy(rows_f, out_tg.at[0:SHIFT], sems.at[1]),
    ]
    for copy in copies:
        copy.start()
    me = me_ref[0]
    depth, chan = o_proj.shape
    ups = o_up.shape[1] // chan
    mine = total([both[step] for step in range(0, bands, 2)])
    other = total([both[step] for step in range(1, bands, 2)])
    even = band_ref[0] % 2 == 0
    summed = jnp.concatenate([jnp.where(even, mine, other), jnp.where(even, other, mine)], axis=0)
    first = (1 + 2 * ups) * depth
    o_proj[...] = summed[0:depth]
    for col in range(ups):
        o_up[:, col * chan : (col + 1) * chan] = summed[(1 + col) * depth : (2 + col) * depth]
    o_down[...] = summed[(1 + ups) * depth : first]
    for col in range(3):
        o_qkv[:, col * chan : (col + 1) * chan] = summed[first + col * depth : first + (col + 1) * depth]
    early = summed[first + 3 * depth : first + 3 * depth + SMALL]
    late = summed[first + 3 * depth + SMALL :]
    mine = jnp.concatenate([early[0:8], late[0:8]], axis=0)
    turned = pltpu.roll(mine, (chan - me * depth) % chan, 1)
    o_bias_proj[...] = turned[0:1, :depth]
    o_gain_two[...] = turned[1:2, :depth]
    o_shift_two[...] = turned[2:3, :depth]
    o_bias_down[...] = turned[3:4, :depth]
    o_gain_one[...] = turned[8:9, :depth]
    o_shift_one[...] = turned[9:10, :depth]
    o_query[...] = turned[10:11, :depth]
    o_value[...] = turned[11:12, :depth]
    at = me * depth * ups
    chosen = jnp.where(iota((8, chan), 0) == 4 + at // chan, early[0:8], 0.0)
    chosen = jnp.broadcast_to(jnp.sum(chosen, axis=0, keepdims=True), (8, chan))
    chosen = pltpu.roll(chosen, (chan - at % chan) % chan, 1)
    o_bias_up[...] = chosen[0:1, : depth * ups]
    for head in range(HEADS):
        for digit in range((TABLE + DIGIT - 1) // DIGIT):
            width = min(DIGIT, TABLE - digit * DIGIT)
            o_table[head : head + 1, digit * DIGIT : digit * DIGIT + width] = late[
                4 + digit : 5 + digit, head * DIGIT : head * DIGIT + width
            ]
    for copy in copies:
        copy.wait()


def call(body, outs, *args, scratch=(), ins=None, outs_at=None, name=None, limit=16, micros=1, aliases=None):
    at = lambda space: pl.BlockSpec(memory_space=space)
    return pl.pallas_call(
        body,
        out_shape=[jax.ShapeDtypeStruct(shape, dtype) for shape, dtype in outs],
        in_specs=[at(space) for space in (ins or [VMEM] * len(args))],
        out_specs=[at(space) for space in (outs_at or [VMEM] * len(outs))],
        scratch_shapes=[VMEM(*one) if isinstance(one, tuple) else one for one in scratch],
        input_output_aliases=aliases or {},
        compiler_params=pltpu.CompilerParams(vmem_limit_bytes=limit << 20),
        cost_estimate=pl.CostEstimate(flops=micros * 10**9, bytes_accessed=micros * 3 * 10**6, transcendentals=0),
        name=name,
    )(*args)


def shifted(value, axis, steps):
    count = lax.axis_size(axis)
    return lax.ppermute(value, axis, [(source, (source + steps) % count) for source in range(count)])


def swap(value, axis, step):
    count = lax.axis_size(axis)
    return lax.ppermute(value, axis, [(source, source ^ step) for source in range(count)])


def one_way(value, axis, parity):
    count = lax.axis_size(axis)
    return lax.ppermute(value, axis, [(source, (source - 1) % count) for source in range(parity, count, 2)])


def spread_out(value, i):
    bands, images = lax.axis_size("seq"), lax.axis_size("fsdp")
    pairs = [
        (band * images + image, band * images + (image ^ (band % 2 * (images // 2) + i)))
        for band in range(bands)
        for image in range(images)
    ]
    return lax.ppermute(value, ("seq", "fsdp"), pairs)


def on_device(
    tokens_in, first_gain, first_shift, qkv_weight, query_bias, value_bias, proj_weight, proj_bias,
    second_gain, second_shift, up_weight, up_bias, down_weight, down_bias, bias_table, table_index,
    region_ids, cotangent,
):
    images, rows, cols, chan = tokens_in.shape
    assert images == 1
    fsdp, bands = lax.axis_size("fsdp"), lax.axis_size("seq")
    wide = up_weight.shape[1]
    depth = proj_weight.shape[0]
    wins = rows // WIN * (cols // WIN)
    direct = depth % 16 == 0
    count = fsdp if direct else 0
    tok, cot = tokens_in[0], cotangent[0]
    region = region_ids.reshape(rows, 1, cols)
    vectors = (
        first_gain, first_shift, query_bias, value_bias, proj_bias, second_gain, second_shift, down_bias, up_bias,
    )
    tokw = (wins, WTOK, chan)
    flatw = (wins * WTOK, chan)
    flatu = (wins * WTOK, wide)
    ups = wide // chan
    piece_rows = (1 + 2 * ups) * depth + 3 * depth + SMALL
    wide_scores = (wins, WTOK, HEADS * QPAD)
    sems = lambda many: pltpu.SemaphoreType.DMA((many,))
    near = fsdp // 2
    me = lax.axis_index("fsdp").astype(jnp.int32).reshape(1)
    band = lax.axis_index("seq").astype(jnp.int32).reshape(1)
    if direct:
        held = [vector.reshape(1, -1) for vector in vectors] + [qkv_weight, proj_weight, up_weight, down_weight]
        piece, halo = call(
            pack_body,
            [((piece_rows, chan), bf16), ((2, SHIFT, cols, chan), bf16)],
            *held, tok, cot, name="pack", limit=58, ins=[pl.ANY] * 15,
            scratch=[(array.shape, bf16) for array in held] + [sems(15)],
        )
        fetched = [spread_out(piece, i) for i in range(near)]
    else:
        halo = jnp.stack([tok[:SHIFT], cot[:SHIFT]])
        gather = functools.partial(lax.all_gather, axis_name="fsdp", axis=0, tiled=True)
        full = [gather(vector).astype(f32).reshape(-1, chan) for vector in vectors]
        full.append(jnp.zeros((SMALL - 8 - ups, chan), f32))
        weights = [
            gather(qkv_weight), jnp.concatenate(full, axis=0), gather(proj_weight), gather(up_weight),
            gather(down_weight),
        ]
    halo_even = one_way(halo, "seq", 0)
    bm, idx = call(
        bias_body,
        [(wide_scores, f32), ((WTOK, HEADS * QPAD), f32)],
        region, bias_table.T, table_index, tok, cot,
        scratch=[((DIGIT, HEADS * DIGIT), f32), ((WTOK, HEADS * QPAD), f32), ((wins, WTOK, 128), f32)],
        name="score_bias", micros=3,
    )
    halo, bm = lax.optimization_barrier((halo, bm))
    halo_odd = one_way(halo, "seq", 1)
    if direct:
        *fetched, bm, idx = lax.optimization_barrier((*fetched, bm, idx))
        (pair,) = call(join_body, [((near, piece_rows, chan), bf16)], *fetched, name="join")
        weights = [pair, swap(pair, "seq", 1)]
    xw, cw, unit, rstd = call(prepare_body, [(tokw, f32)] * 4, tok, cot, halo_even, halo_odd, name="prepare", micros=2)
    big = dict(limit=32)
    place = [pltpu.SMEM] * 2
    nb, qx, k_b, v_b, probs, att, small, w_qkv, w_proj, w_up, w_down = call(
        functools.partial(attend_body, count),
        [
            (flatw, bf16), ((wins, HEADS * QPAD, chan), bf16), (tokw, bf16), (tokw, bf16), (wide_scores, f32),
            (tokw, f32), ((SMALL, chan), f32), ((chan, 3 * chan), bf16), ((chan, chan), bf16), ((chan, wide), bf16),
            ((wide, chan), bf16),
        ],
        me, band, unit, bm, *weights, name="attention", micros=3, ins=place + [VMEM] * (2 + len(weights)), **big,
        scratch=[((wins * WTOK, 3 * chan), f32)],
    )
    bw, dmid, datt, g_proj, g_up, g_down, g_one = call(
        mlp_body,
        [
            (tokw, f32), (tokw, f32), (tokw, f32), ((chan, chan), f32), ((chan, wide), f32), ((wide, chan), f32),
            ((SMALL, chan), f32),
        ],
        xw, cw, att, small, w_proj, w_up, w_down, name="feed_forward", micros=5, **big,
        scratch=[(flatw, bf16)] * 4 + [(flatu, bf16)] * 2 + [(flatu, f32)] * 2 + [(flatw, f32)] * 4,
    )
    if direct:
        halves = ((fsdp, (piece_rows + SMALL) // 2, chan), bf16)
        sent = [halves] * 2
    else:
        sent = [((chan, 3 * chan), f32), ((SMALL, chan), f32)]
    tw, *grads = call(
        functools.partial(back_body, count),
        [(tokw, f32)] + sent,
        band, qx, k_b, v_b, probs, datt, dmid, nb, unit, rstd, small, w_qkv, idx, g_proj, g_up, g_down, g_one,
        name="attention_back", micros=5, ins=place[:1] + [VMEM] * 16, **big,
        scratch=[
            (tokw, f32), (tokw, f32), (tokw, f32), ((wins * WTOK, 3 * chan), bf16), (flatw, f32),
            ((WTOK, HEADS * QPAD), f32), ((WTOK, DIGIT, HEADS * DIGIT), f32), ((chan, 3 * chan), f32), ((SMALL, chan), f32),
            ((max(count, 1), piece_rows + SMALL, chan), bf16),
        ],
    )
    bo, tg, last = call(
        rows_body,
        [((rows, cols, chan), bf16), ((rows, cols, chan), f32), ((2, SHIFT, cols, chan), bf16)],
        bw, tw, name="rows", micros=2,
    )
    if not direct:
        last = shifted(last, "seq", 1)
        g_proj, g_up, g_down, early, g_qkv, late = lax.psum((g_proj, g_up, g_down, g_one, *grads), "seq")
        digits = (TABLE + DIGIT - 1) // DIGIT
        table = lax.psum(late[4 : 4 + digits, : HEADS * DIGIT], "fsdp").reshape(digits, HEADS, DIGIT)
        table = table.transpose(1, 0, 2).reshape(HEADS, digits * DIGIT)[:, :TABLE]
        scatter = functools.partial(lax.psum_scatter, axis_name="fsdp", scatter_dimension=0, tiled=True)
        block_out = jnp.concatenate([last[0], bo[SHIFT:]], axis=0)
        tokens_grad = jnp.concatenate([last[1].astype(f32), tg[SHIFT:]], axis=0)
        return (
            block_out[None], tokens_grad[None], scatter(late[0]), scatter(late[1]), scatter(g_qkv),
            scatter(late[2]), scatter(late[3]), scatter(g_proj), scatter(early[0]), scatter(early[1]),
            scatter(early[2]), scatter(g_up), scatter(early[4 : 4 + ups].reshape(-1)),
            scatter(g_down), scatter(early[3]), table.T,
        )
    kept, given = grads[0], swap(grads[1], "seq", 1)
    kept, given, last = lax.optimization_barrier((kept, given, last))
    last = shifted(last, "seq", 1)
    (kept,) = call(pair_body, [halves], kept, given, name="sum_cores")
    pieces = lax.all_to_all(kept, "fsdp", 0, 0, tiled=True)
    (both,) = call(sum_body, [(halves[0][1:], bf16)], pieces, name="sum_images")
    arrived = [both] + [swap(both, "seq", step) for step in range(1, bands)]
    line = ((1, depth), f32)
    outs = call(
        functools.partial(final_body, bands),
        [
            ((rows, cols, chan), bf16), ((rows, cols, chan), f32), line, line, ((depth, 3 * chan), f32), line,
            line, ((depth, chan), f32), line, line, line, ((depth, wide), f32), ((1, depth * ups), f32),
            ((depth * ups, chan), f32), line, ((HEADS, TABLE), f32),
        ],
        me, band, bo, tg, last, *arrived, name="finish", aliases={2: 0, 3: 1},
        ins=[pltpu.SMEM] * 2 + [pl.ANY] * 2 + [VMEM] * (1 + bands), outs_at=[pl.ANY, pl.ANY] + [VMEM] * 14,
        scratch=[((SHIFT, cols, chan), f32), sems(2)],
    )
    outs = [out.reshape(-1) if out.shape[0] == 1 else out for out in outs]
    return (outs[0][None], outs[1][None], *outs[2:15], outs[15].T)


def solution(mesh):
    placed = (
        P("fsdp", "seq", None, None),
        P("fsdp"),
        P("fsdp"),
        P("fsdp", None),
        P("fsdp"),
        P("fsdp"),
        P("fsdp", None),
        P("fsdp"),
        P("fsdp"),
        P("fsdp"),
        P("fsdp", None),
        P("fsdp"),
        P("fsdp", None),
        P("fsdp"),
        P(),
        P(),
        P("fsdp", "seq", None),
        P("fsdp", "seq", None, None),
    )
    return jax.shard_map(
        on_device,
        mesh=mesh,
        in_specs=placed,
        out_specs=(
            P("fsdp", "seq", None, None),
            P("fsdp", "seq", None, None),
            P("fsdp"),
            P("fsdp"),
            P("fsdp", None),
            P("fsdp"),
            P("fsdp"),
            P("fsdp", None),
            P("fsdp"),
            P("fsdp"),
            P("fsdp"),
            P("fsdp", None),
            P("fsdp"),
            P("fsdp", None),
            P("fsdp"),
            P(),
        ),
        check_vma=False,
    )
```

```python
import functools

import jax
import jax.numpy as jnp
from jax import lax
from jax.experimental import pallas as pl
from jax.experimental.pallas import tpu as pltpu
from jax.sharding import PartitionSpec as P

HEADS = 4
WIN = 7
SHIFT = 3
TABLE = 169
PADDED = 8
WTOK = WIN * PADDED
QPAD = 64
SMALL = 16
DIGIT = 16

norm_eps = 1e-05
masked_fill = -1e30
f32 = jnp.float32
bf16 = jnp.bfloat16
NT = (((1,), (1,)), ((), ()))
TN = (((0,), (0,)), ((), ()))
VMEM = pltpu.VMEM


def mm(left, right, dims=(((1,), (0,)), ((), ()))):
    return lax.dot_general(left, right, dims, preferred_element_type=f32)


def iota(shape, axis):
    return lax.broadcasted_iota(jnp.int32, shape, axis)


def place_matrix(cols, roll):
    spots = cols // WIN * PADDED
    spot, col = iota((spots, cols), 0), iota((spots, cols), 1)
    place = spot % PADDED
    target = spot // PADDED * WIN + place + roll
    target = jnp.where(target >= cols, target - cols, target)
    return jnp.where((place < WIN) & (col == target), 1.0, 0.0).astype(bf16)


def head_mask(shape, lane_axis=1):
    chans = shape[-1] // HEADS
    return jnp.where(iota(shape, len(shape) - 1) // chans == iota(shape, 0), 1.0, 0.0)


def expand_heads(tokens, hmask):
    zeros = jnp.zeros((QPAD - WTOK, tokens.shape[1]), f32)
    full = jnp.concatenate([tokens, zeros], axis=0)
    return (full[None] * hmask).reshape(HEADS * QPAD, tokens.shape[1]).astype(bf16)


def merge_heads(stacked, hmask):
    parts = stacked.reshape(HEADS, QPAD, stacked.shape[1]) * hmask
    return ((parts[0] + parts[1]) + (parts[2] + parts[3]))[:WTOK]


def lane_mean(values):
    return jnp.mean(values, axis=-1, keepdims=True)


def pack_body(*refs):
    given, (out, out_h), scratch, sems = refs[:15], refs[15:17], refs[17:-1], refs[-1]
    sources = list(given[:13]) + [ref.at[0:SHIFT] for ref in given[13:]]
    targets = list(scratch) + [out_h.at[0], out_h.at[1]]
    copies = [
        pltpu.make_async_copy(source, target, sems.at[i])
        for i, (source, target) in enumerate(zip(sources, targets))
    ]
    for copy in copies:
        copy.start()
    for copy in copies:
        copy.wait()
    vectors, (qkv, proj, up, down) = scratch[:9], scratch[9:]
    depth, chan = proj.shape
    blocks, ups = qkv.shape[1] // chan, up.shape[1] // chan
    small = jnp.concatenate(
        [jnp.pad(vector[...].astype(f32), ((0, 0), (0, chan - vector.shape[1]))) for vector in vectors]
        + [jnp.zeros((SMALL - 9, chan), f32)],
        axis=0,
    ).astype(bf16)
    parts = [proj[...]]
    parts += [up[:, col * chan : (col + 1) * chan] for col in range(ups)]
    parts += [down[...]]
    parts += [qkv[:, col * chan : (col + 1) * chan] for col in range(blocks)]
    parts += [small]
    at = 0
    for part in parts:
        out[at : at + part.shape[0]] = part
        at += part.shape[0]


def join_body(*refs):
    for i, piece in enumerate(refs[:-1]):
        refs[-1][i] = piece[...]


def bias_body(region, table, index, tok, cot, out_bm, out_idx, tab, rel, ident):
    rows, _, cols = region.shape
    tokens = index.shape[0]
    wide = HEADS * QPAD
    token_a, spot_a = iota((tokens, WTOK), 0), iota((tokens, WTOK), 1)
    keys_at = jnp.where(token_a // WIN * PADDED + token_a % WIN == spot_a, 1.0, 0.0).astype(bf16)
    token_b, lane_b = iota((tokens, wide), 0), iota((tokens, wide), 1)
    queries_at = jnp.where(token_b // WIN * PADDED + token_b % WIN == lane_b % QPAD, 1.0, 0.0).astype(bf16)
    half = mm(index[...].astype(f32).astype(bf16), keys_at).astype(bf16)
    out_idx[...] = mm(half, queries_at, TN)
    tab[...] = jnp.zeros_like(tab)
    for head in range(HEADS):
        for digit in range((TABLE + DIGIT - 1) // DIGIT):
            width = min(DIGIT, TABLE - digit * DIGIT)
            tab[digit : digit + 1, head * DIGIT : head * DIGIT + width] = table[
                head : head + 1, digit * DIGIT : digit * DIGIT + width
            ]
    entries = tab[...]
    first = entries.astype(bf16).astype(f32)
    second = (entries - first).astype(bf16).astype(f32)
    terms = jnp.concatenate([first, second, entries - first - second], axis=0).astype(bf16)
    digit_a = (iota((3 * DIGIT, wide), 0) % DIGIT).astype(f32)
    row_b = iota((HEADS * DIGIT, wide), 0).astype(f32)
    head_of = (iota((1, wide), 1) // QPAD * DIGIT).astype(f32)

    for start in range(0, WTOK, 8):
        keys = range(start, start + 8)
        lines = [out_idx[key : key + 1, :] for key in keys]
        highs = [jnp.floor(entry * (1.0 / DIGIT)) for entry in lines]
        lows = [entry - high * DIGIT + head_of for entry, high in zip(lines, highs)]
        found = [mm(terms, jnp.where(row_b == low, 1.0, 0.0).astype(bf16)) for low in lows]
        found = [jnp.where(digit_a == high, one, 0.0) for high, one in zip(highs, found)]
        for key, one in zip(keys, found):
            rel[key : key + 1, :] = jnp.sum(one, axis=0, keepdims=True)
    place = place_matrix(cols, 0)
    across = cols // WIN
    for row in range(rows):
        classes = jnp.where(iota((128, cols), 0) == region[row], 1.0, 0.0).astype(bf16)
        at = row // WIN * across
        down = row % WIN * PADDED
        ident[at : at + across, down : down + PADDED, :] = mm(place, classes, NT).reshape(
            across, PADDED, 128
        )
    bias = rel[...]
    for win in range(rows // WIN * across):
        here = ident[win]
        other = jnp.concatenate([here, jnp.zeros((QPAD - WTOK, 128), f32)], axis=0)
        other = jnp.broadcast_to(other[None], (HEADS, QPAD, 128)).reshape(wide, 128).astype(bf16)
        out_bm[win] = jnp.where(mm(here.astype(bf16), other, NT) > 0.5, bias, masked_fill)


def assemble_vectors(pieces, sources, count, offset, out_small):
    chan = pieces[0].shape[1]
    per, per_up = chan // count, 4 * chan // count
    row = iota((8, chan), 0)
    vecs, ups = jnp.zeros((8, chan), f32), jnp.zeros((8, chan), f32)
    for piece, source in zip(pieces, sources):
        block = piece[offset : offset + SMALL].astype(f32)
        vecs += pltpu.roll(block[0:8], source * per, 1)
        at = source * per_up
        line = pltpu.roll(jnp.broadcast_to(block[8:9], (8, chan)), at % chan, 1)
        ups += jnp.where(row == at // chan, line, 0.0)
    out_small[0:8] = vecs
    out_small[8:16] = ups


def gelu_parts(hidden):
    base = 1.0 + (0.3275911 * 0.5**0.5) * jnp.abs(hidden)
    term = pl.reciprocal(base, approx=True)
    term = term * (2.0 - base * term)
    bell = jnp.exp(-0.5 * (hidden * hidden))
    poly = (0.5 * 1.061405429) * term - (0.5 * 1.453152027)
    poly = poly * term + (0.5 * 1.421413741)
    poly = poly * term - (0.5 * 0.284496736)
    poly = poly * term + (0.5 * 0.254829592)
    tail = poly * term * bell
    cdf = jnp.where(hidden >= 0, 1.0 - tail, tail)
    return cdf, cdf + hidden * (bell * 0.3989422804014327)


def layer_stats(values):
    centred = values - lane_mean(values)
    rstd = lax.rsqrt(lane_mean(centred * centred) + norm_eps)
    return centred * rstd, rstd


def layer_back(d_unit, unit, rstd):
    return rstd * (d_unit - lane_mean(d_unit) - unit * lane_mean(d_unit * unit))


def my_images(me_ref, band_ref, count):
    near = count // 2
    return [me_ref[0] ^ ((band_ref[0] % 2 ^ core) * near + i) for core in range(2) for i in range(near)]


def prepare_body(tok, cot, halo, out_xw, out_cw, out_unit, out_rstd):
    rows, cols, chan = tok.shape
    across = cols // WIN
    place = place_matrix(cols, SHIFT)
    for which, source, target in ((0, tok, out_xw), (1, cot, out_cw)):
        for row in range(rows):
            line = source[row + SHIFT] if row + SHIFT < rows else halo[which, row + SHIFT - rows]
            at, down = row // WIN * across, row % WIN * PADDED
            target[at : at + across, down : down + PADDED, :] = mm(place, line).reshape(across, PADDED, chan)
    step_wins = 4
    for at in range(0, out_xw.shape[0], step_wins):
        span = slice(at, at + step_wins)
        unit, rstd = layer_stats(out_xw[span])
        out_unit[span] = unit
        out_rstd[span] = jnp.broadcast_to(rstd, unit.shape)


def attend_body(count, me_ref, band_ref, unit, bm, *refs):
    inputs = 2 if count else 5
    weights, outs = refs[:inputs], refs[inputs:]
    out_nb, out_qx, out_k, out_v, out_p, out_att, out_small, w_qkv, w_proj, w_up, w_down, mixed = outs
    wins, _, chan = unit.shape
    if count:
        sources = my_images(me_ref, band_ref, count)
        pieces = [weights[core].at[i] for core in range(2) for i in range(count // 2)]
        depth, ups = chan // count, w_up.shape[1] // chan
        deep = ups * depth
        first = (1 + 2 * ups) * depth
        for piece, source in zip(pieces, sources):
            here = pl.ds(pl.multiple_of(source * depth, depth), depth)
            for col in range(3):
                w_qkv[here, col * chan : (col + 1) * chan] = piece[first + col * depth : first + (col + 1) * depth]
            w_proj[here] = piece[0:depth]
            for col in range(ups):
                w_up[here, col * chan : (col + 1) * chan] = piece[(1 + col) * depth : (2 + col) * depth]
            w_down[pl.ds(pl.multiple_of(source * deep, deep), deep)] = piece[(1 + ups) * depth : first]
        assemble_vectors(pieces, sources, count, first + 3 * depth, out_small)
    else:
        for source, target in zip(weights, (w_qkv, out_small, w_proj, w_up, w_down)):
            target[...] = source[...]
    small = out_small[...]
    gain, shift, bias_q, bias_v = small[0:1], small[1:2], small[2:3], small[3:4]
    hmask = head_mask((HEADS, QPAD, chan))
    scale = (chan // HEADS) ** -0.5
    step_wins = 4
    weight = w_qkv[...]
    for at in range(0, wins, step_wins):
        normed = (unit[at : at + step_wins].reshape(step_wins * WTOK, chan) * gain + shift).astype(bf16)
        out_nb[at * WTOK : (at + step_wins) * WTOK] = normed
    mixed[...] = mm(out_nb[...], weight)
    for at in range(0, wins, step_wins):
        three = mixed[at * WTOK : (at + step_wins) * WTOK]
        query = three[:, :chan] + bias_q
        key = three[:, chan : 2 * chan]
        value = three[:, 2 * chan :] + bias_v
        for win in range(step_wins):
            span = slice(win * WTOK, (win + 1) * WTOK)
            out_qx[at + win] = expand_heads(query[span].astype(bf16).astype(f32), hmask)
            out_k[at + win] = key[span].astype(bf16)
            out_v[at + win] = value[span].astype(bf16)
    for at in range(0, wins, step_wins):
        group = range(at, at + step_wins)
        scores = [mm(out_k[win], out_qx[win], NT) * scale + bm[win] for win in group]
        expos = [jnp.exp(one - jnp.max(one, axis=0, keepdims=True)) for one in scores]
        probs = [one * (1.0 / jnp.sum(one, axis=0, keepdims=True)) for one in expos]
        for win, one in zip(group, probs):
            out_p[win] = one
        parts = [mm(one.astype(bf16), out_v[win], TN) for win, one in zip(group, probs)]
        for win, one in zip(group, parts):
            out_att[win] = merge_heads(one, hmask)


def mlp_body(xw, cw, att, small_ref, w_proj, w_up, w_down, *refs):
    out_bw, out_dmid, out_datt, g_proj, g_up, g_down, g_one, *scratch = refs
    att_b, n2_b, dbr_b, dy_b, act_b, dh_b, hid, dact, mid, unit2, rstd2, back = scratch
    wins, _, chan = xw.shape
    wide = w_up.shape[1]
    ups = wide // chan
    small = small_ref[...]
    bias_p, gain, shift, bias_d = small[4:5], small[5:6], small[6:7], small[7:8]
    bias_u = jnp.concatenate([small[8 + i : 9 + i] for i in range(ups)], axis=1)
    weight_p, weight_u, weight_d = w_proj[...], w_up[...], w_down[...]
    half = wins // 2
    few = 4
    full, split = (few * WTOK, chan), (few, WTOK, chan)
    sums = [jnp.zeros((1, chan), f32) for _ in range(4)]
    sum_up = jnp.zeros((8, wide), f32)

    def rows_of(at, many):
        return slice(at, at + many), slice(at * WTOK, (at + many) * WTOK)

    def enter(at):
        span, flat = rows_of(at, half)
        dy_b[flat] = cw[span].reshape(half * WTOK, chan).astype(bf16)
        dact[flat] = mm(dy_b[flat], weight_d, NT)
        att_b[flat] = att[span].reshape(half * WTOK, chan).astype(bf16)
        mid[flat] = mm(att_b[flat], weight_p)
        for some in range(at, at + half, few):
            here, line = rows_of(some, few)
            middle = xw[here].reshape(full) + (mid[line] + bias_p)
            mid[line] = middle
            unit, rstd = layer_stats(middle)
            unit2[line] = unit
            rstd2[line] = jnp.broadcast_to(rstd, full)
            n2_b[line] = (unit * gain + shift).astype(bf16)
        hid[flat] = mm(n2_b[flat], weight_u)

    def tiles(at, have):
        for row in range(at * WTOK, (at + half) * WTOK, 16):
            line = slice(row, row + 16)
            hidden = hid[line] + bias_u
            cdf, slope = gelu_parts(hidden)
            act_b[line] = (hidden * cdf).astype(bf16)
            d_hidden = dact[line] * slope
            dh_b[line] = d_hidden.astype(bf16)
            have = have + (d_hidden[0:8] + d_hidden[8:16])
        return have

    def leave(at, have):
        span, flat = rows_of(at, half)
        out_bw[span] = (mid[flat] + mm(act_b[flat], weight_d) + bias_d).reshape(half, WTOK, chan)
        back[flat] = mm(dh_b[flat], weight_u, NT)
        for some in range(at, at + half, few):
            here, line = rows_of(some, few)
            d_normed = back[line]
            unit = unit2[line]
            grad = cw[here].reshape(full)
            d_middle = grad + layer_back(d_normed * gain, unit, rstd2[line])
            out_dmid[here] = d_middle.reshape(split)
            dbr_b[line] = d_middle.astype(bf16)
            terms = (d_middle, d_normed * unit, d_normed, grad)
            have = [one + jnp.sum(term, axis=0, keepdims=True) for one, term in zip(have, terms)]
        out_datt[span] = mm(dbr_b[flat], weight_p, NT).reshape(half, WTOK, chan)
        return have

    enter(0)
    enter(half)
    sum_up = tiles(0, sum_up)
    sums = leave(0, sums)
    sum_up = tiles(half, sum_up)
    sums = leave(half, sums)
    g_one[...] = jnp.zeros_like(g_one)
    for row in range(4):
        g_one[row : row + 1] = sums[row]
    total_up = jnp.sum(sum_up, axis=0, keepdims=True)
    for col in range(ups):
        g_one[4 + col : 5 + col] = total_up[:, col * chan : (col + 1) * chan]
    g_down[...] = mm(dy_b[...], act_b[...], TN).T
    g_up[...] = mm(n2_b[...], dh_b[...], TN)
    g_proj[...] = mm(att_b[...], dbr_b[...], TN)


def back_body(count, band_ref, qx, k_ref, v_ref, p_ref, datt, dmid, nb, unit_ref, rstd_ref, *refs):
    small_ref, w_qkv, idx, g_proj, g_up, g_down, g_one, out_tw, *refs = refs
    outs, scratch = refs[:2], refs[2:]
    dq, dk, dv, mixed, d_one, drel, spread, g_qkv, g_two, g_all = scratch
    wins, _, chan = dmid.shape
    hmask = head_mask((HEADS, QPAD, chan))
    scale = (chan // HEADS) ** -0.5
    step_wins = 4
    drel[...] = jnp.zeros_like(drel)
    for at in range(0, wins, step_wins):
        group = range(at, at + step_wins)
        grads = [expand_heads(datt[win].astype(bf16).astype(f32), hmask) for win in group]
        d_probs = [mm(v_ref[win], one, NT) for win, one in zip(group, grads)]
        for win, one in zip(group, grads):
            dv[win] = mm(p_ref[win].astype(bf16), one)
        weighted = [p_ref[win] * one for win, one in zip(group, d_probs)]
        d_scores = [
            (one - p_ref[win] * jnp.sum(one, axis=0, keepdims=True)).astype(bf16) for win, one in zip(group, weighted)
        ]
        four = [one.astype(f32) for one in d_scores]
        drel[...] += (four[0] + four[1]) + (four[2] + four[3])
        for win, one in zip(group, d_scores):
            dk[win] = mm(one, qx[win]) * scale
        parts = [mm(one, k_ref[win], TN) for win, one in zip(group, d_scores)]
        for win, one in zip(group, parts):
            dq[win] = merge_heads(one, hmask) * scale
    sums = []
    for col, ref in enumerate((dq, dk, dv)):
        part = ref[...].reshape(wins * WTOK, chan).astype(bf16)
        mixed[:, col * chan : (col + 1) * chan] = part
        if col != 1:
            sums.append(jnp.sum(ref[...].reshape(wins * WTOK, chan), axis=0, keepdims=True))
    g_two[...] = jnp.zeros_like(g_two)
    g_two[2:3] = sums[0]
    g_two[3:4] = sums[1]
    g_qkv[...] = mm(nb[...], mixed[...], TN)
    weight = w_qkv[...]
    gain = small_ref[0:1]
    full = (step_wins * WTOK, chan)
    sum_gain, sum_shift = jnp.zeros((1, chan), f32), jnp.zeros((1, chan), f32)
    d_one[...] = mm(mixed[...], weight, NT)
    for at in range(0, wins, step_wins):
        span = slice(at, at + step_wins)
        d_normed = d_one[at * WTOK : (at + step_wins) * WTOK]
        unit = unit_ref[span].reshape(full)
        grad = dmid[span].reshape(full) + layer_back(d_normed * gain, unit, rstd_ref[span].reshape(full))
        out_tw[span] = grad.reshape(step_wins, WTOK, chan)
        sum_gain += jnp.sum(d_normed * unit, axis=0, keepdims=True)
        sum_shift += jnp.sum(d_normed, axis=0, keepdims=True)
    g_two[0:1] = sum_gain
    g_two[1:2] = sum_shift

    lanes = HEADS * QPAD
    row_a, row_b = iota((DIGIT, lanes), 0).astype(f32), iota((HEADS * DIGIT, lanes), 0).astype(f32)
    head_of = (iota((1, lanes), 1) // QPAD * DIGIT).astype(f32)

    for start in range(0, WTOK, 8):
        keys = range(start, start + 8)
        entries = [idx[key : key + 1, :] for key in keys]
        highs = [jnp.floor(entry * (1.0 / DIGIT)) for entry in entries]
        lows = [entry - high * DIGIT + head_of for entry, high in zip(entries, highs)]
        lefts = [
            jnp.where(row_a == high, drel[key : key + 1, :], 0.0).astype(bf16) for key, high in zip(keys, highs)
        ]
        rights = [jnp.where(row_b == low, 1.0, 0.0).astype(bf16) for low in lows]
        for key, left, right in zip(keys, lefts, rights):
            spread[key] = mm(left, right, NT)
    table = jnp.sum(spread[...], axis=0)
    g_two[4:SMALL, 0 : HEADS * DIGIT] = table[0 : SMALL - 4]
    if not count:
        outs[0][...] = g_qkv[...]
        outs[1][...] = g_two[...]
        return
    depth, ups = chan // count, g_up.shape[1] // chan
    deep = ups * depth
    first = (1 + 2 * ups) * depth
    for dest in range(count):
        at = dest * depth
        g_all[dest, 0:depth] = g_proj[at : at + depth].astype(bf16)
        for col in range(ups):
            part = g_up[at : at + depth, col * chan : (col + 1) * chan]
            g_all[dest, (1 + col) * depth : (2 + col) * depth] = part.astype(bf16)
        g_all[dest, (1 + ups) * depth : first] = g_down[dest * deep : (dest + 1) * deep].astype(bf16)
        for col in range(3):
            part = g_qkv[at : at + depth, col * chan : (col + 1) * chan]
            g_all[dest, first + col * depth : first + (col + 1) * depth] = part.astype(bf16)
        g_all[dest, first + 3 * depth : first + 3 * depth + SMALL] = g_one[...].astype(bf16)
        g_all[dest, first + 3 * depth + SMALL :] = g_two[...].astype(bf16)
    side = band_ref[0] % 2
    many = g_all.shape[1] // 2
    outs[0][...] = g_all[:, pl.ds(pl.multiple_of(side * many, many), many), :]
    outs[1][...] = g_all[:, pl.ds(pl.multiple_of((1 - side) * many, many), many), :]


def rows_body(bw, tw, out_bo, out_tg, out_halo):
    rows, cols, chan = out_bo.shape
    across = cols // WIN
    place = place_matrix(cols, SHIFT)
    twice = jnp.concatenate([place, place], axis=0)
    for row in range(rows):
        at, down = row // WIN * across, row % WIN * PADDED
        block = bw[at : at + across, down : down + PADDED, :].reshape(across * PADDED, chan).astype(bf16)
        block = mm(place, block, TN).astype(bf16)
        grad = tw[at : at + across, down : down + PADDED, :].reshape(across * PADDED, chan)
        high = grad.astype(bf16)
        low = (grad - high.astype(f32)).astype(bf16)
        grad = mm(twice, jnp.concatenate([high, low], axis=0), TN)
        if row + SHIFT < rows:
            out_bo[row + SHIFT] = block
            out_tg[row + SHIFT] = grad
        else:
            out_halo[0, row + SHIFT - rows] = block
            out_halo[1, row + SHIFT - rows] = grad.astype(bf16)
    for row in range(SHIFT):
        out_bo[row] = jnp.zeros((cols, chan), bf16)
        out_tg[row] = jnp.zeros((cols, chan), f32)


def total(refs):
    parts = [refs[source][...].astype(f32) for source in range(len(refs))]
    while len(parts) > 1:
        parts = [parts[i] + parts[i + 1] for i in range(0, len(parts), 2)]
    return parts[0]


def pair_body(mine, other, out):
    out[...] = (mine[...].astype(f32) + other[...].astype(f32)).astype(bf16)


def sum_body(pieces, out):
    out[...] = total([pieces.at[i] for i in range(pieces.shape[0])]).astype(bf16)


def final_body(bands, me_ref, band_ref, bo, tg, halo, *refs):
    both, outs, (rows_f, sems) = refs[:bands], refs[bands:-2], refs[-2:]
    (
        out_bo, out_tg, o_gain_one, o_shift_one, o_qkv, o_query, o_value, o_proj, o_bias_proj,
        o_gain_two, o_shift_two, o_up, o_bias_up, o_down, o_bias_down, o_table,
    ) = outs
    rows_f[...] = halo[1].astype(f32)
    copies = [
        pltpu.make_async_copy(halo.at[0], out_bo.at[0:SHIFT], sems.at[0]),
        pltpu.make_async_copy(rows_f, out_tg.at[0:SHIFT], sems.at[1]),
    ]
    for copy in copies:
        copy.start()
    me = me_ref[0]
    depth, chan = o_proj.shape
    ups = o_up.shape[1] // chan
    mine = total([both[step] for step in range(0, bands, 2)])
    other = total([both[step] for step in range(1, bands, 2)])
    even = band_ref[0] % 2 == 0
    summed = jnp.concatenate([jnp.where(even, mine, other), jnp.where(even, other, mine)], axis=0)
    first = (1 + 2 * ups) * depth
    o_proj[...] = summed[0:depth]
    for col in range(ups):
        o_up[:, col * chan : (col + 1) * chan] = summed[(1 + col) * depth : (2 + col) * depth]
    o_down[...] = summed[(1 + ups) * depth : first]
    for col in range(3):
        o_qkv[:, col * chan : (col + 1) * chan] = summed[first + col * depth : first + (col + 1) * depth]
    early = summed[first + 3 * depth : first + 3 * depth + SMALL]
    late = summed[first + 3 * depth + SMALL :]
    mine = jnp.concatenate([early[0:8], late[0:8]], axis=0)
    turned = pltpu.roll(mine, (chan - me * depth) % chan, 1)
    o_bias_proj[...] = turned[0:1, :depth]
    o_gain_two[...] = turned[1:2, :depth]
    o_shift_two[...] = turned[2:3, :depth]
    o_bias_down[...] = turned[3:4, :depth]
    o_gain_one[...] = turned[8:9, :depth]
    o_shift_one[...] = turned[9:10, :depth]
    o_query[...] = turned[10:11, :depth]
    o_value[...] = turned[11:12, :depth]
    at = me * depth * ups
    chosen = jnp.where(iota((8, chan), 0) == 4 + at // chan, early[0:8], 0.0)
    chosen = jnp.broadcast_to(jnp.sum(chosen, axis=0, keepdims=True), (8, chan))
    chosen = pltpu.roll(chosen, (chan - at % chan) % chan, 1)
    o_bias_up[...] = chosen[0:1, : depth * ups]
    for head in range(HEADS):
        for digit in range((TABLE + DIGIT - 1) // DIGIT):
            width = min(DIGIT, TABLE - digit * DIGIT)
            o_table[head : head + 1, digit * DIGIT : digit * DIGIT + width] = late[
                4 + digit : 5 + digit, head * DIGIT : head * DIGIT + width
            ]
    for copy in copies:
        copy.wait()


def call(body, outs, *args, scratch=(), ins=None, outs_at=None, name=None, limit=16, micros=1, aliases=None):
    at = lambda space: pl.BlockSpec(memory_space=space)
    return pl.pallas_call(
        body,
        out_shape=[jax.ShapeDtypeStruct(shape, dtype) for shape, dtype in outs],
        in_specs=[at(space) for space in (ins or [VMEM] * len(args))],
        out_specs=[at(space) for space in (outs_at or [VMEM] * len(outs))],
        scratch_shapes=[VMEM(*one) if isinstance(one, tuple) else one for one in scratch],
        input_output_aliases=aliases or {},
        compiler_params=pltpu.CompilerParams(vmem_limit_bytes=limit << 20),
        cost_estimate=pl.CostEstimate(flops=micros * 10**9, bytes_accessed=micros * 3 * 10**6, transcendentals=0),
        name=name,
    )(*args)


def shifted(value, axis, steps):
    count = lax.axis_size(axis)
    return lax.ppermute(value, axis, [(source, (source + steps) % count) for source in range(count)])


def swap(value, axis, step):
    count = lax.axis_size(axis)
    return lax.ppermute(value, axis, [(source, source ^ step) for source in range(count)])


def spread_out(value, i):
    bands, images = lax.axis_size("seq"), lax.axis_size("fsdp")
    pairs = [
        (band * images + image, band * images + (image ^ (band % 2 * (images // 2) + i)))
        for band in range(bands)
        for image in range(images)
    ]
    return lax.ppermute(value, ("seq", "fsdp"), pairs)


def on_device(
    tokens_in, first_gain, first_shift, qkv_weight, query_bias, value_bias, proj_weight, proj_bias,
    second_gain, second_shift, up_weight, up_bias, down_weight, down_bias, bias_table, table_index,
    region_ids, cotangent,
):
    images, rows, cols, chan = tokens_in.shape
    assert images == 1
    fsdp, bands = lax.axis_size("fsdp"), lax.axis_size("seq")
    wide = up_weight.shape[1]
    depth = proj_weight.shape[0]
    wins = rows // WIN * (cols // WIN)
    direct = depth % 16 == 0
    count = fsdp if direct else 0
    tok, cot = tokens_in[0], cotangent[0]
    region = region_ids.reshape(rows, 1, cols)
    vectors = (
        first_gain, first_shift, query_bias, value_bias, proj_bias, second_gain, second_shift, down_bias, up_bias,
    )
    tokw = (wins, WTOK, chan)
    flatw = (wins * WTOK, chan)
    flatu = (wins * WTOK, wide)
    ups = wide // chan
    piece_rows = (1 + 2 * ups) * depth + 3 * depth + SMALL
    wide_scores = (wins, WTOK, HEADS * QPAD)
    sems = lambda many: pltpu.SemaphoreType.DMA((many,))
    near = fsdp // 2
    me = lax.axis_index("fsdp").astype(jnp.int32).reshape(1)
    band = lax.axis_index("seq").astype(jnp.int32).reshape(1)
    if direct:
        held = [vector.reshape(1, -1) for vector in vectors] + [qkv_weight, proj_weight, up_weight, down_weight]
        piece, halo = call(
            pack_body,
            [((piece_rows, chan), bf16), ((2, SHIFT, cols, chan), bf16)],
            *held, tok, cot, name="pack", limit=58, ins=[pl.ANY] * 15,
            scratch=[(array.shape, bf16) for array in held] + [sems(15)],
        )
        fetched = [spread_out(piece, i) for i in range(near)]
    else:
        halo = jnp.stack([tok[:SHIFT], cot[:SHIFT]])
        gather = functools.partial(lax.all_gather, axis_name="fsdp", axis=0, tiled=True)
        full = [gather(vector).astype(f32).reshape(-1, chan) for vector in vectors]
        full.append(jnp.zeros((SMALL - 8 - ups, chan), f32))
        weights = [
            gather(qkv_weight), jnp.concatenate(full, axis=0), gather(proj_weight), gather(up_weight),
            gather(down_weight),
        ]
    halo = shifted(halo, "seq", -1)
    bm, idx = call(
        bias_body,
        [(wide_scores, f32), ((WTOK, HEADS * QPAD), f32)],
        region, bias_table.T, table_index, tok, cot,
        scratch=[((DIGIT, HEADS * DIGIT), f32), ((WTOK, HEADS * QPAD), f32), ((wins, WTOK, 128), f32)],
        name="score_bias", micros=3,
    )
    if direct:
        *fetched, bm, idx = lax.optimization_barrier((*fetched, bm, idx))
        (pair,) = call(join_body, [((near, piece_rows, chan), bf16)], *fetched, name="join")
        weights = [pair, swap(pair, "seq", 1)]
    xw, cw, unit, rstd = call(prepare_body, [(tokw, f32)] * 4, tok, cot, halo, name="prepare", micros=2)
    big = dict(limit=32)
    place = [pltpu.SMEM] * 2
    nb, qx, k_b, v_b, probs, att, small, w_qkv, w_proj, w_up, w_down = call(
        functools.partial(attend_body, count),
        [
            (flatw, bf16), ((wins, HEADS * QPAD, chan), bf16), (tokw, bf16), (tokw, bf16), (wide_scores, f32),
            (tokw, f32), ((SMALL, chan), f32), ((chan, 3 * chan), bf16), ((chan, chan), bf16), ((chan, wide), bf16),
            ((wide, chan), bf16),
        ],
        me, band, unit, bm, *weights, name="attention", micros=3, ins=place + [VMEM] * (2 + len(weights)), **big,
        scratch=[((wins * WTOK, 3 * chan), f32)],
    )
    bw, dmid, datt, g_proj, g_up, g_down, g_one = call(
        mlp_body,
        [
            (tokw, f32), (tokw, f32), (tokw, f32), ((chan, chan), f32), ((chan, wide), f32), ((wide, chan), f32),
            ((SMALL, chan), f32),
        ],
        xw, cw, att, small, w_proj, w_up, w_down, name="feed_forward", micros=5, **big,
        scratch=[(flatw, bf16)] * 4 + [(flatu, bf16)] * 2 + [(flatu, f32)] * 2 + [(flatw, f32)] * 4,
    )
    if direct:
        halves = ((fsdp, (piece_rows + SMALL) // 2, chan), bf16)
        sent = [halves] * 2
    else:
        sent = [((chan, 3 * chan), f32), ((SMALL, chan), f32)]
    tw, *grads = call(
        functools.partial(back_body, count),
        [(tokw, f32)] + sent,
        band, qx, k_b, v_b, probs, datt, dmid, nb, unit, rstd, small, w_qkv, idx, g_proj, g_up, g_down, g_one,
        name="attention_back", micros=5, ins=place[:1] + [VMEM] * 16, **big,
        scratch=[
            (tokw, f32), (tokw, f32), (tokw, f32), ((wins * WTOK, 3 * chan), bf16), (flatw, f32),
            ((WTOK, HEADS * QPAD), f32), ((WTOK, DIGIT, HEADS * DIGIT), f32), ((chan, 3 * chan), f32), ((SMALL, chan), f32),
            ((max(count, 1), piece_rows + SMALL, chan), bf16),
        ],
    )
    bo, tg, last = call(
        rows_body,
        [((rows, cols, chan), bf16), ((rows, cols, chan), f32), ((2, SHIFT, cols, chan), bf16)],
        bw, tw, name="rows", micros=2,
    )
    if not direct:
        last = shifted(last, "seq", 1)
        g_proj, g_up, g_down, early, g_qkv, late = lax.psum((g_proj, g_up, g_down, g_one, *grads), "seq")
        digits = (TABLE + DIGIT - 1) // DIGIT
        table = lax.psum(late[4 : 4 + digits, : HEADS * DIGIT], "fsdp").reshape(digits, HEADS, DIGIT)
        table = table.transpose(1, 0, 2).reshape(HEADS, digits * DIGIT)[:, :TABLE]
        scatter = functools.partial(lax.psum_scatter, axis_name="fsdp", scatter_dimension=0, tiled=True)
        block_out = jnp.concatenate([last[0], bo[SHIFT:]], axis=0)
        tokens_grad = jnp.concatenate([last[1].astype(f32), tg[SHIFT:]], axis=0)
        return (
            block_out[None], tokens_grad[None], scatter(late[0]), scatter(late[1]), scatter(g_qkv),
            scatter(late[2]), scatter(late[3]), scatter(g_proj), scatter(early[0]), scatter(early[1]),
            scatter(early[2]), scatter(g_up), scatter(early[4 : 4 + ups].reshape(-1)),
            scatter(g_down), scatter(early[3]), table.T,
        )
    kept, given = grads[0], swap(grads[1], "seq", 1)
    kept, given, last = lax.optimization_barrier((kept, given, last))
    last = shifted(last, "seq", 1)
    (kept,) = call(pair_body, [halves], kept, given, name="sum_cores")
    pieces = lax.all_to_all(kept, "fsdp", 0, 0, tiled=True)
    (both,) = call(sum_body, [(halves[0][1:], bf16)], pieces, name="sum_images")
    arrived = [both] + [swap(both, "seq", step) for step in range(1, bands)]
    line = ((1, depth), f32)
    outs = call(
        functools.partial(final_body, bands),
        [
            ((rows, cols, chan), bf16), ((rows, cols, chan), f32), line, line, ((depth, 3 * chan), f32), line,
            line, ((depth, chan), f32), line, line, line, ((depth, wide), f32), ((1, depth * ups), f32),
            ((depth * ups, chan), f32), line, ((HEADS, TABLE), f32),
        ],
        me, band, bo, tg, last, *arrived, name="finish", aliases={2: 0, 3: 1},
        ins=[pltpu.SMEM] * 2 + [pl.ANY] * 2 + [VMEM] * (1 + bands), outs_at=[pl.ANY, pl.ANY] + [VMEM] * 14,
        scratch=[((SHIFT, cols, chan), f32), sems(2)],
    )
    outs = [out.reshape(-1) if out.shape[0] == 1 else out for out in outs]
    return (outs[0][None], outs[1][None], *outs[2:15], outs[15].T)


def solution(mesh):
    placed = (
        P("fsdp", "seq", None, None),
        P("fsdp"),
        P("fsdp"),
        P("fsdp", None),
        P("fsdp"),
        P("fsdp"),
        P("fsdp", None),
        P("fsdp"),
        P("fsdp"),
        P("fsdp"),
        P("fsdp", None),
        P("fsdp"),
        P("fsdp", None),
        P("fsdp"),
        P(),
        P(),
        P("fsdp", "seq", None),
        P("fsdp", "seq", None, None),
    )
    return jax.shard_map(
        on_device,
        mesh=mesh,
        in_specs=placed,
        out_specs=(
            P("fsdp", "seq", None, None),
            P("fsdp", "seq", None, None),
            P("fsdp"),
            P("fsdp"),
            P("fsdp", None),
            P("fsdp"),
            P("fsdp"),
            P("fsdp", None),
            P("fsdp"),
            P("fsdp"),
            P("fsdp"),
            P("fsdp", None),
            P("fsdp"),
            P("fsdp", None),
            P("fsdp"),
            P(),
        ),
        check_vma=False,
    )
```

```python
import functools

import jax
import jax.numpy as jnp
from jax import lax
from jax.experimental import pallas as pl
from jax.experimental.pallas import tpu as pltpu
from jax.sharding import PartitionSpec as P

HEADS = 4
WIN = 7
SHIFT = 3
TABLE = 169
PADDED = 8
WTOK = WIN * PADDED
QPAD = 64
SMALL = 16
DIGIT = 16

norm_eps = 1e-05
masked_fill = -1e30
f32 = jnp.float32
bf16 = jnp.bfloat16
NT = (((1,), (1,)), ((), ()))
TN = (((0,), (0,)), ((), ()))
VMEM = pltpu.VMEM


def mm(left, right, dims=(((1,), (0,)), ((), ()))):
    return lax.dot_general(left, right, dims, preferred_element_type=f32)


def iota(shape, axis):
    return lax.broadcasted_iota(jnp.int32, shape, axis)


def place_matrix(cols, roll):
    spots = cols // WIN * PADDED
    spot, col = iota((spots, cols), 0), iota((spots, cols), 1)
    place = spot % PADDED
    target = spot // PADDED * WIN + place + roll
    target = jnp.where(target >= cols, target - cols, target)
    return jnp.where((place < WIN) & (col == target), 1.0, 0.0).astype(bf16)


def head_mask(shape, lane_axis=1):
    chans = shape[-1] // HEADS
    return jnp.where(iota(shape, len(shape) - 1) // chans == iota(shape, 0), 1.0, 0.0)


def expand_heads(tokens, hmask):
    zeros = jnp.zeros((QPAD - WTOK, tokens.shape[1]), f32)
    full = jnp.concatenate([tokens, zeros], axis=0)
    return (full[None] * hmask).reshape(HEADS * QPAD, tokens.shape[1]).astype(bf16)


def merge_heads(stacked, hmask):
    parts = stacked.reshape(HEADS, QPAD, stacked.shape[1]) * hmask
    return ((parts[0] + parts[1]) + (parts[2] + parts[3]))[:WTOK]


def lane_mean(values):
    return jnp.mean(values, axis=-1, keepdims=True)


def pack_body(*refs):
    given, (out, out_h), scratch, sems = refs[:15], refs[15:17], refs[17:-1], refs[-1]
    sources = list(given[:13]) + [ref.at[0:SHIFT] for ref in given[13:]]
    targets = list(scratch) + [out_h.at[0], out_h.at[1]]
    copies = [
        pltpu.make_async_copy(source, target, sems.at[i])
        for i, (source, target) in enumerate(zip(sources, targets))
    ]
    for copy in copies:
        copy.start()
    for copy in copies:
        copy.wait()
    vectors, (qkv, proj, up, down) = scratch[:9], scratch[9:]
    depth, chan = proj.shape
    blocks, ups = qkv.shape[1] // chan, up.shape[1] // chan
    small = jnp.concatenate(
        [jnp.pad(vector[...].astype(f32), ((0, 0), (0, chan - vector.shape[1]))) for vector in vectors]
        + [jnp.zeros((SMALL - 9, chan), f32)],
        axis=0,
    ).astype(bf16)
    parts = [proj[...]]
    parts += [up[:, col * chan : (col + 1) * chan] for col in range(ups)]
    parts += [down[...]]
    parts += [qkv[:, col * chan : (col + 1) * chan] for col in range(blocks)]
    parts += [small]
    at = 0
    for part in parts:
        out[at : at + part.shape[0]] = part
        at += part.shape[0]


def join_body(band_ref, own, first, *refs):
    even = band_ref[0] % 2 == 0
    refs[-1][0] = jnp.where(even, own[...].astype(f32), first[...].astype(f32)).astype(bf16)
    for i, piece in enumerate(refs[:-1]):
        refs[-1][i + 1] = piece[...]


def bias_body(region, table, index, tok, cot, out_bm, out_idx, tab, rel, ident):
    rows, _, cols = region.shape
    tokens = index.shape[0]
    wide = HEADS * QPAD
    token_a, spot_a = iota((tokens, WTOK), 0), iota((tokens, WTOK), 1)
    keys_at = jnp.where(token_a // WIN * PADDED + token_a % WIN == spot_a, 1.0, 0.0).astype(bf16)
    token_b, lane_b = iota((tokens, wide), 0), iota((tokens, wide), 1)
    queries_at = jnp.where(token_b // WIN * PADDED + token_b % WIN == lane_b % QPAD, 1.0, 0.0).astype(bf16)
    half = mm(index[...].astype(f32).astype(bf16), keys_at).astype(bf16)
    out_idx[...] = mm(half, queries_at, TN)
    tab[...] = jnp.zeros_like(tab)
    for head in range(HEADS):
        for digit in range((TABLE + DIGIT - 1) // DIGIT):
            width = min(DIGIT, TABLE - digit * DIGIT)
            tab[digit : digit + 1, head * DIGIT : head * DIGIT + width] = table[
                head : head + 1, digit * DIGIT : digit * DIGIT + width
            ]
    entries = tab[...]
    first = entries.astype(bf16).astype(f32)
    second = (entries - first).astype(bf16).astype(f32)
    terms = jnp.concatenate([first, second, entries - first - second], axis=0).astype(bf16)
    digit_a = (iota((3 * DIGIT, wide), 0) % DIGIT).astype(f32)
    row_b = iota((HEADS * DIGIT, wide), 0).astype(f32)
    head_of = (iota((1, wide), 1) // QPAD * DIGIT).astype(f32)

    for start in range(0, WTOK, 8):
        keys = range(start, start + 8)
        lines = [out_idx[key : key + 1, :] for key in keys]
        highs = [jnp.floor(entry * (1.0 / DIGIT)) for entry in lines]
        lows = [entry - high * DIGIT + head_of for entry, high in zip(lines, highs)]
        found = [mm(terms, jnp.where(row_b == low, 1.0, 0.0).astype(bf16)) for low in lows]
        found = [jnp.where(digit_a == high, one, 0.0) for high, one in zip(highs, found)]
        for key, one in zip(keys, found):
            rel[key : key + 1, :] = jnp.sum(one, axis=0, keepdims=True)
    place = place_matrix(cols, 0)
    across = cols // WIN
    for row in range(rows):
        classes = jnp.where(iota((128, cols), 0) == region[row], 1.0, 0.0).astype(bf16)
        at = row // WIN * across
        down = row % WIN * PADDED
        ident[at : at + across, down : down + PADDED, :] = mm(place, classes, NT).reshape(
            across, PADDED, 128
        )
    bias = rel[...]
    for win in range(rows // WIN * across):
        here = ident[win]
        other = jnp.concatenate([here, jnp.zeros((QPAD - WTOK, 128), f32)], axis=0)
        other = jnp.broadcast_to(other[None], (HEADS, QPAD, 128)).reshape(wide, 128).astype(bf16)
        out_bm[win] = jnp.where(mm(here.astype(bf16), other, NT) > 0.5, bias, masked_fill)


def assemble_vectors(pieces, sources, count, offset, out_small):
    chan = pieces[0].shape[1]
    per, per_up = chan // count, 4 * chan // count
    row = iota((8, chan), 0)
    vecs, ups = jnp.zeros((8, chan), f32), jnp.zeros((8, chan), f32)
    for piece, source in zip(pieces, sources):
        block = piece[offset : offset + SMALL].astype(f32)
        vecs += pltpu.roll(block[0:8], source * per, 1)
        at = source * per_up
        line = pltpu.roll(jnp.broadcast_to(block[8:9], (8, chan)), at % chan, 1)
        ups += jnp.where(row == at // chan, line, 0.0)
    out_small[0:8] = vecs
    out_small[8:16] = ups


def gelu_parts(hidden):
    base = 1.0 + (0.3275911 * 0.5**0.5) * jnp.abs(hidden)
    term = pl.reciprocal(base, approx=True)
    term = term * (2.0 - base * term)
    bell = jnp.exp(-0.5 * (hidden * hidden))
    poly = (0.5 * 1.061405429) * term - (0.5 * 1.453152027)
    poly = poly * term + (0.5 * 1.421413741)
    poly = poly * term - (0.5 * 0.284496736)
    poly = poly * term + (0.5 * 0.254829592)
    tail = poly * term * bell
    cdf = jnp.where(hidden >= 0, 1.0 - tail, tail)
    return cdf, cdf + hidden * (bell * 0.3989422804014327)


def layer_stats(values):
    centred = values - lane_mean(values)
    rstd = lax.rsqrt(lane_mean(centred * centred) + norm_eps)
    return centred * rstd, rstd


def layer_back(d_unit, unit, rstd):
    return rstd * (d_unit - lane_mean(d_unit) - unit * lane_mean(d_unit * unit))


def my_images(me_ref, band_ref, count):
    near = count // 2
    return [me_ref[0] ^ ((band_ref[0] % 2 ^ core) * near + i) for core in range(2) for i in range(near)]


def prepare_body(tok, cot, halo, out_xw, out_cw, out_unit, out_rstd):
    rows, cols, chan = tok.shape
    across = cols // WIN
    place = place_matrix(cols, SHIFT)
    for which, source, target in ((0, tok, out_xw), (1, cot, out_cw)):
        for row in range(rows):
            line = source[row + SHIFT] if row + SHIFT < rows else halo[which, row + SHIFT - rows]
            at, down = row // WIN * across, row % WIN * PADDED
            target[at : at + across, down : down + PADDED, :] = mm(place, line).reshape(across, PADDED, chan)
    step_wins = 4
    for at in range(0, out_xw.shape[0], step_wins):
        span = slice(at, at + step_wins)
        unit, rstd = layer_stats(out_xw[span])
        out_unit[span] = unit
        out_rstd[span] = jnp.broadcast_to(rstd, unit.shape)


def attend_body(count, me_ref, band_ref, unit, bm, *refs):
    inputs = 2 if count else 5
    weights, outs = refs[:inputs], refs[inputs:]
    out_nb, out_qx, out_k, out_v, out_p, out_att, out_small, w_qkv, w_proj, w_up, w_down, mixed = outs
    wins, _, chan = unit.shape
    if count:
        sources = my_images(me_ref, band_ref, count)
        pieces = [weights[core].at[i] for core in range(2) for i in range(count // 2)]
        depth, ups = chan // count, w_up.shape[1] // chan
        deep = ups * depth
        first = (1 + 2 * ups) * depth
        for piece, source in zip(pieces, sources):
            here = pl.ds(pl.multiple_of(source * depth, depth), depth)
            for col in range(3):
                w_qkv[here, col * chan : (col + 1) * chan] = piece[first + col * depth : first + (col + 1) * depth]
            w_proj[here] = piece[0:depth]
            for col in range(ups):
                w_up[here, col * chan : (col + 1) * chan] = piece[(1 + col) * depth : (2 + col) * depth]
            w_down[pl.ds(pl.multiple_of(source * deep, deep), deep)] = piece[(1 + ups) * depth : first]
        assemble_vectors(pieces, sources, count, first + 3 * depth, out_small)
    else:
        for source, target in zip(weights, (w_qkv, out_small, w_proj, w_up, w_down)):
            target[...] = source[...]
    small = out_small[...]
    gain, shift, bias_q, bias_v = small[0:1], small[1:2], small[2:3], small[3:4]
    hmask = head_mask((HEADS, QPAD, chan))
    scale = (chan // HEADS) ** -0.5
    step_wins = 4
    weight = w_qkv[...]
    for at in range(0, wins, step_wins):
        normed = (unit[at : at + step_wins].reshape(step_wins * WTOK, chan) * gain + shift).astype(bf16)
        out_nb[at * WTOK : (at + step_wins) * WTOK] = normed
    mixed[...] = mm(out_nb[...], weight)
    for at in range(0, wins, step_wins):
        three = mixed[at * WTOK : (at + step_wins) * WTOK]
        query = three[:, :chan] + bias_q
        key = three[:, chan : 2 * chan]
        value = three[:, 2 * chan :] + bias_v
        for win in range(step_wins):
            span = slice(win * WTOK, (win + 1) * WTOK)
            out_qx[at + win] = expand_heads(query[span].astype(bf16).astype(f32), hmask)
            out_k[at + win] = key[span].astype(bf16)
            out_v[at + win] = value[span].astype(bf16)
    for at in range(0, wins, step_wins):
        group = range(at, at + step_wins)
        scores = [mm(out_k[win], out_qx[win], NT) * scale + bm[win] for win in group]
        expos = [jnp.exp(one - jnp.max(one, axis=0, keepdims=True)) for one in scores]
        probs = [one * (1.0 / jnp.sum(one, axis=0, keepdims=True)) for one in expos]
        for win, one in zip(group, probs):
            out_p[win] = one
        parts = [mm(one.astype(bf16), out_v[win], TN) for win, one in zip(group, probs)]
        for win, one in zip(group, parts):
            out_att[win] = merge_heads(one, hmask)


def mlp_body(xw, cw, att, small_ref, w_proj, w_up, w_down, *refs):
    out_bw, out_dmid, out_datt, g_proj, g_up, g_down, g_one, *scratch = refs
    att_b, n2_b, dbr_b, dy_b, act_b, dh_b, hid, dact, mid, unit2, rstd2, back = scratch
    wins, _, chan = xw.shape
    wide = w_up.shape[1]
    ups = wide // chan
    small = small_ref[...]
    bias_p, gain, shift, bias_d = small[4:5], small[5:6], small[6:7], small[7:8]
    bias_u = jnp.concatenate([small[8 + i : 9 + i] for i in range(ups)], axis=1)
    weight_p, weight_u, weight_d = w_proj[...], w_up[...], w_down[...]
    half = wins // 2
    few = 4
    full, split = (few * WTOK, chan), (few, WTOK, chan)
    sums = [jnp.zeros((1, chan), f32) for _ in range(4)]
    sum_up = jnp.zeros((8, wide), f32)

    def rows_of(at, many):
        return slice(at, at + many), slice(at * WTOK, (at + many) * WTOK)

    def enter(at):
        span, flat = rows_of(at, half)
        dy_b[flat] = cw[span].reshape(half * WTOK, chan).astype(bf16)
        dact[flat] = mm(dy_b[flat], weight_d, NT)
        att_b[flat] = att[span].reshape(half * WTOK, chan).astype(bf16)
        mid[flat] = mm(att_b[flat], weight_p)
        for some in range(at, at + half, few):
            here, line = rows_of(some, few)
            middle = xw[here].reshape(full) + (mid[line] + bias_p)
            mid[line] = middle
            unit, rstd = layer_stats(middle)
            unit2[line] = unit
            rstd2[line] = jnp.broadcast_to(rstd, full)
            n2_b[line] = (unit * gain + shift).astype(bf16)
        hid[flat] = mm(n2_b[flat], weight_u)

    def tiles(at, have):
        for row in range(at * WTOK, (at + half) * WTOK, 16):
            line = slice(row, row + 16)
            hidden = hid[line] + bias_u
            cdf, slope = gelu_parts(hidden)
            act_b[line] = (hidden * cdf).astype(bf16)
            d_hidden = dact[line] * slope
            dh_b[line] = d_hidden.astype(bf16)
            have = have + (d_hidden[0:8] + d_hidden[8:16])
        return have

    def leave(at, have):
        span, flat = rows_of(at, half)
        out_bw[span] = (mid[flat] + mm(act_b[flat], weight_d) + bias_d).reshape(half, WTOK, chan)
        back[flat] = mm(dh_b[flat], weight_u, NT)
        for some in range(at, at + half, few):
            here, line = rows_of(some, few)
            d_normed = back[line]
            unit = unit2[line]
            grad = cw[here].reshape(full)
            d_middle = grad + layer_back(d_normed * gain, unit, rstd2[line])
            out_dmid[here] = d_middle.reshape(split)
            dbr_b[line] = d_middle.astype(bf16)
            terms = (d_middle, d_normed * unit, d_normed, grad)
            have = [one + jnp.sum(term, axis=0, keepdims=True) for one, term in zip(have, terms)]
        out_datt[span] = mm(dbr_b[flat], weight_p, NT).reshape(half, WTOK, chan)
        return have

    enter(0)
    enter(half)
    sum_up = tiles(0, sum_up)
    sums = leave(0, sums)
    sum_up = tiles(half, sum_up)
    sums = leave(half, sums)
    g_one[...] = jnp.zeros_like(g_one)
    for row in range(4):
        g_one[row : row + 1] = sums[row]
    total_up = jnp.sum(sum_up, axis=0, keepdims=True)
    for col in range(ups):
        g_one[4 + col : 5 + col] = total_up[:, col * chan : (col + 1) * chan]
    g_down[...] = mm(dy_b[...], act_b[...], TN).T
    g_up[...] = mm(n2_b[...], dh_b[...], TN)
    g_proj[...] = mm(att_b[...], dbr_b[...], TN)


def back_body(count, band_ref, qx, k_ref, v_ref, p_ref, datt, dmid, nb, unit_ref, rstd_ref, *refs):
    small_ref, w_qkv, idx, g_proj, g_up, g_down, g_one, out_tw, *refs = refs
    outs, scratch = refs[:2], refs[2:]
    dq, dk, dv, mixed, d_one, drel, spread, g_qkv, g_two, g_all = scratch
    wins, _, chan = dmid.shape
    hmask = head_mask((HEADS, QPAD, chan))
    scale = (chan // HEADS) ** -0.5
    step_wins = 4
    drel[...] = jnp.zeros_like(drel)
    for at in range(0, wins, step_wins):
        group = range(at, at + step_wins)
        grads = [expand_heads(datt[win].astype(bf16).astype(f32), hmask) for win in group]
        d_probs = [mm(v_ref[win], one, NT) for win, one in zip(group, grads)]
        for win, one in zip(group, grads):
            dv[win] = mm(p_ref[win].astype(bf16), one)
        weighted = [p_ref[win] * one for win, one in zip(group, d_probs)]
        d_scores = [
            (one - p_ref[win] * jnp.sum(one, axis=0, keepdims=True)).astype(bf16) for win, one in zip(group, weighted)
        ]
        four = [one.astype(f32) for one in d_scores]
        drel[...] += (four[0] + four[1]) + (four[2] + four[3])
        for win, one in zip(group, d_scores):
            dk[win] = mm(one, qx[win]) * scale
        parts = [mm(one, k_ref[win], TN) for win, one in zip(group, d_scores)]
        for win, one in zip(group, parts):
            dq[win] = merge_heads(one, hmask) * scale
    sums = []
    for col, ref in enumerate((dq, dk, dv)):
        part = ref[...].reshape(wins * WTOK, chan).astype(bf16)
        mixed[:, col * chan : (col + 1) * chan] = part
        if col != 1:
            sums.append(jnp.sum(ref[...].reshape(wins * WTOK, chan), axis=0, keepdims=True))
    g_two[...] = jnp.zeros_like(g_two)
    g_two[2:3] = sums[0]
    g_two[3:4] = sums[1]
    g_qkv[...] = mm(nb[...], mixed[...], TN)
    weight = w_qkv[...]
    gain = small_ref[0:1]
    full = (step_wins * WTOK, chan)
    sum_gain, sum_shift = jnp.zeros((1, chan), f32), jnp.zeros((1, chan), f32)
    d_one[...] = mm(mixed[...], weight, NT)
    for at in range(0, wins, step_wins):
        span = slice(at, at + step_wins)
        d_normed = d_one[at * WTOK : (at + step_wins) * WTOK]
        unit = unit_ref[span].reshape(full)
        grad = dmid[span].reshape(full) + layer_back(d_normed * gain, unit, rstd_ref[span].reshape(full))
        out_tw[span] = grad.reshape(step_wins, WTOK, chan)
        sum_gain += jnp.sum(d_normed * unit, axis=0, keepdims=True)
        sum_shift += jnp.sum(d_normed, axis=0, keepdims=True)
    g_two[0:1] = sum_gain
    g_two[1:2] = sum_shift

    lanes = HEADS * QPAD
    row_a, row_b = iota((DIGIT, lanes), 0).astype(f32), iota((HEADS * DIGIT, lanes), 0).astype(f32)
    head_of = (iota((1, lanes), 1) // QPAD * DIGIT).astype(f32)

    for start in range(0, WTOK, 8):
        keys = range(start, start + 8)
        entries = [idx[key : key + 1, :] for key in keys]
        highs = [jnp.floor(entry * (1.0 / DIGIT)) for entry in entries]
        lows = [entry - high * DIGIT + head_of for entry, high in zip(entries, highs)]
        lefts = [
            jnp.where(row_a == high, drel[key : key + 1, :], 0.0).astype(bf16) for key, high in zip(keys, highs)
        ]
        rights = [jnp.where(row_b == low, 1.0, 0.0).astype(bf16) for low in lows]
        for key, left, right in zip(keys, lefts, rights):
            spread[key] = mm(left, right, NT)
    table = jnp.sum(spread[...], axis=0)
    g_two[4:SMALL, 0 : HEADS * DIGIT] = table[0 : SMALL - 4]
    if not count:
        outs[0][...] = g_qkv[...]
        outs[1][...] = g_two[...]
        return
    depth, ups = chan // count, g_up.shape[1] // chan
    deep = ups * depth
    first = (1 + 2 * ups) * depth
    for dest in range(count):
        at = dest * depth
        g_all[dest, 0:depth] = g_proj[at : at + depth].astype(bf16)
        for col in range(ups):
            part = g_up[at : at + depth, col * chan : (col + 1) * chan]
            g_all[dest, (1 + col) * depth : (2 + col) * depth] = part.astype(bf16)
        g_all[dest, (1 + ups) * depth : first] = g_down[dest * deep : (dest + 1) * deep].astype(bf16)
        for col in range(3):
            part = g_qkv[at : at + depth, col * chan : (col + 1) * chan]
            g_all[dest, first + col * depth : first + (col + 1) * depth] = part.astype(bf16)
        g_all[dest, first + 3 * depth : first + 3 * depth + SMALL] = g_one[...].astype(bf16)
        g_all[dest, first + 3 * depth + SMALL :] = g_two[...].astype(bf16)
    side = band_ref[0] % 2
    many = g_all.shape[1] // 2
    outs[0][...] = g_all[:, pl.ds(pl.multiple_of(side * many, many), many), :]
    outs[1][...] = g_all[:, pl.ds(pl.multiple_of((1 - side) * many, many), many), :]


def rows_body(bw, tw, out_bo, out_tg, out_halo):
    rows, cols, chan = out_bo.shape
    across = cols // WIN
    place = place_matrix(cols, SHIFT)
    twice = jnp.concatenate([place, place], axis=0)
    for row in range(rows):
        at, down = row // WIN * across, row % WIN * PADDED
        block = bw[at : at + across, down : down + PADDED, :].reshape(across * PADDED, chan).astype(bf16)
        block = mm(place, block, TN).astype(bf16)
        grad = tw[at : at + across, down : down + PADDED, :].reshape(across * PADDED, chan)
        high = grad.astype(bf16)
        low = (grad - high.astype(f32)).astype(bf16)
        grad = mm(twice, jnp.concatenate([high, low], axis=0), TN)
        if row + SHIFT < rows:
            out_bo[row + SHIFT] = block
            out_tg[row + SHIFT] = grad
        else:
            out_halo[0, row + SHIFT - rows] = block
            out_halo[1, row + SHIFT - rows] = grad.astype(bf16)
    for row in range(SHIFT):
        out_bo[row] = jnp.zeros((cols, chan), bf16)
        out_tg[row] = jnp.zeros((cols, chan), f32)


def total(refs):
    parts = [refs[source][...].astype(f32) for source in range(len(refs))]
    while len(parts) > 1:
        parts = [parts[i] + parts[i + 1] for i in range(0, len(parts), 2)]
    return parts[0]


def pair_body(mine, other, out):
    out[...] = (mine[...].astype(f32) + other[...].astype(f32)).astype(bf16)


def sum_body(pieces, out):
    out[...] = total([pieces.at[i] for i in range(pieces.shape[0])]).astype(bf16)


def final_body(bands, me_ref, band_ref, bo, tg, halo, *refs):
    both, outs, (rows_f, sems) = refs[:bands], refs[bands:-2], refs[-2:]
    (
        out_bo, out_tg, o_gain_one, o_shift_one, o_qkv, o_query, o_value, o_proj, o_bias_proj,
        o_gain_two, o_shift_two, o_up, o_bias_up, o_down, o_bias_down, o_table,
    ) = outs
    rows_f[...] = halo[1].astype(f32)
    copies = [
        pltpu.make_async_copy(halo.at[0], out_bo.at[0:SHIFT], sems.at[0]),
        pltpu.make_async_copy(rows_f, out_tg.at[0:SHIFT], sems.at[1]),
    ]
    for copy in copies:
        copy.start()
    me = me_ref[0]
    depth, chan = o_proj.shape
    ups = o_up.shape[1] // chan
    mine = total([both[step] for step in range(0, bands, 2)])
    other = total([both[step] for step in range(1, bands, 2)])
    even = band_ref[0] % 2 == 0
    summed = jnp.concatenate([jnp.where(even, mine, other), jnp.where(even, other, mine)], axis=0)
    first = (1 + 2 * ups) * depth
    o_proj[...] = summed[0:depth]
    for col in range(ups):
        o_up[:, col * chan : (col + 1) * chan] = summed[(1 + col) * depth : (2 + col) * depth]
    o_down[...] = summed[(1 + ups) * depth : first]
    for col in range(3):
        o_qkv[:, col * chan : (col + 1) * chan] = summed[first + col * depth : first + (col + 1) * depth]
    early = summed[first + 3 * depth : first + 3 * depth + SMALL]
    late = summed[first + 3 * depth + SMALL :]
    mine = jnp.concatenate([early[0:8], late[0:8]], axis=0)
    turned = pltpu.roll(mine, (chan - me * depth) % chan, 1)
    o_bias_proj[...] = turned[0:1, :depth]
    o_gain_two[...] = turned[1:2, :depth]
    o_shift_two[...] = turned[2:3, :depth]
    o_bias_down[...] = turned[3:4, :depth]
    o_gain_one[...] = turned[8:9, :depth]
    o_shift_one[...] = turned[9:10, :depth]
    o_query[...] = turned[10:11, :depth]
    o_value[...] = turned[11:12, :depth]
    at = me * depth * ups
    chosen = jnp.where(iota((8, chan), 0) == 4 + at // chan, early[0:8], 0.0)
    chosen = jnp.broadcast_to(jnp.sum(chosen, axis=0, keepdims=True), (8, chan))
    chosen = pltpu.roll(chosen, (chan - at % chan) % chan, 1)
    o_bias_up[...] = chosen[0:1, : depth * ups]
    for head in range(HEADS):
        for digit in range((TABLE + DIGIT - 1) // DIGIT):
            width = min(DIGIT, TABLE - digit * DIGIT)
            o_table[head : head + 1, digit * DIGIT : digit * DIGIT + width] = late[
                4 + digit : 5 + digit, head * DIGIT : head * DIGIT + width
            ]
    for copy in copies:
        copy.wait()


def call(body, outs, *args, scratch=(), ins=None, outs_at=None, name=None, limit=16, micros=1, aliases=None):
    at = lambda space: pl.BlockSpec(memory_space=space)
    return pl.pallas_call(
        body,
        out_shape=[jax.ShapeDtypeStruct(shape, dtype) for shape, dtype in outs],
        in_specs=[at(space) for space in (ins or [VMEM] * len(args))],
        out_specs=[at(space) for space in (outs_at or [VMEM] * len(outs))],
        scratch_shapes=[VMEM(*one) if isinstance(one, tuple) else one for one in scratch],
        input_output_aliases=aliases or {},
        compiler_params=pltpu.CompilerParams(vmem_limit_bytes=limit << 20),
        cost_estimate=pl.CostEstimate(flops=micros * 10**9, bytes_accessed=micros * 3 * 10**6, transcendentals=0),
        name=name,
    )(*args)


def shifted(value, axis, steps):
    count = lax.axis_size(axis)
    return lax.ppermute(value, axis, [(source, (source + steps) % count) for source in range(count)])


def swap(value, axis, step):
    count = lax.axis_size(axis)
    return lax.ppermute(value, axis, [(source, source ^ step) for source in range(count)])


def spread_out(value, i):
    bands, images = lax.axis_size("seq"), lax.axis_size("fsdp")
    pairs = [
        (band * images + image, band * images + (image ^ (band % 2 * (images // 2) + i)))
        for band in range(bands)
        for image in range(images)
    ]
    pairs = [pair for pair in pairs if pair[0] != pair[1]]
    return lax.ppermute(value, ("seq", "fsdp"), pairs)


def on_device(
    tokens_in, first_gain, first_shift, qkv_weight, query_bias, value_bias, proj_weight, proj_bias,
    second_gain, second_shift, up_weight, up_bias, down_weight, down_bias, bias_table, table_index,
    region_ids, cotangent,
):
    images, rows, cols, chan = tokens_in.shape
    assert images == 1
    fsdp, bands = lax.axis_size("fsdp"), lax.axis_size("seq")
    wide = up_weight.shape[1]
    depth = proj_weight.shape[0]
    wins = rows // WIN * (cols // WIN)
    direct = depth % 16 == 0
    count = fsdp if direct else 0
    tok, cot = tokens_in[0], cotangent[0]
    region = region_ids.reshape(rows, 1, cols)
    vectors = (
        first_gain, first_shift, query_bias, value_bias, proj_bias, second_gain, second_shift, down_bias, up_bias,
    )
    tokw = (wins, WTOK, chan)
    flatw = (wins * WTOK, chan)
    flatu = (wins * WTOK, wide)
    ups = wide // chan
    piece_rows = (1 + 2 * ups) * depth + 3 * depth + SMALL
    wide_scores = (wins, WTOK, HEADS * QPAD)
    sems = lambda many: pltpu.SemaphoreType.DMA((many,))
    near = fsdp // 2
    me = lax.axis_index("fsdp").astype(jnp.int32).reshape(1)
    band = lax.axis_index("seq").astype(jnp.int32).reshape(1)
    if direct:
        held = [vector.reshape(1, -1) for vector in vectors] + [qkv_weight, proj_weight, up_weight, down_weight]
        piece, halo = call(
            pack_body,
            [((piece_rows, chan), bf16), ((2, SHIFT, cols, chan), bf16)],
            *held, tok, cot, name="pack", limit=58, ins=[pl.ANY] * 15,
            scratch=[(array.shape, bf16) for array in held] + [sems(15)],
        )
        fetched = [spread_out(piece, i) for i in range(near)]
    else:
        halo = jnp.stack([tok[:SHIFT], cot[:SHIFT]])
        gather = functools.partial(lax.all_gather, axis_name="fsdp", axis=0, tiled=True)
        full = [gather(vector).astype(f32).reshape(-1, chan) for vector in vectors]
        full.append(jnp.zeros((SMALL - 8 - ups, chan), f32))
        weights = [
            gather(qkv_weight), jnp.concatenate(full, axis=0), gather(proj_weight), gather(up_weight),
            gather(down_weight),
        ]
    halo = shifted(halo, "seq", -1)
    bm, idx = call(
        bias_body,
        [(wide_scores, f32), ((WTOK, HEADS * QPAD), f32)],
        region, bias_table.T, table_index, tok, cot,
        scratch=[((DIGIT, HEADS * DIGIT), f32), ((WTOK, HEADS * QPAD), f32), ((wins, WTOK, 128), f32)],
        name="score_bias", micros=3,
    )
    if direct:
        *fetched, bm, idx = lax.optimization_barrier((*fetched, bm, idx))
        (pair,) = call(
            join_body, [((near, piece_rows, chan), bf16)], band, piece, *fetched, name="join",
            ins=[pltpu.SMEM] + [VMEM] * (1 + near),
        )
        weights = [pair, swap(pair, "seq", 1)]
    xw, cw, unit, rstd = call(prepare_body, [(tokw, f32)] * 4, tok, cot, halo, name="prepare", micros=2)
    big = dict(limit=32)
    place = [pltpu.SMEM] * 2
    nb, qx, k_b, v_b, probs, att, small, w_qkv, w_proj, w_up, w_down = call(
        functools.partial(attend_body, count),
        [
            (flatw, bf16), ((wins, HEADS * QPAD, chan), bf16), (tokw, bf16), (tokw, bf16), (wide_scores, f32),
            (tokw, f32), ((SMALL, chan), f32), ((chan, 3 * chan), bf16), ((chan, chan), bf16), ((chan, wide), bf16),
            ((wide, chan), bf16),
        ],
        me, band, unit, bm, *weights, name="attention", micros=3, ins=place + [VMEM] * (2 + len(weights)), **big,
        scratch=[((wins * WTOK, 3 * chan), f32)],
    )
    bw, dmid, datt, g_proj, g_up, g_down, g_one = call(
        mlp_body,
        [
            (tokw, f32), (tokw, f32), (tokw, f32), ((chan, chan), f32), ((chan, wide), f32), ((wide, chan), f32),
            ((SMALL, chan), f32),
        ],
        xw, cw, att, small, w_proj, w_up, w_down, name="feed_forward", micros=5, **big,
        scratch=[(flatw, bf16)] * 4 + [(flatu, bf16)] * 2 + [(flatu, f32)] * 2 + [(flatw, f32)] * 4,
    )
    if direct:
        halves = ((fsdp, (piece_rows + SMALL) // 2, chan), bf16)
        sent = [halves] * 2
    else:
        sent = [((chan, 3 * chan), f32), ((SMALL, chan), f32)]
    tw, *grads = call(
        functools.partial(back_body, count),
        [(tokw, f32)] + sent,
        band, qx, k_b, v_b, probs, datt, dmid, nb, unit, rstd, small, w_qkv, idx, g_proj, g_up, g_down, g_one,
        name="attention_back", micros=5, ins=place[:1] + [VMEM] * 16, **big,
        scratch=[
            (tokw, f32), (tokw, f32), (tokw, f32), ((wins * WTOK, 3 * chan), bf16), (flatw, f32),
            ((WTOK, HEADS * QPAD), f32), ((WTOK, DIGIT, HEADS * DIGIT), f32), ((chan, 3 * chan), f32), ((SMALL, chan), f32),
            ((max(count, 1), piece_rows + SMALL, chan), bf16),
        ],
    )
    bo, tg, last = call(
        rows_body,
        [((rows, cols, chan), bf16), ((rows, cols, chan), f32), ((2, SHIFT, cols, chan), bf16)],
        bw, tw, name="rows", micros=2,
    )
    if not direct:
        last = shifted(last, "seq", 1)
        g_proj, g_up, g_down, early, g_qkv, late = lax.psum((g_proj, g_up, g_down, g_one, *grads), "seq")
        digits = (TABLE + DIGIT - 1) // DIGIT
        table = lax.psum(late[4 : 4 + digits, : HEADS * DIGIT], "fsdp").reshape(digits, HEADS, DIGIT)
        table = table.transpose(1, 0, 2).reshape(HEADS, digits * DIGIT)[:, :TABLE]
        scatter = functools.partial(lax.psum_scatter, axis_name="fsdp", scatter_dimension=0, tiled=True)
        block_out = jnp.concatenate([last[0], bo[SHIFT:]], axis=0)
        tokens_grad = jnp.concatenate([last[1].astype(f32), tg[SHIFT:]], axis=0)
        return (
            block_out[None], tokens_grad[None], scatter(late[0]), scatter(late[1]), scatter(g_qkv),
            scatter(late[2]), scatter(late[3]), scatter(g_proj), scatter(early[0]), scatter(early[1]),
            scatter(early[2]), scatter(g_up), scatter(early[4 : 4 + ups].reshape(-1)),
            scatter(g_down), scatter(early[3]), table.T,
        )
    kept, given = grads[0], swap(grads[1], "seq", 1)
    kept, given, last = lax.optimization_barrier((kept, given, last))
    last = shifted(last, "seq", 1)
    (kept,) = call(pair_body, [halves], kept, given, name="sum_cores")
    pieces = lax.all_to_all(kept, "fsdp", 0, 0, tiled=True)
    (both,) = call(sum_body, [(halves[0][1:], bf16)], pieces, name="sum_images")
    arrived = [both] + [swap(both, "seq", step) for step in range(1, bands)]
    line = ((1, depth), f32)
    outs = call(
        functools.partial(final_body, bands),
        [
            ((rows, cols, chan), bf16), ((rows, cols, chan), f32), line, line, ((depth, 3 * chan), f32), line,
            line, ((depth, chan), f32), line, line, line, ((depth, wide), f32), ((1, depth * ups), f32),
            ((depth * ups, chan), f32), line, ((HEADS, TABLE), f32),
        ],
        me, band, bo, tg, last, *arrived, name="finish", aliases={2: 0, 3: 1},
        ins=[pltpu.SMEM] * 2 + [pl.ANY] * 2 + [VMEM] * (1 + bands), outs_at=[pl.ANY, pl.ANY] + [VMEM] * 14,
        scratch=[((SHIFT, cols, chan), f32), sems(2)],
    )
    outs = [out.reshape(-1) if out.shape[0] == 1 else out for out in outs]
    return (outs[0][None], outs[1][None], *outs[2:15], outs[15].T)


def solution(mesh):
    placed = (
        P("fsdp", "seq", None, None),
        P("fsdp"),
        P("fsdp"),
        P("fsdp", None),
        P("fsdp"),
        P("fsdp"),
        P("fsdp", None),
        P("fsdp"),
        P("fsdp"),
        P("fsdp"),
        P("fsdp", None),
        P("fsdp"),
        P("fsdp", None),
        P("fsdp"),
        P(),
        P(),
        P("fsdp", "seq", None),
        P("fsdp", "seq", None, None),
    )
    return jax.shard_map(
        on_device,
        mesh=mesh,
        in_specs=placed,
        out_specs=(
            P("fsdp", "seq", None, None),
            P("fsdp", "seq", None, None),
            P("fsdp"),
            P("fsdp"),
            P("fsdp", None),
            P("fsdp"),
            P("fsdp"),
            P("fsdp", None),
            P("fsdp"),
            P("fsdp"),
            P("fsdp"),
            P("fsdp", None),
            P("fsdp"),
            P("fsdp", None),
            P("fsdp"),
            P(),
        ),
        check_vma=False,
    )
```

```python
import functools

import jax
import jax.numpy as jnp
from jax import lax
from jax.experimental import pallas as pl
from jax.experimental.pallas import tpu as pltpu
from jax.sharding import PartitionSpec as P

HEADS = 4
WIN = 7
SHIFT = 3
TABLE = 169
PADDED = 8
WTOK = WIN * PADDED
QPAD = 64
SMALL = 16
DIGIT = 16

norm_eps = 1e-05
masked_fill = -1e30
f32 = jnp.float32
bf16 = jnp.bfloat16
NT = (((1,), (1,)), ((), ()))
TN = (((0,), (0,)), ((), ()))
VMEM = pltpu.VMEM


def mm(left, right, dims=(((1,), (0,)), ((), ()))):
    return lax.dot_general(left, right, dims, preferred_element_type=f32)


def iota(shape, axis):
    return lax.broadcasted_iota(jnp.int32, shape, axis)


def place_matrix(cols, roll):
    spots = cols // WIN * PADDED
    spot, col = iota((spots, cols), 0), iota((spots, cols), 1)
    place = spot % PADDED
    target = spot // PADDED * WIN + place + roll
    target = jnp.where(target >= cols, target - cols, target)
    return jnp.where((place < WIN) & (col == target), 1.0, 0.0).astype(bf16)


def head_mask(shape, lane_axis=1):
    chans = shape[-1] // HEADS
    return jnp.where(iota(shape, len(shape) - 1) // chans == iota(shape, 0), 1.0, 0.0)


def expand_heads(tokens, hmask):
    zeros = jnp.zeros((QPAD - WTOK, tokens.shape[1]), f32)
    full = jnp.concatenate([tokens, zeros], axis=0)
    return (full[None] * hmask).reshape(HEADS * QPAD, tokens.shape[1]).astype(bf16)


def merge_heads(stacked, hmask):
    parts = stacked.reshape(HEADS, QPAD, stacked.shape[1]) * hmask
    return ((parts[0] + parts[1]) + (parts[2] + parts[3]))[:WTOK]


def lane_mean(values):
    return jnp.mean(values, axis=-1, keepdims=True)


def pack_body(*refs):
    given, (out, out_h), scratch, sems = refs[:15], refs[15:17], refs[17:-1], refs[-1]
    sources = list(given[:13]) + [ref.at[0:SHIFT] for ref in given[13:]]
    targets = list(scratch) + [out_h.at[0], out_h.at[1]]
    copies = [
        pltpu.make_async_copy(source, target, sems.at[i])
        for i, (source, target) in enumerate(zip(sources, targets))
    ]
    for copy in copies:
        copy.start()
    for copy in copies:
        copy.wait()
    vectors, (qkv, proj, up, down) = scratch[:9], scratch[9:]
    depth, chan = proj.shape
    blocks, ups = qkv.shape[1] // chan, up.shape[1] // chan
    small = jnp.concatenate(
        [jnp.pad(vector[...].astype(f32), ((0, 0), (0, chan - vector.shape[1]))) for vector in vectors]
        + [jnp.zeros((SMALL - 9, chan), f32)],
        axis=0,
    ).astype(bf16)
    parts = [proj[...]]
    parts += [up[:, col * chan : (col + 1) * chan] for col in range(ups)]
    parts += [down[...]]
    parts += [qkv[:, col * chan : (col + 1) * chan] for col in range(blocks)]
    parts += [small]
    at = 0
    for part in parts:
        out[at : at + part.shape[0]] = part
        at += part.shape[0]


def join_body(*refs):
    for i, piece in enumerate(refs[:-1]):
        refs[-1][i] = piece[...]


def bias_body(region, table, index, tok, cot, out_bm, out_idx, tab, rel, ident):
    rows, _, cols = region.shape
    tokens = index.shape[0]
    wide = HEADS * QPAD
    token_a, spot_a = iota((tokens, WTOK), 0), iota((tokens, WTOK), 1)
    keys_at = jnp.where(token_a // WIN * PADDED + token_a % WIN == spot_a, 1.0, 0.0).astype(bf16)
    token_b, lane_b = iota((tokens, wide), 0), iota((tokens, wide), 1)
    queries_at = jnp.where(token_b // WIN * PADDED + token_b % WIN == lane_b % QPAD, 1.0, 0.0).astype(bf16)
    half = mm(index[...].astype(f32).astype(bf16), keys_at).astype(bf16)
    out_idx[...] = mm(half, queries_at, TN)
    tab[...] = jnp.zeros_like(tab)
    for head in range(HEADS):
        for digit in range((TABLE + DIGIT - 1) // DIGIT):
            width = min(DIGIT, TABLE - digit * DIGIT)
            tab[digit : digit + 1, head * DIGIT : head * DIGIT + width] = table[
                head : head + 1, digit * DIGIT : digit * DIGIT + width
            ]
    entries = tab[...]
    first = entries.astype(bf16).astype(f32)
    second = (entries - first).astype(bf16).astype(f32)
    terms = jnp.concatenate([first, second, entries - first - second], axis=0).astype(bf16)
    digit_a = (iota((3 * DIGIT, wide), 0) % DIGIT).astype(f32)
    row_b = iota((HEADS * DIGIT, wide), 0).astype(f32)
    head_of = (iota((1, wide), 1) // QPAD * DIGIT).astype(f32)

    for start in range(0, WTOK, 8):
        keys = range(start, start + 8)
        lines = [out_idx[key : key + 1, :] for key in keys]
        highs = [jnp.floor(entry * (1.0 / DIGIT)) for entry in lines]
        lows = [entry - high * DIGIT + head_of for entry, high in zip(lines, highs)]
        found = [mm(terms, jnp.where(row_b == low, 1.0, 0.0).astype(bf16)) for low in lows]
        found = [jnp.where(digit_a == high, one, 0.0) for high, one in zip(highs, found)]
        for key, one in zip(keys, found):
            rel[key : key + 1, :] = jnp.sum(one, axis=0, keepdims=True)
    place = place_matrix(cols, 0)
    across = cols // WIN
    for row in range(rows):
        classes = jnp.where(iota((128, cols), 0) == region[row], 1.0, 0.0).astype(bf16)
        at = row // WIN * across
        down = row % WIN * PADDED
        ident[at : at + across, down : down + PADDED, :] = mm(place, classes, NT).reshape(
            across, PADDED, 128
        )
    bias = rel[...]
    for win in range(rows // WIN * across):
        here = ident[win]
        other = jnp.concatenate([here, jnp.zeros((QPAD - WTOK, 128), f32)], axis=0)
        other = jnp.broadcast_to(other[None], (HEADS, QPAD, 128)).reshape(wide, 128).astype(bf16)
        out_bm[win] = jnp.where(mm(here.astype(bf16), other, NT) > 0.5, bias, masked_fill)


def assemble_vectors(pieces, sources, count, offset, out_small):
    chan = pieces[0].shape[1]
    per, per_up = chan // count, 4 * chan // count
    row = iota((8, chan), 0)
    vecs, ups = jnp.zeros((8, chan), f32), jnp.zeros((8, chan), f32)
    for piece, source in zip(pieces, sources):
        block = piece[offset : offset + SMALL].astype(f32)
        vecs += pltpu.roll(block[0:8], source * per, 1)
        at = source * per_up
        line = pltpu.roll(jnp.broadcast_to(block[8:9], (8, chan)), at % chan, 1)
        ups += jnp.where(row == at // chan, line, 0.0)
    out_small[0:8] = vecs
    out_small[8:16] = ups


def gelu_parts(hidden):
    base = 1.0 + (0.3275911 * 0.5**0.5) * jnp.abs(hidden)
    term = pl.reciprocal(base, approx=True)
    term = term * (2.0 - base * term)
    bell = jnp.exp(-0.5 * (hidden * hidden))
    poly = (0.5 * 1.061405429) * term - (0.5 * 1.453152027)
    poly = poly * term + (0.5 * 1.421413741)
    poly = poly * term - (0.5 * 0.284496736)
    poly = poly * term + (0.5 * 0.254829592)
    tail = poly * term * bell
    cdf = jnp.where(hidden >= 0, 1.0 - tail, tail)
    return cdf, cdf + hidden * (bell * 0.3989422804014327)


def layer_stats(values):
    centred = values - lane_mean(values)
    rstd = lax.rsqrt(lane_mean(centred * centred) + norm_eps)
    return centred * rstd, rstd


def layer_back(d_unit, unit, rstd):
    return rstd * (d_unit - lane_mean(d_unit) - unit * lane_mean(d_unit * unit))


def my_images(me_ref, band_ref, count):
    near = count // 2
    return [me_ref[0] ^ ((band_ref[0] % 2 ^ core) * near + i) for core in range(2) for i in range(near)]


def prepare_body(tok, cot, halo, out_xw, out_cw, out_unit, out_rstd):
    rows, cols, chan = tok.shape
    across = cols // WIN
    place = place_matrix(cols, SHIFT)
    for which, source, target in ((0, tok, out_xw), (1, cot, out_cw)):
        for row in range(rows):
            line = source[row + SHIFT] if row + SHIFT < rows else halo[which, row + SHIFT - rows]
            at, down = row // WIN * across, row % WIN * PADDED
            target[at : at + across, down : down + PADDED, :] = mm(place, line).reshape(across, PADDED, chan)
    step_wins = 4
    for at in range(0, out_xw.shape[0], step_wins):
        span = slice(at, at + step_wins)
        unit, rstd = layer_stats(out_xw[span])
        out_unit[span] = unit
        out_rstd[span] = jnp.broadcast_to(rstd, unit.shape)


def attend_body(count, me_ref, band_ref, unit, bm, *refs):
    inputs = 2 if count else 5
    weights, outs = refs[:inputs], refs[inputs:]
    out_nb, out_qx, out_k, out_v, out_p, out_att, out_small, w_qkv, w_proj, w_up, w_down, mixed = outs
    wins, _, chan = unit.shape
    if count:
        sources = my_images(me_ref, band_ref, count)
        pieces = [weights[core].at[i] for core in range(2) for i in range(count // 2)]
        depth, ups = chan // count, w_up.shape[1] // chan
        deep = ups * depth
        first = (1 + 2 * ups) * depth
        for piece, source in zip(pieces, sources):
            here = pl.ds(pl.multiple_of(source * depth, depth), depth)
            for col in range(3):
                w_qkv[here, col * chan : (col + 1) * chan] = piece[first + col * depth : first + (col + 1) * depth]
            w_proj[here] = piece[0:depth]
            for col in range(ups):
                w_up[here, col * chan : (col + 1) * chan] = piece[(1 + col) * depth : (2 + col) * depth]
            w_down[pl.ds(pl.multiple_of(source * deep, deep), deep)] = piece[(1 + ups) * depth : first]
        assemble_vectors(pieces, sources, count, first + 3 * depth, out_small)
    else:
        for source, target in zip(weights, (w_qkv, out_small, w_proj, w_up, w_down)):
            target[...] = source[...]
    small = out_small[...]
    gain, shift, bias_q, bias_v = small[0:1], small[1:2], small[2:3], small[3:4]
    hmask = head_mask((HEADS, QPAD, chan))
    scale = (chan // HEADS) ** -0.5
    step_wins = 4
    weight = w_qkv[...]
    for at in range(0, wins, step_wins):
        normed = (unit[at : at + step_wins].reshape(step_wins * WTOK, chan) * gain + shift).astype(bf16)
        out_nb[at * WTOK : (at + step_wins) * WTOK] = normed
    mixed[...] = mm(out_nb[...], weight)
    for at in range(0, wins, step_wins):
        three = mixed[at * WTOK : (at + step_wins) * WTOK]
        query = three[:, :chan] + bias_q
        key = three[:, chan : 2 * chan]
        value = three[:, 2 * chan :] + bias_v
        for win in range(step_wins):
            span = slice(win * WTOK, (win + 1) * WTOK)
            out_qx[at + win] = expand_heads(query[span].astype(bf16).astype(f32), hmask)
            out_k[at + win] = key[span].astype(bf16)
            out_v[at + win] = value[span].astype(bf16)
    for at in range(0, wins, step_wins):
        group = range(at, at + step_wins)
        scores = [mm(out_k[win], out_qx[win], NT) * scale + bm[win] for win in group]
        expos = [jnp.exp(one - jnp.max(one, axis=0, keepdims=True)) for one in scores]
        probs = [one * (1.0 / jnp.sum(one, axis=0, keepdims=True)) for one in expos]
        for win, one in zip(group, probs):
            out_p[win] = one
        parts = [mm(one.astype(bf16), out_v[win], TN) for win, one in zip(group, probs)]
        for win, one in zip(group, parts):
            out_att[win] = merge_heads(one, hmask)


def mlp_body(xw, cw, att, small_ref, w_proj, w_up, w_down, *refs):
    out_bw, out_dmid, out_datt, g_proj, g_up, g_down, g_one, *scratch = refs
    att_b, n2_b, dbr_b, dy_b, act_b, dh_b, hid, dact, mid, unit2, rstd2, back = scratch
    wins, _, chan = xw.shape
    wide = w_up.shape[1]
    ups = wide // chan
    small = small_ref[...]
    bias_p, gain, shift, bias_d = small[4:5], small[5:6], small[6:7], small[7:8]
    bias_u = jnp.concatenate([small[8 + i : 9 + i] for i in range(ups)], axis=1)
    weight_p, weight_u, weight_d = w_proj[...], w_up[...], w_down[...]
    half = wins // 2
    few = 4
    full, split = (few * WTOK, chan), (few, WTOK, chan)
    sums = [jnp.zeros((1, chan), f32) for _ in range(4)]
    sum_up = jnp.zeros((8, wide), f32)

    def rows_of(at, many):
        return slice(at, at + many), slice(at * WTOK, (at + many) * WTOK)

    def enter(at):
        span, flat = rows_of(at, half)
        dy_b[flat] = cw[span].reshape(half * WTOK, chan).astype(bf16)
        dact[flat] = mm(dy_b[flat], weight_d, NT)
        att_b[flat] = att[span].reshape(half * WTOK, chan).astype(bf16)
        mid[flat] = mm(att_b[flat], weight_p)
        for some in range(at, at + half, few):
            here, line = rows_of(some, few)
            middle = xw[here].reshape(full) + (mid[line] + bias_p)
            mid[line] = middle
            unit, rstd = layer_stats(middle)
            unit2[line] = unit
            rstd2[line] = jnp.broadcast_to(rstd, full)
            n2_b[line] = (unit * gain + shift).astype(bf16)
        hid[flat] = mm(n2_b[flat], weight_u)

    def tiles(at, have):
        for row in range(at * WTOK, (at + half) * WTOK, 16):
            line = slice(row, row + 16)
            hidden = hid[line] + bias_u
            cdf, slope = gelu_parts(hidden)
            act_b[line] = (hidden * cdf).astype(bf16)
            d_hidden = dact[line] * slope
            dh_b[line] = d_hidden.astype(bf16)
            have = have + (d_hidden[0:8] + d_hidden[8:16])
        return have

    def leave(at, have):
        span, flat = rows_of(at, half)
        out_bw[span] = (mid[flat] + mm(act_b[flat], weight_d) + bias_d).reshape(half, WTOK, chan)
        back[flat] = mm(dh_b[flat], weight_u, NT)
        for some in range(at, at + half, few):
            here, line = rows_of(some, few)
            d_normed = back[line]
            unit = unit2[line]
            grad = cw[here].reshape(full)
            d_middle = grad + layer_back(d_normed * gain, unit, rstd2[line])
            out_dmid[here] = d_middle.reshape(split)
            dbr_b[line] = d_middle.astype(bf16)
            terms = (d_middle, d_normed * unit, d_normed, grad)
            have = [one + jnp.sum(term, axis=0, keepdims=True) for one, term in zip(have, terms)]
        out_datt[span] = mm(dbr_b[flat], weight_p, NT).reshape(half, WTOK, chan)
        return have

    enter(0)
    enter(half)
    sum_up = tiles(0, sum_up)
    sums = leave(0, sums)
    sum_up = tiles(half, sum_up)
    sums = leave(half, sums)
    g_one[...] = jnp.zeros_like(g_one)
    for row in range(4):
        g_one[row : row + 1] = sums[row]
    total_up = jnp.sum(sum_up, axis=0, keepdims=True)
    for col in range(ups):
        g_one[4 + col : 5 + col] = total_up[:, col * chan : (col + 1) * chan]
    g_down[...] = mm(dy_b[...], act_b[...], TN).T
    g_up[...] = mm(n2_b[...], dh_b[...], TN)
    g_proj[...] = mm(att_b[...], dbr_b[...], TN)


def back_body(count, band_ref, qx, k_ref, v_ref, p_ref, datt, dmid, nb, unit_ref, rstd_ref, *refs):
    small_ref, w_qkv, idx, g_proj, g_up, g_down, g_one, out_tw, *refs = refs
    outs, scratch = refs[:2], refs[2:]
    dq, dk, dv, mixed, d_one, drel, spread, g_qkv, g_two, g_all = scratch
    wins, _, chan = dmid.shape
    hmask = head_mask((HEADS, QPAD, chan))
    scale = (chan // HEADS) ** -0.5
    step_wins = 4
    drel[...] = jnp.zeros_like(drel)
    for at in range(0, wins, step_wins):
        group = range(at, at + step_wins)
        grads = [expand_heads(datt[win].astype(bf16).astype(f32), hmask) for win in group]
        d_probs = [mm(v_ref[win], one, NT) for win, one in zip(group, grads)]
        for win, one in zip(group, grads):
            dv[win] = mm(p_ref[win].astype(bf16), one)
        weighted = [p_ref[win] * one for win, one in zip(group, d_probs)]
        d_scores = [
            (one - p_ref[win] * jnp.sum(one, axis=0, keepdims=True)).astype(bf16) for win, one in zip(group, weighted)
        ]
        four = [one.astype(f32) for one in d_scores]
        drel[...] += (four[0] + four[1]) + (four[2] + four[3])
        for win, one in zip(group, d_scores):
            dk[win] = mm(one, qx[win]) * scale
        parts = [mm(one, k_ref[win], TN) for win, one in zip(group, d_scores)]
        for win, one in zip(group, parts):
            dq[win] = merge_heads(one, hmask) * scale
    sums = []
    for col, ref in enumerate((dq, dk, dv)):
        part = ref[...].reshape(wins * WTOK, chan).astype(bf16)
        mixed[:, col * chan : (col + 1) * chan] = part
        if col != 1:
            sums.append(jnp.sum(ref[...].reshape(wins * WTOK, chan), axis=0, keepdims=True))
    g_two[...] = jnp.zeros_like(g_two)
    g_two[2:3] = sums[0]
    g_two[3:4] = sums[1]
    g_qkv[...] = mm(nb[...], mixed[...], TN)
    weight = w_qkv[...]
    gain = small_ref[0:1]
    full = (step_wins * WTOK, chan)
    sum_gain, sum_shift = jnp.zeros((1, chan), f32), jnp.zeros((1, chan), f32)
    d_one[...] = mm(mixed[...], weight, NT)
    for at in range(0, wins, step_wins):
        span = slice(at, at + step_wins)
        d_normed = d_one[at * WTOK : (at + step_wins) * WTOK]
        unit = unit_ref[span].reshape(full)
        grad = dmid[span].reshape(full) + layer_back(d_normed * gain, unit, rstd_ref[span].reshape(full))
        out_tw[span] = grad.reshape(step_wins, WTOK, chan)
        sum_gain += jnp.sum(d_normed * unit, axis=0, keepdims=True)
        sum_shift += jnp.sum(d_normed, axis=0, keepdims=True)
    g_two[0:1] = sum_gain
    g_two[1:2] = sum_shift

    lanes = HEADS * QPAD
    row_a, row_b = iota((DIGIT, lanes), 0).astype(f32), iota((HEADS * DIGIT, lanes), 0).astype(f32)
    head_of = (iota((1, lanes), 1) // QPAD * DIGIT).astype(f32)

    for start in range(0, WTOK, 8):
        keys = range(start, start + 8)
        entries = [idx[key : key + 1, :] for key in keys]
        highs = [jnp.floor(entry * (1.0 / DIGIT)) for entry in entries]
        lows = [entry - high * DIGIT + head_of for entry, high in zip(entries, highs)]
        lefts = [
            jnp.where(row_a == high, drel[key : key + 1, :], 0.0).astype(bf16) for key, high in zip(keys, highs)
        ]
        rights = [jnp.where(row_b == low, 1.0, 0.0).astype(bf16) for low in lows]
        for key, left, right in zip(keys, lefts, rights):
            spread[key] = mm(left, right, NT)
    table = jnp.sum(spread[...], axis=0)
    g_two[4:SMALL, 0 : HEADS * DIGIT] = table[0 : SMALL - 4]
    if not count:
        outs[0][...] = g_qkv[...]
        outs[1][...] = g_two[...]
        return
    depth, ups = chan // count, g_up.shape[1] // chan
    deep = ups * depth
    first = (1 + 2 * ups) * depth
    for dest in range(count):
        at = dest * depth
        g_all[dest, 0:depth] = g_proj[at : at + depth].astype(bf16)
        for col in range(ups):
            part = g_up[at : at + depth, col * chan : (col + 1) * chan]
            g_all[dest, (1 + col) * depth : (2 + col) * depth] = part.astype(bf16)
        g_all[dest, (1 + ups) * depth : first] = g_down[dest * deep : (dest + 1) * deep].astype(bf16)
        for col in range(3):
            part = g_qkv[at : at + depth, col * chan : (col + 1) * chan]
            g_all[dest, first + col * depth : first + (col + 1) * depth] = part.astype(bf16)
        g_all[dest, first + 3 * depth : first + 3 * depth + SMALL] = g_one[...].astype(bf16)
        g_all[dest, first + 3 * depth + SMALL :] = g_two[...].astype(bf16)
    side = band_ref[0] % 2
    many = g_all.shape[1] // 2
    outs[0][...] = g_all[:, pl.ds(pl.multiple_of(side * many, many), many), :]
    outs[1][...] = g_all[:, pl.ds(pl.multiple_of((1 - side) * many, many), many), :]


def rows_body(bw, tw, out_bo, out_tg, out_halo):
    rows, cols, chan = out_bo.shape
    across = cols // WIN
    place = place_matrix(cols, SHIFT)
    twice = jnp.concatenate([place, place], axis=0)
    for row in range(rows):
        at, down = row // WIN * across, row % WIN * PADDED
        block = bw[at : at + across, down : down + PADDED, :].reshape(across * PADDED, chan).astype(bf16)
        block = mm(place, block, TN).astype(bf16)
        grad = tw[at : at + across, down : down + PADDED, :].reshape(across * PADDED, chan)
        high = grad.astype(bf16)
        low = (grad - high.astype(f32)).astype(bf16)
        grad = mm(twice, jnp.concatenate([high, low], axis=0), TN)
        if row + SHIFT < rows:
            out_bo[row + SHIFT] = block
            out_tg[row + SHIFT] = grad
        else:
            out_halo[0, row + SHIFT - rows] = block
            out_halo[1, row + SHIFT - rows] = grad.astype(bf16)
    for row in range(SHIFT):
        out_bo[row] = jnp.zeros((cols, chan), bf16)
        out_tg[row] = jnp.zeros((cols, chan), f32)


def total(refs):
    parts = [refs[source][...].astype(f32) for source in range(len(refs))]
    while len(parts) > 1:
        parts = [parts[i] + parts[i + 1] for i in range(0, len(parts), 2)]
    return parts[0]


def pair_body(mine, other, out):
    out[...] = (mine[...].astype(f32) + other[...].astype(f32)).astype(bf16)


def sum_body(pieces, out):
    out[...] = total([pieces.at[i] for i in range(pieces.shape[0])]).astype(bf16)


def final_body(bands, me_ref, band_ref, bo, tg, halo, *refs):
    both, outs = refs[:bands], refs[bands:]
    (
        out_bo, out_tg, o_gain_one, o_shift_one, o_qkv, o_query, o_value, o_proj, o_bias_proj,
        o_gain_two, o_shift_two, o_up, o_bias_up, o_down, o_bias_down, o_table,
    ) = outs
    out_bo[SHIFT:] = bo[SHIFT:]
    out_tg[SHIFT:] = tg[SHIFT:]
    for row in range(SHIFT):
        out_bo[row] = halo[0, row]
        out_tg[row] = halo[1, row].astype(f32)
    me = me_ref[0]
    depth, chan = o_proj.shape
    ups = o_up.shape[1] // chan
    mine = total([both[step] for step in range(0, bands, 2)])
    other = total([both[step] for step in range(1, bands, 2)])
    even = band_ref[0] % 2 == 0
    summed = jnp.concatenate([jnp.where(even, mine, other), jnp.where(even, other, mine)], axis=0)
    first = (1 + 2 * ups) * depth
    o_proj[...] = summed[0:depth]
    for col in range(ups):
        o_up[:, col * chan : (col + 1) * chan] = summed[(1 + col) * depth : (2 + col) * depth]
    o_down[...] = summed[(1 + ups) * depth : first]
    for col in range(3):
        o_qkv[:, col * chan : (col + 1) * chan] = summed[first + col * depth : first + (col + 1) * depth]
    early = summed[first + 3 * depth : first + 3 * depth + SMALL]
    late = summed[first + 3 * depth + SMALL :]
    mine = jnp.concatenate([early[0:8], late[0:8]], axis=0)
    turned = pltpu.roll(mine, (chan - me * depth) % chan, 1)
    o_bias_proj[...] = turned[0:1, :depth]
    o_gain_two[...] = turned[1:2, :depth]
    o_shift_two[...] = turned[2:3, :depth]
    o_bias_down[...] = turned[3:4, :depth]
    o_gain_one[...] = turned[8:9, :depth]
    o_shift_one[...] = turned[9:10, :depth]
    o_query[...] = turned[10:11, :depth]
    o_value[...] = turned[11:12, :depth]
    at = me * depth * ups
    chosen = jnp.where(iota((8, chan), 0) == 4 + at // chan, early[0:8], 0.0)
    chosen = jnp.broadcast_to(jnp.sum(chosen, axis=0, keepdims=True), (8, chan))
    chosen = pltpu.roll(chosen, (chan - at % chan) % chan, 1)
    o_bias_up[...] = chosen[0:1, : depth * ups]
    for head in range(HEADS):
        for digit in range((TABLE + DIGIT - 1) // DIGIT):
            width = min(DIGIT, TABLE - digit * DIGIT)
            o_table[head : head + 1, digit * DIGIT : digit * DIGIT + width] = late[
                4 + digit : 5 + digit, head * DIGIT : head * DIGIT + width
            ]


def call(body, outs, *args, scratch=(), ins=None, outs_at=None, name=None, limit=16, micros=1, aliases=None):
    at = lambda space: pl.BlockSpec(memory_space=space)
    return pl.pallas_call(
        body,
        out_shape=[jax.ShapeDtypeStruct(shape, dtype) for shape, dtype in outs],
        in_specs=[at(space) for space in (ins or [VMEM] * len(args))],
        out_specs=[at(space) for space in (outs_at or [VMEM] * len(outs))],
        scratch_shapes=[VMEM(*one) if isinstance(one, tuple) else one for one in scratch],
        input_output_aliases=aliases or {},
        compiler_params=pltpu.CompilerParams(vmem_limit_bytes=limit << 20),
        cost_estimate=pl.CostEstimate(flops=micros * 10**9, bytes_accessed=micros * 3 * 10**6, transcendentals=0),
        name=name,
    )(*args)


def shifted(value, axis, steps):
    count = lax.axis_size(axis)
    return lax.ppermute(value, axis, [(source, (source + steps) % count) for source in range(count)])


def swap(value, axis, step):
    count = lax.axis_size(axis)
    return lax.ppermute(value, axis, [(source, source ^ step) for source in range(count)])


def spread_out(value, i):
    bands, images = lax.axis_size("seq"), lax.axis_size("fsdp")
    pairs = [
        (band * images + image, band * images + (image ^ (band % 2 * (images // 2) + i)))
        for band in range(bands)
        for image in range(images)
    ]
    return lax.ppermute(value, ("seq", "fsdp"), pairs)


def on_device(
    tokens_in, first_gain, first_shift, qkv_weight, query_bias, value_bias, proj_weight, proj_bias,
    second_gain, second_shift, up_weight, up_bias, down_weight, down_bias, bias_table, table_index,
    region_ids, cotangent,
):
    images, rows, cols, chan = tokens_in.shape
    assert images == 1
    fsdp, bands = lax.axis_size("fsdp"), lax.axis_size("seq")
    wide = up_weight.shape[1]
    depth = proj_weight.shape[0]
    wins = rows // WIN * (cols // WIN)
    direct = depth % 16 == 0
    count = fsdp if direct else 0
    tok, cot = tokens_in[0], cotangent[0]
    region = region_ids.reshape(rows, 1, cols)
    vectors = (
        first_gain, first_shift, query_bias, value_bias, proj_bias, second_gain, second_shift, down_bias, up_bias,
    )
    tokw = (wins, WTOK, chan)
    flatw = (wins * WTOK, chan)
    flatu = (wins * WTOK, wide)
    ups = wide // chan
    piece_rows = (1 + 2 * ups) * depth + 3 * depth + SMALL
    wide_scores = (wins, WTOK, HEADS * QPAD)
    sems = lambda many: pltpu.SemaphoreType.DMA((many,))
    near = fsdp // 2
    me = lax.axis_index("fsdp").astype(jnp.int32).reshape(1)
    band = lax.axis_index("seq").astype(jnp.int32).reshape(1)
    if direct:
        held = [vector.reshape(1, -1) for vector in vectors] + [qkv_weight, proj_weight, up_weight, down_weight]
        piece, halo = call(
            pack_body,
            [((piece_rows, chan), bf16), ((2, SHIFT, cols, chan), bf16)],
            *held, tok, cot, name="pack", limit=58, ins=[pl.ANY] * 15,
            scratch=[(array.shape, bf16) for array in held] + [sems(15)],
        )
        fetched = [spread_out(piece, i) for i in range(near)]
    else:
        halo = jnp.stack([tok[:SHIFT], cot[:SHIFT]])
        gather = functools.partial(lax.all_gather, axis_name="fsdp", axis=0, tiled=True)
        full = [gather(vector).astype(f32).reshape(-1, chan) for vector in vectors]
        full.append(jnp.zeros((SMALL - 8 - ups, chan), f32))
        weights = [
            gather(qkv_weight), jnp.concatenate(full, axis=0), gather(proj_weight), gather(up_weight),
            gather(down_weight),
        ]
    halo = shifted(halo, "seq", -1)
    bm, idx = call(
        bias_body,
        [(wide_scores, f32), ((WTOK, HEADS * QPAD), f32)],
        region, bias_table.T, table_index, tok, cot,
        scratch=[((DIGIT, HEADS * DIGIT), f32), ((WTOK, HEADS * QPAD), f32), ((wins, WTOK, 128), f32)],
        name="score_bias", micros=3,
    )
    if direct:
        *fetched, bm, idx = lax.optimization_barrier((*fetched, bm, idx))
        (pair,) = call(join_body, [((near, piece_rows, chan), bf16)], *fetched, name="join")
        weights = [pair, swap(pair, "seq", 1)]
    xw, cw, unit, rstd = call(prepare_body, [(tokw, f32)] * 4, tok, cot, halo, name="prepare", micros=2)
    big = dict(limit=32)
    place = [pltpu.SMEM] * 2
    nb, qx, k_b, v_b, probs, att, small, w_qkv, w_proj, w_up, w_down = call(
        functools.partial(attend_body, count),
        [
            (flatw, bf16), ((wins, HEADS * QPAD, chan), bf16), (tokw, bf16), (tokw, bf16), (wide_scores, f32),
            (tokw, f32), ((SMALL, chan), f32), ((chan, 3 * chan), bf16), ((chan, chan), bf16), ((chan, wide), bf16),
            ((wide, chan), bf16),
        ],
        me, band, unit, bm, *weights, name="attention", micros=3, ins=place + [VMEM] * (2 + len(weights)), **big,
        scratch=[((wins * WTOK, 3 * chan), f32)],
    )
    bw, dmid, datt, g_proj, g_up, g_down, g_one = call(
        mlp_body,
        [
            (tokw, f32), (tokw, f32), (tokw, f32), ((chan, chan), f32), ((chan, wide), f32), ((wide, chan), f32),
            ((SMALL, chan), f32),
        ],
        xw, cw, att, small, w_proj, w_up, w_down, name="feed_forward", micros=5, **big,
        scratch=[(flatw, bf16)] * 4 + [(flatu, bf16)] * 2 + [(flatu, f32)] * 2 + [(flatw, f32)] * 4,
    )
    if direct:
        halves = ((fsdp, (piece_rows + SMALL) // 2, chan), bf16)
        sent = [halves] * 2
    else:
        sent = [((chan, 3 * chan), f32), ((SMALL, chan), f32)]
    tw, *grads = call(
        functools.partial(back_body, count),
        [(tokw, f32)] + sent,
        band, qx, k_b, v_b, probs, datt, dmid, nb, unit, rstd, small, w_qkv, idx, g_proj, g_up, g_down, g_one,
        name="attention_back", micros=5, ins=place[:1] + [VMEM] * 16, **big,
        scratch=[
            (tokw, f32), (tokw, f32), (tokw, f32), ((wins * WTOK, 3 * chan), bf16), (flatw, f32),
            ((WTOK, HEADS * QPAD), f32), ((WTOK, DIGIT, HEADS * DIGIT), f32), ((chan, 3 * chan), f32), ((SMALL, chan), f32),
            ((max(count, 1), piece_rows + SMALL, chan), bf16),
        ],
    )
    bo, tg, last = call(
        rows_body,
        [((rows, cols, chan), bf16), ((rows, cols, chan), f32), ((2, SHIFT, cols, chan), bf16)],
        bw, tw, name="rows", micros=2,
    )
    if not direct:
        last = shifted(last, "seq", 1)
        g_proj, g_up, g_down, early, g_qkv, late = lax.psum((g_proj, g_up, g_down, g_one, *grads), "seq")
        digits = (TABLE + DIGIT - 1) // DIGIT
        table = lax.psum(late[4 : 4 + digits, : HEADS * DIGIT], "fsdp").reshape(digits, HEADS, DIGIT)
        table = table.transpose(1, 0, 2).reshape(HEADS, digits * DIGIT)[:, :TABLE]
        scatter = functools.partial(lax.psum_scatter, axis_name="fsdp", scatter_dimension=0, tiled=True)
        block_out = jnp.concatenate([last[0], bo[SHIFT:]], axis=0)
        tokens_grad = jnp.concatenate([last[1].astype(f32), tg[SHIFT:]], axis=0)
        return (
            block_out[None], tokens_grad[None], scatter(late[0]), scatter(late[1]), scatter(g_qkv),
            scatter(late[2]), scatter(late[3]), scatter(g_proj), scatter(early[0]), scatter(early[1]),
            scatter(early[2]), scatter(g_up), scatter(early[4 : 4 + ups].reshape(-1)),
            scatter(g_down), scatter(early[3]), table.T,
        )
    kept, given = grads[0], swap(grads[1], "seq", 1)
    kept, given, last = lax.optimization_barrier((kept, given, last))
    last = shifted(last, "seq", 1)
    (kept,) = call(pair_body, [halves], kept, given, name="sum_cores")
    pieces = lax.all_to_all(kept, "fsdp", 0, 0, tiled=True)
    (both,) = call(sum_body, [(halves[0][1:], bf16)], pieces, name="sum_images")
    arrived = [both] + [swap(both, "seq", step) for step in range(1, bands)]
    line = ((1, depth), f32)
    outs = call(
        functools.partial(final_body, bands),
        [
            ((rows, cols, chan), bf16), ((rows, cols, chan), f32), line, line, ((depth, 3 * chan), f32), line,
            line, ((depth, chan), f32), line, line, line, ((depth, wide), f32), ((1, depth * ups), f32),
            ((depth * ups, chan), f32), line, ((HEADS, TABLE), f32),
        ],
        me, band, bo, tg, last, *arrived, name="finish", ins=[pltpu.SMEM] * 2 + [VMEM] * (3 + bands),
    )
    outs = [out.reshape(-1) if out.shape[0] == 1 else out for out in outs]
    return (outs[0][None], outs[1][None], *outs[2:15], outs[15].T)


def solution(mesh):
    placed = (
        P("fsdp", "seq", None, None),
        P("fsdp"),
        P("fsdp"),
        P("fsdp", None),
        P("fsdp"),
        P("fsdp"),
        P("fsdp", None),
        P("fsdp"),
        P("fsdp"),
        P("fsdp"),
        P("fsdp", None),
        P("fsdp"),
        P("fsdp", None),
        P("fsdp"),
        P(),
        P(),
        P("fsdp", "seq", None),
        P("fsdp", "seq", None, None),
    )
    return jax.shard_map(
        on_device,
        mesh=mesh,
        in_specs=placed,
        out_specs=(
            P("fsdp", "seq", None, None),
            P("fsdp", "seq", None, None),
            P("fsdp"),
            P("fsdp"),
            P("fsdp", None),
            P("fsdp"),
            P("fsdp"),
            P("fsdp", None),
            P("fsdp"),
            P("fsdp"),
            P("fsdp"),
            P("fsdp", None),
            P("fsdp"),
            P("fsdp", None),
            P("fsdp"),
            P(),
        ),
        check_vma=False,
    )
```
